32 devices in a mesh: rep: 2 (over core), shard: 16 (over z, y, x).
Axes of the slice: x: 2, y: 2, z: 4, core: 2. Of those that a mesh axis runs over, the one named last changes fastest.
Arguments:
- frames: bfloat16 [24000, 1280], P(('rep', 'shard')), may hold values from -6 to 6
- upstream: bfloat16 [24000, 1280], P(('rep', 'shard')), may hold values from -6 to 6
- lengths: int32 [16], replicated, may hold values from 375 to 1500, as said below
- master_qkv: float32 [3, 1280, 1280], P(None, 'shard'), may hold values from -0.15625 to 0.15625
- master_out: float32 [1280, 1280], P('shard'), may hold values from -0.25 to 0.25
- master_up: float32 [1280, 5120], P('shard'), may hold values from -0.15625 to 0.15625
- master_down: float32 [5120, 1280], P('shard'), may hold values from -0.078125 to 0.078125
- master_small: float32 [15360], P('shard'), may hold values from -1.2 to 1.5, as said below
- first_qkv: bfloat16 [3, 1280, 1280], P(None, 'shard'), may hold values from -448 to 448
- first_out: bfloat16 [1280, 1280], P('shard'), may hold values from -48 to 48
- first_up: bfloat16 [1280, 5120], P('shard'), may hold values from -256 to 256
- first_down: bfloat16 [5120, 1280], P('shard'), may hold values from -640 to 640
- first_small: bfloat16 [15360], P('shard'), may hold values from -627.4233 to 627.4233
- second_qkv: float32 [3, 1280, 1280], P(None, 'shard'), may hold values from 6000 to 24000
- second_out: float32 [1280, 1280], P('shard'), may hold values from 64 to 256
- second_up: float32 [1280, 5120], P('shard'), may hold values from 2400 to 9600
- second_down: float32 [5120, 1280], P('shard'), may hold values from 12000 to 48000
- second_small: float32 [15360], P('shard'), may hold values from 2160 to 96000
Outputs:
- mixed: float32 [24000, 1280], P(('rep', 'shard'))
- grad_frames: float32 [24000, 1280], P(('rep', 'shard'))
- updated_qkv: float32 [3, 1280, 1280], P(None, 'shard')
- casted_qkv: bfloat16 [3, 1280, 1280], P(None, 'shard')
- momentum_qkv: float32 [3, 1280, 1280], P(None, 'shard')
- variance_qkv: float32 [3, 1280, 1280], P(None, 'shard')
- updated_out: float32 [1280, 1280], P('shard')
- casted_out: bfloat16 [1280, 1280], P('shard')
- momentum_out: float32 [1280, 1280], P('shard')
- variance_out: float32 [1280, 1280], P('shard')
- updated_up: float32 [1280, 5120], P('shard')
- casted_up: bfloat16 [1280, 5120], P('shard')
- momentum_up: float32 [1280, 5120], P('shard')
- variance_up: float32 [1280, 5120], P('shard')
- updated_down: float32 [5120, 1280], P('shard')
- casted_down: bfloat16 [5120, 1280], P('shard')
- momentum_down: float32 [5120, 1280], P('shard')
- variance_down: float32 [5120, 1280], P('shard')
- updated_small: float32 [15360], P('shard')
- casted_small: bfloat16 [15360], P('shard')
- momentum_small: float32 [15360], P('shard')
- variance_small: float32 [15360], P('shard')
The draws below stay inside these ranges and needn't reach their ends.
Inputs may be any that keep to these rules, and one draw needn't show every extreme that they name: lengths[c] frames of clip c count; some clip has all 1500. `master_small`: gains in the two norms' gain blocks, biases elsewhere.
All inputs are finite; a program needn't handle non-finite values.
Results may differ from the reference program's by a relative error of at most 0.012.
The reference program's roundings to bfloat16 on the way count: a program that leaves them out, or rounds other values in their place, can miss the bound.
Values may be sent and summed in bfloat16 or wider, within the bound.
No kernel may reach another device: no remote copies, remote signals or barrier semaphores. Data moves between devices by JAX's collectives and lax.ppermute only.
A program may use at most 320 MiB of HBM per device.

```python
import functools
import math
import jax
import jax.numpy as jnp
from jax import lax

D = 1280
HEADS = 16
HEAD_DIM = 80
FF = 5120
STEP = 10
CLIP = 1500
CLIPS = 16
TOKENS = 24000
SMALL = 15360


def small_segments():
    return jnp.minimum(jnp.arange(SMALL, dtype=jnp.int32) // D, 8)


def small_scale():
    return jnp.where(small_segments() == 8, 0.3, 1.0) * TOKENS ** 0.5


def draw_lengths(key, part):
    key = jax.random.fold_in(key, 11)
    spread_lengths = jax.random.randint(key, (CLIPS,), CLIP // 4, CLIP + 1)
    chosen = jax.random.randint(jax.random.fold_in(key, 1), (), 0, CLIPS)
    return jnp.where(jnp.arange(CLIPS, dtype=jnp.int32) == chosen, CLIP, spread_lengths).astype(jnp.int32)


def draw_master_small(key, part):
    key = jax.random.fold_in(key, 12)
    segments = small_segments()
    noise = jnp.clip(jax.random.normal(key, (SMALL,), jnp.float32), -4.0, 4.0)
    gains = jax.random.uniform(jax.random.fold_in(key, 1), (SMALL,), jnp.float32, 0.5, 1.5)
    is_gain = (segments == 0) | (segments == 5)
    return jnp.where(is_gain, gains, 0.3 * noise).astype(jnp.float32)


def draw_first_small(key, part):
    key = jax.random.fold_in(key, 13)
    noise = jnp.clip(jax.random.normal(key, (SMALL,), jnp.float32), -4.0, 4.0)
    return (noise * small_scale()).astype(jnp.bfloat16)


def draw_second_small(key, part):
    key = jax.random.fold_in(key, 14)
    factor = jnp.exp(jax.random.uniform(key, (SMALL,), jnp.float32, 0.0, math.log(4.0)))
    scale_now = small_scale()
    return (scale_now * scale_now * factor).astype(jnp.float32)


def levels(rng, shape, shards, smallest, top_value):
    factor_of = 1.0
    for position, blocks in shards:
        draws = jax.random.uniform(jax.random.fold_in(jax.random.fold_in(rng, 6), position), (blocks,), jnp.float32, smallest / len(shards), top_value / len(shards))
        factor_of = factor_of * jnp.repeat(jnp.exp(draws), shape[position] // blocks).reshape((-1,) + (1,) * (len(shape) - 1 - position))
    return factor_of


def gaussian(rng, extent, scale, most, cuts=(), kind=jnp.bfloat16):
    array = jax.random.normal(rng, extent, jnp.float32) * scale
    if len(cuts) > 0:
        array = levels(rng, extent, cuts, -0.22, 0.18) * array
    return jnp.clip(array, min=-most, max=most).astype(kind)


def setup_inputs(seed: int = 0) -> dict:
    splits = jax.random.split(jax.random.key(seed), 19)
    return {
        "frames": gaussian(splits[0], (TOKENS, D), 1.0, 6.0, ((0, 32),)),
        "upstream": gaussian(splits[1], (TOKENS, D), 1.0, 6.0, ((0, 32),)),
        "lengths": draw_lengths(jax.random.fold_in(splits[18], 71), 0),
        "master_qkv": gaussian(splits[3], (3, D, D), D ** -0.5, 0.15625, ((1, 16),), jnp.float32),
        "master_out": gaussian(splits[4], (D, D), (D // 2) ** -0.5, 0.25, ((0, 16),), jnp.float32),
        "master_up": gaussian(splits[5], (D, FF), D ** -0.5, 0.15625, ((0, 16),), jnp.float32),
        "master_down": gaussian(splits[6], (FF, D), FF ** -0.5, 0.078125, ((0, 16),), jnp.float32),
        "master_small": draw_master_small(jax.random.fold_in(splits[18], 71), 0),
        "first_qkv": gaussian(splits[8], (3, D, D), ((TOKENS // 4) ** 0.5), 448.0, ((1, 16),)),
        "first_out": gaussian(splits[9], (D, D), ((4 * TOKENS // CLIP) ** 0.5), 48.0, ((0, 16),)),
        "first_up": gaussian(splits[10], (D, FF), ((TOKENS // 10) ** 0.5), 256.0, ((0, 16),)),
        "first_down": gaussian(splits[11], (FF, D), ((TOKENS // 2) ** 0.5), 640.0, ((0, 16),)),
        "first_small": draw_first_small(jax.random.fold_in(splits[18], 71), 0),
        "second_qkv": jnp.clip(jnp.exp(math.log(24000.0) - 1.3862944 * jax.random.uniform(splits[13], (3, D, D), jnp.float32) ** levels(splits[13], (3, D, D), ((1, 16),), -0.2, 0.2)), 6000.0, 24000.0),
        "second_out": jnp.clip(jnp.exp(math.log(256.0) - 1.3862944 * jax.random.uniform(splits[14], (D, D), jnp.float32) ** levels(splits[14], (D, D), ((0, 16),), -0.2, 0.2)), 64.0, 256.0),
        "second_up": jnp.clip(jnp.exp(math.log(9600.0) - 1.3862944 * jax.random.uniform(splits[15], (D, FF), jnp.float32) ** levels(splits[15], (D, FF), ((0, 16),), -0.2, 0.2)), 2400.0, 9600.0),
        "second_down": jnp.clip(jnp.exp(math.log(48000.0) - 1.3862944 * jax.random.uniform(splits[16], (FF, D), jnp.float32) ** levels(splits[16], (FF, D), ((0, 16),), -0.2, 0.2)), 12000.0, 48000.0),
        "second_small": draw_second_small(jax.random.fold_in(splits[18], 71), 0),
    }


LN_EPS = 1e-05
NEG_FILL = -1e+30
BETA_ONE = 0.5
BETA_TWO = 0.5
ADAM_EPS = 1e-08
RATES = (0.04, 0.5, 0.04, 0.02, 0.3)
DECAYS = (0.01, 0.01, 0.01, 0.01, 0.0)

@jax.custom_vjp
def low(v):
    return lax.optimization_barrier(v.astype(jnp.bfloat16)).astype(jnp.float32)

@jax.custom_vjp
def low_back(v):
    return v

def low_keep(v):
    return (low(v), None)

def low_pass(kept, grad):
    return (grad,)

def back_keep(v):
    return (v, None)

def back_low(kept, grad):
    return (low(grad),)
low.defvjp(low_keep, low_pass)
low_back.defvjp(back_keep, back_low)

def product(left, right):
    return jnp.dot(left, right, precision=lax.Precision.HIGHEST, preferred_element_type=jnp.float32)

def normalize(values, gain, shift):
    center = values - lax.optimization_barrier(jnp.mean(values, -1, keepdims=True))
    spread = lax.optimization_barrier(jnp.mean(center * center, -1, keepdims=True))
    return center * lax.rsqrt(spread + LN_EPS) * gain + shift

def gelu_exact(values):
    return jax.nn.gelu(values, approximate=False)

def split_heads(matrix):
    return matrix.reshape(matrix.shape[0], HEADS, HEAD_DIM).transpose(1, 0, 2)

def attend_head(counted, bundle):
    query_head, key_head, value_head = bundle
    scores = low_back(product(query_head, key_head.T) * HEAD_DIM ** (-0.5))
    scores = jnp.where(counted[None, :], scores, NEG_FILL)
    row_top = lax.optimization_barrier(jnp.max(scores, -1, keepdims=True))
    powers = jnp.exp(scores - row_top)
    attn_probs = powers / lax.optimization_barrier(jnp.sum(powers, -1, keepdims=True))
    return product(low(attn_probs), value_head)

def clip_forward(counted, params, frames_clip):
    w_qkv, w_out, w_up, w_down, small_vec = params
    pieces = [small_vec[segment * D:(segment + 1) * D] for segment in range(8)]
    gain_one, shift_one, bias_query, bias_value, bias_out, gain_two, shift_two, bias_down = pieces
    bias_up = small_vec[8 * D:]
    normed_one = low(normalize(frames_clip, gain_one, shift_one))
    query_rows = low(low_back(product(normed_one, w_qkv[0]) + bias_query))
    key_rows = low(low_back(product(normed_one, w_qkv[1])))
    value_rows = low(low_back(product(normed_one, w_qkv[2]) + bias_value))
    context_heads = lax.map(jax.checkpoint(functools.partial(attend_head, counted)), (split_heads(query_rows), split_heads(key_rows), split_heads(value_rows)))
    context = low(low_back(context_heads.transpose(1, 0, 2).reshape(CLIP, D)))
    middle = frames_clip + low_back(product(context, w_out) + bias_out)
    normed_two = low(normalize(middle, gain_two, shift_two))
    hidden_pre = low_back(product(normed_two, w_up) + bias_up)
    hidden = low(gelu_exact(hidden_pre))
    return product(hidden, w_down) + bias_down + middle

def adam_update(master, moment_one, second, gradient, step_rate, decay_rate):
    momentum = BETA_ONE * moment_one.astype(jnp.float32) + (1.0 - BETA_ONE) * gradient
    variance = BETA_TWO * second + (1.0 - BETA_TWO) * gradient * gradient
    momentum_hat = momentum / (1.0 - BETA_ONE ** STEP)
    variance_hat = variance / (1.0 - BETA_TWO ** STEP)
    updated = master - step_rate * (momentum_hat / (jnp.sqrt(variance_hat) + ADAM_EPS) + decay_rate * master)
    return (updated, updated.astype(jnp.bfloat16), momentum, variance)

def reference(frames, upstream, lengths, master_qkv, master_out, master_up, master_down, master_small, first_qkv, first_out, first_up, first_down, first_small, second_qkv, second_out, second_up, second_down, second_small):
    masters = (master_qkv, master_out, master_up, master_down, master_small)
    params = tuple((master.astype(jnp.bfloat16).astype(jnp.float32) for master in masters))
    frame_clips = frames.astype(jnp.float32).reshape(CLIPS, CLIP, D)
    upstream_clips = upstream.astype(jnp.float32).reshape(CLIPS, CLIP, D)
    positions = jnp.arange(CLIP, dtype=jnp.int32)

    def per_clip(totals, bundle):
        frames_clip, upstream_clip, length = bundle
        counted = positions < length
        mixed_clip, pull = jax.vjp(functools.partial(clip_forward, counted), params, frames_clip)
        grad_params, grad_clip = pull(upstream_clip)
        totals = tuple((total + gradient for total, gradient in zip(totals, grad_params)))
        return (totals, (mixed_clip, grad_clip))
    zeros = tuple((jnp.zeros_like(param) for param in params))
    totals, (mixed_clips, grad_clips) = lax.scan(per_clip, zeros, (frame_clips, upstream_clips, lengths))
    new_qkv, cast_qkv, mom_qkv, var_qkv = adam_update(master_qkv, first_qkv, second_qkv, totals[0], RATES[0], DECAYS[0])
    new_out, cast_out, mom_out, var_out = adam_update(master_out, first_out, second_out, totals[1], RATES[1], DECAYS[1])
    new_up, cast_up, mom_up, var_up = adam_update(master_up, first_up, second_up, totals[2], RATES[2], DECAYS[2])
    new_down, cast_down, mom_down, var_down = adam_update(master_down, first_down, second_down, totals[3], RATES[3], DECAYS[3])
    new_small, cast_small, mom_small, var_small = adam_update(master_small, first_small, second_small, totals[4], RATES[4], DECAYS[4])
    return (mixed_clips.reshape(TOKENS, D), grad_clips.reshape(TOKENS, D), new_qkv, cast_qkv, mom_qkv, var_qkv, new_out, cast_out, mom_out, var_out, new_up, cast_up, mom_up, var_up, new_down, cast_down, mom_down, var_down, new_small, cast_small, mom_small, var_small)
```

```python
import functools
import math

import jax
import jax.numpy as jnp
from jax import lax
from jax.experimental import pallas as pl
from jax.experimental.pallas import tpu as pltpu
from jax.sharding import PartitionSpec as P

HEAD_DIM = 80
STEP = 10

LN_EPS = 1e-05
NEG_FILL = -1e30
BETA_ONE = 0.5
BETA_TWO = 0.5
ADAM_EPS = 1e-08
RATES = (0.04, 0.5, 0.04, 0.02, 0.3)
DECAYS = (0.01, 0.01, 0.01, 0.01, 0.0)

F32 = jnp.float32
BF16 = jnp.bfloat16
MIB = 1024 * 1024
SCALING = HEAD_DIM**-0.5
SCORE_SCALE = SCALING * math.log2(math.e)
MASK_ROWS = 16
SMALL_COST = pl.CostEstimate(flops=0, bytes_accessed=MIB, transcendentals=0)
VMEM_SPEC = pl.BlockSpec(memory_space=pltpu.VMEM)
ANY_SPEC = pl.BlockSpec(memory_space=pl.ANY)
NN = (((1,), (0,)), ((), ()))
NT = (((1,), (1,)), ((), ()))


def product(left, right, dims=NN):
    return lax.dot_general(left, right, dims, preferred_element_type=F32)


def call(body, out_shape, limit=48, **options):
    return pl.pallas_call(
        body,
        out_shape=out_shape,
        compiler_params=pltpu.CompilerParams(vmem_limit_bytes=limit * MIB),
        cost_estimate=SMALL_COST,
        **options,
    )


def array(shape, dtype):
    return jax.ShapeDtypeStruct(tuple(shape), dtype)


def xor_pairs(count, mask):
    return [(source, source ^ mask) for source in range(count)]


def across_cores(value):
    return lax.ppermute(value, "rep", xor_pairs(lax.axis_size("rep"), 1))


def swap_clips(value):
    reps, shards = lax.axis_size("rep"), lax.axis_size("shard")
    pairs = []
    for rep in range(reps):
        for shard in range(shards):
            if (rep % 2) != (shard % 2):
                pairs.append((rep * shards + shard, (rep ^ 1) * shards + (shard ^ 1)))
    got = lax.ppermute(value.astype(BF16), ("rep", "shard"), pairs)
    moved = (lax.axis_index("rep") % 2) != (lax.axis_index("shard") % 2)
    return jnp.where(moved, got.astype(value.dtype), value)


def after(value, *others):
    return lax.optimization_barrier((value,) + others)[0]


def flip(index, mask):
    out, bit = index, 1
    while bit <= mask:
        if mask & bit:
            out = out + bit * (1 - 2 * ((index // bit) % 2))
        bit *= 2
    return out


def gather_orders(shards):
    far = [1 << k for k in range(int(math.log2(shards)))][::-1]
    most = [b for b in far if b >= 8]
    axes = {"x": 1, "y": 2, "z": 4}
    names = ("xyz", "xzy", "yxz", "yzx", "zxy", "zyx")
    return {name: most + [axes[axis] for axis in name] for name in names}


def relative_places(order):
    places = [0]
    for mask in order:
        places = places + [mask ^ r for r in places]
    return places


class Doubling:
    def __init__(self, blocks, orders):
        self.held, self.orders, self.step, self.got = blocks, orders, 0, None

    def behind(self, *others):
        self.held = [after(held, *others) for held in self.held]

    def start(self):
        shards = lax.axis_size("shard")
        masks = [order[self.step] for order in self.orders]
        if self.step == 0:
            rows = [held.shape[1] for held in self.held]
            together = jnp.concatenate(self.held, 1)
            together = lax.ppermute(together, "shard", xor_pairs(shards, masks[0]))
            ends = [sum(rows[: i + 1]) for i in range(len(rows))]
            self.got = [together[:, end - row : end] for end, row in zip(ends, rows)]
        else:
            self.got = [
                lax.ppermute(held, "shard", xor_pairs(shards, mask))
                for held, mask in zip(self.held, masks)
            ]
        self.step += 1

    def finish(self, *behind):
        if behind:
            self.got = [after(got, *behind) for got in self.got]
        if self.step < len(self.orders[0]):
            self.held = [jnp.concatenate(pair, 0) for pair in zip(self.held, self.got)]
        return self.held

    def halves(self):
        return list(zip(self.held, self.got, self.orders))

    def pair(self, at):
        part = Doubling(self.held[at : at + 2], self.orders[at : at + 2])
        part.step = self.step
        return part


def scatter_plan(order):
    kept = [0]
    sent = []
    for mask in order[::-1]:
        sent.append([mask ^ r for r in kept])
        kept = kept + sent[-1]
    return sent[::-1] + [[0]]


class Halving:
    def __init__(self, chunks, orders):
        self.chunks, self.orders = chunks, orders
        self.got = [[] for _ in chunks]

    def step(self, *behind):
        index = len(self.got[0])
        shards = lax.axis_size("shard")
        sends = [chunk[index] for chunk in self.chunks]
        if behind:
            sends = [after(send, *behind) for send in sends]
        if index:
            sends = add_blocks(sends, self.got, 1, BF16)
        masks = [order[index] for order in self.orders]
        if index == len(self.orders[0]) - 1 and len(sends) > 1:
            rows = [send.shape[1] for send in sends]
            together = jnp.concatenate(sends, 1)
            together = lax.ppermute(together, "shard", xor_pairs(shards, masks[0]))
            ends = [sum(rows[: i + 1]) for i in range(len(rows))]
            arrived = [together[:, end - row : end] for end, row in zip(ends, rows)]
        else:
            arrived = [
                lax.ppermute(send, "shard", xor_pairs(shards, mask))
                for send, mask in zip(sends, masks)
            ]
        for got, new in zip(self.got, arrived):
            got.append(new)
        return sends

    def result(self, *behind):
        stays = [chunk[-1] for chunk in self.chunks]
        if behind:
            stays = [after(stay, *behind) for stay in stays]
        return add_blocks(stays, self.got, 0, F32)


def over_groups(value):
    reps = lax.axis_size("rep")
    mask = 2
    while mask < reps:
        value = value + lax.ppermute(value, "rep", xor_pairs(reps, mask))
        mask *= 2
    return value


def reduce_small(vector):
    shards, here = lax.axis_size("shard"), lax.axis_index("shard")
    reps = lax.axis_size("rep")
    held, mask = vector, shards // 2
    while mask >= 1:
        upper = (here // mask) % 2 == 1
        low, high = held[:mask], held[mask:]
        got = lax.ppermute(jnp.where(upper, low, high), "shard", xor_pairs(shards, mask))
        held = jnp.where(upper, high, low) + got
        mask //= 2
    held, mask = held[0], 1
    while mask < reps:
        held = held + lax.ppermute(held, "rep", xor_pairs(reps, mask))
        mask *= 2
    return held


def row_slice(start, size):
    return pl.ds(pl.multiple_of(start, 8), size)


def place_first(halves, shards, block, half, cut, small_rows):
    rest = block - 2 * cut

    def body(*refs):
        ins, (qkv, out, small) = refs[:6], refs[6:]
        here = lax.axis_index("shard")
        for index, (low, _, order) in enumerate(halves):
            for place, rel in enumerate(relative_places(order)):
                ref = ins[2 * index + place // low.shape[0]].at[place % low.shape[0]]
                at = flip(here, rel)
                qkv[at, :, index * half : (index + 1) * half] = ref[:block, :]
                if index < 2:
                    out[at, index * cut : (index + 1) * cut, :] = ref[block : block + cut, :]
                else:
                    out[at, 2 * cut :, :] = ref[block : block + rest, :]
                    small[at] = ref[block + rest :, :]

    shapes = (
        array((shards, block, 3 * half), BF16),
        array((shards, block, half), BF16),
        array((shards, small_rows, half), BF16),
    )
    return call(
        body, shapes, in_specs=[VMEM_SPEC] * 6, out_specs=[VMEM_SPEC] * 3, name="place_first"
    )(*[part for low, got, _ in halves for part in (low, got)])


def write_parts(outs, plan, source, here):
    for out, part in zip(outs, plan):
        for place, rel in enumerate(part):
            out[place] = source[flip(here, rel)]


def add_blocks(firsts, others, place, dtype):
    inputs, specs = [], []
    for first, rest in zip(firsts, others):
        inputs.append(first)
        specs.append(pl.BlockSpec(first.shape, lambda i: (0, 0, 0)))
        for other in rest:
            inputs.append(other)
            specs.append(pl.BlockSpec(first.shape, lambda i, at=place: (at, 0, 0)))

    def body(*refs):
        at = 0
        for index, rest in enumerate(others):
            total = refs[at][...].astype(F32)
            for ref in refs[at + 1 : at + 1 + len(rest)]:
                total = total + ref[...].astype(F32)
            refs[len(inputs) + index][...] = total.astype(dtype)
            at += 1 + len(rest)

    return list(call(
        body,
        [array(first.shape, dtype) for first in firsts],
        grid=(1,),
        in_specs=specs,
        out_specs=[pl.BlockSpec(first.shape, lambda i: (0, 0, 0)) for first in firsts],
        name="add_blocks",
    )(*inputs))


def part_shapes(plan, rows, width):
    return [array((len(part), rows, width), BF16) for part in plan]


def norm_rows(values):
    center = values - jnp.mean(values, -1, keepdims=True)
    spread = jnp.mean(center * center, -1, keepdims=True)
    inverse = lax.rsqrt(spread + LN_EPS)
    return center * inverse, inverse


def project(own, other, gain, shift, w_qkv, bias):
    _, padded, width = own.shape
    columns = w_qkv.shape[1]
    third = columns // 3

    def body(own_ref, other_ref, gain_ref, shift_ref, w_ref, bias_ref, normed_ref, out_ref):
        values = jnp.where(pl.program_id(0) == 0, own_ref[...], other_ref[...]).astype(F32)
        unit, _ = norm_rows(values)
        normed = (unit * gain_ref[...] + shift_ref[...]).astype(BF16)
        normed_ref[...] = normed
        for part in range(3):
            cols = slice(part * third, (part + 1) * third)
            result = product(normed, w_ref[:, cols]) + bias_ref[:, cols]
            out_ref[cols, :] = result.astype(BF16).T

    line = pl.BlockSpec((1, width), lambda i: (0, 0))
    rows = pl.BlockSpec((None, padded, width), lambda i: (0, 0, 0))
    return call(
        body,
        (array((2 * padded, width), BF16), array((columns, 2 * padded), BF16)),
        grid=(2,),
        in_specs=[
            rows,
            rows,
            line,
            line,
            pl.BlockSpec((width, columns), lambda i: (0, 0)),
            pl.BlockSpec((1, columns), lambda i: (0, 0)),
        ],
        out_specs=(
            pl.BlockSpec((padded, width), lambda i: (i, 0)),
            pl.BlockSpec((columns, padded), lambda i: (0, i)),
        ),
        name="project",
    )(own, other, gain, shift, w_qkv, bias)


def attend_kernel(mask_ref, q_ref, k_ref, v_ref, out_ref, lse_ref, kt, qt, *, step):
    dim, keys = k_ref.shape
    kt[...] = jnp.zeros_like(kt)
    kt[:dim, :] = k_ref[...]
    kt[dim : dim + MASK_ROWS, :] = mask_ref[:MASK_ROWS, :]
    k_rows = kt[...].T
    qt[...] = jnp.zeros_like(qt)
    qt[:dim, :] = q_ref[...]
    qt[dim : dim + MASK_ROWS, :] = mask_ref[MASK_ROWS:, :]
    for start in range(0, keys, step):
        cols = slice(start, start + step)
        scores = jnp.dot(k_rows, qt[:, cols], preferred_element_type=F32)
        top = jnp.max(scores, 0, keepdims=True) * SCORE_SCALE
        powers = jnp.exp2(scores * SCORE_SCALE - top)
        total = jnp.sum(powers, 0, keepdims=True)
        context = jnp.dot(v_ref[...], powers.astype(BF16), preferred_element_type=F32)
        out_ref[:, cols] = (context / total).astype(BF16)
        lse_ref[:, cols] = top + jnp.log2(total)


def attend(qkv, masks, first, heads):
    _, _, dim, rows = qkv.shape
    step = 512

    def head_block(which):
        return pl.BlockSpec((None, None, dim, rows), lambda h: (which, first + h, 0, 0))

    return pl.pallas_call(
        functools.partial(attend_kernel, step=step),
        grid=(heads,),
        out_shape=(
            jax.ShapeDtypeStruct((heads, dim, rows), BF16),
            jax.ShapeDtypeStruct((heads, 1, rows), F32),
        ),
        in_specs=[
            pl.BlockSpec(masks.shape, lambda h: (0, 0)),
            head_block(0),
            head_block(1),
            head_block(2),
        ],
        out_specs=(
            pl.BlockSpec((None, dim, rows), lambda h: (h, 0, 0)),
            pl.BlockSpec((None, 1, rows), lambda h: (h, 0, 0)),
        ),
        scratch_shapes=[pltpu.VMEM((128, rows), BF16), pltpu.VMEM((128, rows), BF16)],
        compiler_params=pltpu.CompilerParams(vmem_limit_bytes=48 * MIB),
        cost_estimate=SMALL_COST,
        name="attend",
    )(masks, qkv, qkv, qkv)


def attend_back_kernel(
    mask_ref, q_ref, k_ref, v_ref, g_ref, ctx_ref, lse_ref, gq_ref, gk_ref, gv_ref, kt, qt, pad, acc_k, acc_v, *, step
):
    dim, keys = k_ref.shape
    kt[...] = jnp.zeros_like(kt)
    kt[:dim, :] = k_ref[...]
    kt[dim : dim + MASK_ROWS, :] = mask_ref[:MASK_ROWS, :]
    k_rows = kt[...].T
    pad[...] = jnp.zeros_like(pad)
    pad[:dim, :] = v_ref[...]
    v_rows = pad[...].T
    qt[...] = jnp.zeros_like(qt)
    qt[:dim, :] = q_ref[...]
    qt[dim : dim + MASK_ROWS, :] = mask_ref[MASK_ROWS:, :]
    q_rows = qt[...].T
    pad[:dim, :] = g_ref[...]
    g_rows = pad[...].T
    inner = jnp.sum(g_ref[...].astype(F32) * ctx_ref[...].astype(F32), 0, keepdims=True)
    for start in range(0, keys, step):
        cols = slice(start, start + step)
        scores = jnp.dot(k_rows, qt[:, cols], preferred_element_type=F32)
        probs = jnp.exp2(scores * SCORE_SCALE - lse_ref[:, cols])
        grad_probs = jnp.dot(v_rows, pad[:, cols], preferred_element_type=F32)
        grad_scores = (probs * (grad_probs - inner[:, cols])).astype(BF16)
        part_v = jnp.dot(probs.astype(BF16), g_rows[cols, :], preferred_element_type=F32)
        part_k = jnp.dot(grad_scores, q_rows[cols, :], preferred_element_type=F32)
        if start == 0:
            acc_v[...] = part_v
            acc_k[...] = part_k
        else:
            acc_v[...] += part_v
            acc_k[...] += part_k
        grad_query = jnp.dot(k_ref[...], grad_scores, preferred_element_type=F32)
        gq_ref[:, cols] = (grad_query * SCALING).astype(BF16)
    gv_ref[...] = acc_v[...].T[:dim, :].astype(BF16)
    gk_ref[...] = (acc_k[...].T[:dim, :] * SCALING).astype(BF16)


def attend_back(qkv, masks, grad_context, context, lse, first, inside, heads):
    _, dim, rows = context.shape
    step = 512

    def head_block(which):
        return pl.BlockSpec((None, None, dim, rows), lambda h: (which, first + h, 0, 0))

    plain = pl.BlockSpec((None, dim, rows), lambda h: (h, 0, 0))
    return pl.pallas_call(
        functools.partial(attend_back_kernel, step=step),
        grid=(heads,),
        out_shape=[jax.ShapeDtypeStruct((heads, dim, rows), BF16)] * 3,
        in_specs=[
            pl.BlockSpec(masks.shape, lambda h: (0, 0)),
            head_block(0),
            head_block(1),
            head_block(2),
            pl.BlockSpec((None, dim, rows), lambda h: (first + h, 0, 0)),
            pl.BlockSpec((None, dim, rows), lambda h: (inside + h, 0, 0)),
            pl.BlockSpec((None, 1, rows), lambda h: (inside + h, 0, 0)),
        ],
        out_specs=[plain] * 3,
        scratch_shapes=[pltpu.VMEM((128, rows), BF16)] * 3 + [pltpu.VMEM((rows, 128), F32)] * 2,
        compiler_params=pltpu.CompilerParams(vmem_limit_bytes=48 * MIB),
        cost_estimate=SMALL_COST,
        name="attend_back",
    )(masks, qkv, qkv, qkv, grad_context, context, lse)


def attended(contexts, gots, w_own, w_other, frames, bias, gain, shift):
    _, padded, width = frames.shape
    half = width // 2
    step = 256
    tiles = padded // step

    def body(ca, cb, ga, gb, wo_ref, wt_ref, frames_ref, bias_ref, gain_ref, shift_ref, middle_ref, normed_ref):
        first = lax.axis_index("rep") % 2 == 0
        own = jnp.concatenate([ca[...], cb[...]], 0)
        got = jnp.concatenate([ga[...], gb[...]], 0)
        low = jnp.where(first, own, got).T
        high = jnp.where(first, got, own).T
        by_own = product(low, wo_ref[:half, :]) + product(high, wo_ref[half:, :])
        by_other = product(low, wt_ref[:half, :]) + product(high, wt_ref[half:, :])
        result = jnp.concatenate(
            [jnp.where(first, by_own, by_other), jnp.where(first, by_other, by_own)], 1
        )
        middle = result + frames_ref[...].astype(F32) + bias_ref[...]
        middle_ref[...] = middle
        unit, _ = norm_rows(middle)
        normed_ref[...] = (unit * gain_ref[...] + shift_ref[...]).astype(BF16)

    part = half // 2
    line = pl.BlockSpec((1, width), lambda i: (0, 0))
    here = pl.BlockSpec((part, step), lambda i: (0, i))
    there = pl.BlockSpec((part, step), lambda i: (0, i + tiles))
    matrix = pl.BlockSpec((width, half), lambda i: (0, 0))
    rows = pl.BlockSpec((step, width), lambda i: (i, 0))
    return call(
        body,
        (array((padded, width), F32), array((padded, width), BF16)),
        grid=(tiles,),
        in_specs=[here, here, there, there, matrix, matrix]
        + [pl.BlockSpec((None, step, width), lambda i: (0, i, 0)), line, line, line],
        out_specs=(rows, rows),
        name="attended",
    )(*contexts, *gots, w_own, w_other, frames, bias, gain, shift)


def feed(own, other, up_own, up_other, weights, bias, plans):
    padded, width = own.shape
    stacks_given = [part for halves in weights for part in halves[:2]] if isinstance(weights, list) else [weights]
    count_in = len(stacks_given)
    block, units = stacks_given[0].shape[-2:]
    shards = width // block
    tile = 256
    tiles = units // tile
    up_plan, down_plan = plans

    def body(*refs):
        x_refs, u_refs = refs[0:2], refs[2:4]
        stacks, refs = refs[4 : 4 + count_in], refs[4 + count_in :]
        bias_ref, mixed_own, grad_own, send, sums_ref = refs[:5]
        up_outs = refs[5 : 5 + len(up_plan)]
        down_outs = refs[5 + len(up_plan) : 5 + len(up_plan) + len(down_plan)]
        w_up, w_down, hidden_t, x_t, grad_pre, hidden, blocks, sems = refs[5 + len(up_plan) + len(down_plan) :]
        index = pl.program_id(0)
        here = lax.axis_index("shard")

        def rows_step(which):
            x_ref, u_ref = x_refs[which], u_refs[which]
            cols = slice(which * padded, (which + 1) * padded)
            wu, wd = w_up[...].reshape(width, units), w_down[...].reshape(units, width)

            def products(t):
                part = slice(t * tile, (t + 1) * tile)
                return product(x_ref[...], wu[:, part]), product(u_ref[...], wd[part, :], NT)

            ahead = products(0)
            for t in range(tiles):
                part = slice(t * tile, (t + 1) * tile)
                pre, grad_hidden = ahead
                if t + 1 < tiles:
                    ahead = products(t + 1)
                pre = pre + bias_ref[:, part]
                phi = 0.5 + 0.5 * lax.erf(pre * (0.5**0.5))
                hid = (pre * phi).astype(BF16)
                hidden[:, part] = hid
                hidden_t[part, cols] = hid.T
                density = jnp.exp(pre * pre * -0.5) * (1.0 / math.sqrt(2.0 * math.pi))
                grad = (grad_hidden * (phi + pre * density)).astype(BF16)
                grad_pre[cols, part] = grad
                total = jnp.sum(grad.astype(F32), 0, keepdims=True)
                if which == 1:
                    sums_ref[:, part] = total
                else:
                    sums_ref[:, part] += total
            mixed_ref, grad_ref = ((mixed_own, grad_own), (send.at[1], send.at[0]))[which]
            for t in range(width // tile):
                part = slice(t * tile, (t + 1) * tile)
                mixed_ref[:, part] = product(hidden[...], wd[:, part]).astype(mixed_ref.dtype)
                grad_ref[:, part] = product(grad_pre[cols, :], wu[part, :], NT).astype(grad_ref.dtype)

        @pl.when(index == 0)
        def _():
            copies = []

            def copy_in(source, matrix, at):
                copies.append(pltpu.make_async_copy(source, matrix.at[at], sems.at[len(copies)]))
                copies[-1].start()

            for which, matrix in enumerate((w_up, w_down)):
                if count_in == 1:
                    for at in range(shards):
                        copy_in(stacks[0].at[at, which], matrix, at)
                else:
                    for place, rel in enumerate(relative_places(weights[which][2])):
                        stack = stacks[2 * which + place // (shards // 2)]
                        copy_in(stack.at[place % (shards // 2)], matrix, flip(here, rel))
            for which in range(2):
                x_t[:, which * padded : (which + 1) * padded] = x_refs[which][...].T
            for copy in copies:
                copy.wait()
            rows_step(1)

        @pl.when(index == 1)
        def _():
            rows_step(0)

        @pl.when(index >= 2)
        def _():
            part = pl.ds(pl.multiple_of((index - 2) * tile, tile), tile)
            down = product(hidden_t[:, :padded], u_refs[0][:, part]) + product(
                hidden_t[:, padded:], u_refs[1][:, part]
            )
            blocks[...] = down.astype(BF16).reshape(shards, block, tile)
            write_parts(down_outs, down_plan, blocks, here)
            up = product(x_t[...], grad_pre[:, part])
            blocks[...] = up.astype(BF16).reshape(shards, block, tile)
            write_parts(up_outs, up_plan, blocks, here)

    once = pl.Buffered(1)
    whole = pl.BlockSpec((padded, width), lambda i: (0, 0), pipeline_mode=once)
    line = pl.BlockSpec((1, units), lambda i: (0, 0))
    second = pl.BlockSpec((None, padded, width), lambda i: (1, 0, 0), pipeline_mode=once)
    shapes = [
        array((padded, width), F32),
        array((padded, width), F32),
        array((2, padded, width), BF16),
        array((1, units), F32),
    ]
    specs = [
        whole,
        whole,
        pl.BlockSpec((2, padded, width), lambda i: (0, 0, 0), pipeline_mode=once),
        line,
    ]
    for plan, size in ((up_plan, units), (down_plan, width)):
        shapes += part_shapes(plan, block, size)
        specs += [
            pl.BlockSpec((len(part), block, tile), lambda i: (0, 0, jnp.maximum(i - 2, 0)))
            for part in plan
        ]
    results = call(
        body,
        shapes,
        limit=60,
        grid=(2 + tiles,),
        in_specs=[whole, whole, second, second] + [ANY_SPEC] * count_in + [line],
        out_specs=specs,
        scratch_shapes=[
            pltpu.VMEM((shards, block, units), BF16),
            pltpu.VMEM((shards, block, width), BF16),
            pltpu.VMEM((units, 2 * padded), BF16),
            pltpu.VMEM((width, 2 * padded), BF16),
            pltpu.VMEM((2 * padded, units), BF16),
            pltpu.VMEM((padded, units), BF16),
            pltpu.VMEM((shards, block, tile), BF16),
            pltpu.SemaphoreType.DMA((2 * shards,)),
        ],
        name="feed",
    )(own, other, up_own, up_other, *stacks_given, bias)
    count = 4 + len(up_plan)
    return results[:4], results[4:count], results[count:]


def norm_back(sums, values, gain, base, low_out):
    given = [item if isinstance(item, tuple) else (item, None) for item in (*sums, values, base)]
    padded, width = given[0][0].shape[-2:]
    step = 256

    def body(*refs):
        parts = refs[: len(sums)]
        values_ref, base_ref, gain_ref = refs[len(parts) : len(parts) + 3]
        outs = refs[len(parts) + 3 :]
        sums_ref = outs[-1]
        grads = parts[0][...].astype(F32)
        for ref in parts[1:]:
            grads = grads + ref[...].astype(F32)
        unit, inverse = norm_rows(values_ref[...].astype(F32))
        scaled = grads * gain_ref[...]
        inner = (
            scaled
            - jnp.mean(scaled, -1, keepdims=True)
            - unit * jnp.mean(scaled * unit, -1, keepdims=True)
        )
        result = base_ref[...].astype(F32) + inverse * inner
        outs[0][...] = result
        lines = [jnp.sum(grads * unit, 0, keepdims=True), jnp.sum(grads, 0, keepdims=True)]
        if low_out:
            low = result.astype(BF16)
            outs[1][...] = low
            lines.append(jnp.sum(low.astype(F32), 0, keepdims=True))
            lines.append(jnp.sum(base_ref[...].astype(F32), 0, keepdims=True))

        @pl.when(pl.program_id(0) == 0)
        def _():
            sums_ref[...] = jnp.zeros_like(sums_ref)

        for place, line in enumerate(lines):
            sums_ref[place : place + 1, :] += line

    rows = pl.BlockSpec((step, width), lambda i: (i, 0))
    shapes = [array((padded, width), F32)]
    if low_out:
        shapes.append(array((padded, width), BF16))
    shapes.append(array((8, width), F32))
    return call(
        body,
        shapes,
        grid=(padded // step,),
        in_specs=[
            rows
            if place is None
            else pl.BlockSpec((None, step, width), lambda i, place=place: (place, i, 0))
            for _, place in given
        ]
        + [pl.BlockSpec((1, width), lambda i: (0, 0))],
        out_specs=[rows] * (len(shapes) - 1) + [pl.BlockSpec((8, width), lambda i: (0, 0))],
        name="norm_back",
    )(*[item for item, _ in given], gain)


def attended_back(own, other, w_own, w_other, contexts, gots, plan, shards):
    padded, width = own.shape
    half = width // 2
    block = width // shards

    def body(*refs):
        own_ref, other_ref, wo_ref, wt_ref, ca, cb, ga, gb = refs[:8]
        context_ref, outs, blocks = refs[8], refs[9:-1], refs[-1]
        core = lax.axis_index("rep") % 2
        here = lax.axis_index("shard")
        mine = pl.ds(pl.multiple_of(core * half, half), half)
        theirs = pl.ds(pl.multiple_of((1 - core) * half, half), half)
        for place, ref in enumerate((own_ref, other_ref)):
            cols = slice(place * padded, (place + 1) * padded)
            result = product(wo_ref[mine, :], ref[:, mine], NT)
            result = result + product(wt_ref[mine, :], ref[:, theirs], NT)
            context_ref[:, cols] = result.astype(BF16)
        for heads, (pair, near, far) in enumerate(
            (
                ((ca, cb), slice(0, padded), slice(padded, 2 * padded)),
                ((ga, gb), slice(padded, 2 * padded), slice(0, padded)),
            )
        ):
            for place, ref in enumerate(pair):
                result = product(ref[:, near], own_ref[:, mine])
                result = result + product(ref[:, far], other_ref[:, mine])
                count = shards // 4
                at = (core if heads == 0 else 1 - core) * (shards // 2) + place * count
                blocks[pl.ds(at, count)] = result.astype(BF16).reshape(count, block, half)
        write_parts(outs, plan, blocks, here)

    shapes = [array((half, 2 * padded), BF16)] + part_shapes(plan, block, half)
    results = call(
        body,
        shapes,
        in_specs=[VMEM_SPEC] * 8,
        out_specs=[VMEM_SPEC] * len(shapes),
        scratch_shapes=[pltpu.VMEM((shards, block, half), BF16)],
        name="attended_back",
    )(own, other, w_own, w_other, *contexts, *gots)
    return results[0], results[1:]


def project_back(grads, w_qkv):
    part, rows = grads[0].shape
    count = len(grads)
    padded = rows // 2
    width, columns = w_qkv.shape

    def body(*refs):
        w_ref, own_ref, other_ref = refs[count:]

        def run(out_ref):
            stacked = jnp.concatenate([ref[...] for ref in refs[:count]], 0).T
            out_ref[...] = product(stacked, w_ref[...], NT).astype(out_ref.dtype)

        @pl.when(pl.program_id(0) == 0)
        def _():
            run(other_ref)

        @pl.when(pl.program_id(0) == 1)
        def _():
            run(own_ref)

    whole = pl.BlockSpec((padded, width), lambda i: (0, 0))
    return call(
        body,
        (array((padded, width), F32), array((padded, width), BF16)),
        grid=(2,),
        in_specs=[pl.BlockSpec((part, padded), lambda i: (0, 1 - i))] * count
        + [pl.BlockSpec((width, columns), lambda i: (0, 0))],
        out_specs=(whole, whole),
        name="project_back",
    )(*grads, w_qkv)


def project_grads(normed, groups, plans):
    rows, width = normed.shape
    half = sum(piece.shape[0] for piece in groups[0])
    shards = sum(len(p) for p in plans[0])
    block = width // shards
    given = [normed] + [piece for group in groups for piece in group]

    def body(*refs):
        normed_ref, outs, (turned, blocks) = refs[0], refs[len(given) : -2], refs[-2:]
        here = lax.axis_index("shard")
        turned[...] = normed_ref[...].T
        at, place_in = 0, 1
        for group, plan in zip(groups, plans):
            stacked = jnp.concatenate([ref[...] for ref in refs[place_in : place_in + len(group)]], 0)
            place_in += len(group)
            result = product(turned[...], stacked, NT)
            blocks[...] = result.astype(BF16).reshape(shards, block, half)
            write_parts(outs[at : at + len(plan)], plan, blocks, here)
            at += len(plan)

    shapes = []
    for plan in plans:
        shapes += part_shapes(plan, block, half)
    flat = call(
        body,
        shapes,
        in_specs=[VMEM_SPEC] * len(given),
        out_specs=[VMEM_SPEC] * len(shapes),
        scratch_shapes=[pltpu.VMEM((width, rows), BF16), pltpu.VMEM((shards, block, half), BF16)],
        name="project_grads",
    )(*given)
    parts, at = [], 0
    for plan in plans:
        parts.append(list(flat[at : at + len(plan)]))
        at += len(plan)
    return parts


def adam_values(master, moment_one, second, gradient, step_rate, decay_rate):
    momentum = BETA_ONE * moment_one.astype(F32) + (1.0 - BETA_ONE) * gradient
    variance = BETA_TWO * second + (1.0 - BETA_TWO) * gradient * gradient
    momentum_hat = momentum / (1.0 - BETA_ONE**STEP)
    variance_hat = variance / (1.0 - BETA_TWO**STEP)
    updated = master - step_rate * (
        momentum_hat / (jnp.sqrt(variance_hat) + ADAM_EPS) + decay_rate * master
    )
    return updated, updated.astype(BF16), momentum, variance


def adam_feed(own, other, up_state, down_state, shards):
    block, columns = up_state[0].shape
    down_rows, width = down_state[0].shape
    piece = columns // (4 * shards)
    step = 8
    tiles = block // step

    def gradients(refs, core):
        own_refs, other_refs = refs[:4], refs[4:8]
        first = core == 0
        lows = [jnp.where(first, a[0], b[0]) for a, b in zip(own_refs, other_refs)]
        highs = [jnp.where(first, b[0], a[0]) for a, b in zip(own_refs, other_refs)]
        return lows, highs

    def body(*refs):
        core = lax.axis_index("rep") % 2
        lows, highs = gradients(refs, core)
        ups = refs[8:11]
        downs = refs[11:14]
        up_outs, down_outs = refs[14:18], refs[18:22]
        sources = (lows[0], lows[2], highs[0], highs[2])
        gradient = jnp.concatenate(
            [
                source[:, at * piece : (at + 1) * piece]
                for at in range(shards)
                for source in sources
            ],
            1,
        )
        values = adam_values(*[ref[...] for ref in ups], gradient, RATES[2], DECAYS[2])
        for out, value in zip(up_outs, values):
            out[...] = value
        for place, gradient in enumerate((lows[1], lows[3], highs[1], highs[3])):
            values = adam_values(*[ref[place] for ref in downs], gradient, RATES[3], DECAYS[3])
            for out, value in zip(down_outs, values):
                out[place] = value

    grads = [pl.BlockSpec((1, step * 2, g.shape[2]), lambda i: (0, i, 0)) for g in own]
    up_spec = pl.BlockSpec((step * 2, columns), lambda i: (i, 0))
    down_spec = pl.BlockSpec((4, step * 2, width), lambda i: (0, i, 0))
    kinds = (F32, BF16, F32, F32)
    downs = [value.reshape(4, block, width) for value in down_state]
    results = call(
        body,
        [array((block, columns), kind) for kind in kinds]
        + [array((4, block, width), kind) for kind in kinds],
        grid=(-(-block // (step * 2)),),
        in_specs=grads * 2 + [up_spec] * 3 + [down_spec] * 3,
        out_specs=[up_spec] * 4 + [down_spec] * 4,
        name="adam_feed",
    )(*own, *other, *up_state, *downs)
    return tuple(results[:4]), tuple(value.reshape(down_rows, width) for value in results[4:])


def adam_update(master, moment_one, second, gradient, step_rate, decay_rate):
    momentum = BETA_ONE * moment_one.astype(F32) + (1.0 - BETA_ONE) * gradient
    variance = BETA_TWO * second + (1.0 - BETA_TWO) * gradient * gradient
    momentum_hat = momentum / (1.0 - BETA_ONE**STEP)
    variance_hat = variance / (1.0 - BETA_TWO**STEP)
    updated = master - step_rate * (
        momentum_hat / (jnp.sqrt(variance_hat) + ADAM_EPS) + decay_rate * master
    )
    return (updated, updated.astype(BF16), momentum, variance)


def by_core(core, own, other, axis):
    return jnp.where(
        core == 0, jnp.concatenate([own, other], axis), jnp.concatenate([other, own], axis)
    )


def local(
    frames,
    upstream,
    lengths,
    master_qkv,
    master_out,
    master_up,
    master_down,
    master_small,
    first_qkv,
    first_out,
    first_up,
    first_down,
    first_small,
    second_qkv,
    second_out,
    second_up,
    second_down,
    second_small,
):
    half_rows, width = frames.shape
    shards, here = lax.axis_size("shard"), lax.axis_index("shard")
    rep = lax.axis_index("rep")
    core = rep % 2
    padded = -(-half_rows // 256) * 256
    rows = 2 * padded
    half = width // 2
    heads = half // HEAD_DIM
    units = master_up.shape[1] // 2
    unit_block = units // shards
    block = width // shards
    quarter = units // 2
    orders = gather_orders(shards)
    count = len(orders["xyz"])
    cut = 2 * block // 5
    small_rows = 16 * block // 80
    small_size = master_small.shape[0]

    both_moved = swap_clips(jnp.stack([frames, upstream]))
    low_qkv = lax.dynamic_slice_in_dim(master_qkv, core * half, half, 2).astype(BF16)
    low_out = lax.dynamic_slice_in_dim(master_out, core * half, half, 1).astype(BF16)
    low_small = jnp.pad(master_small.astype(BF16), (0, small_rows * half - small_size))
    first_wave = Doubling(
        [
            jnp.concatenate([low_qkv[0], low_out[:cut]], 0)[None],
            jnp.concatenate([low_qkv[1], low_out[cut : 2 * cut]], 0)[None],
            jnp.concatenate(
                [low_qkv[2], low_out[2 * cut :], low_small.reshape(small_rows, half)], 0
            )[None],
        ],
        [orders["xzy"], orders["yxz"], orders["zyx"]],
    )
    first_wave.start()

    low_up = lax.dynamic_index_in_dim(
        master_up.reshape(block, shards, 2, 2, unit_block // 2), core, 2, keepdims=False
    ).astype(BF16)
    low_down = lax.dynamic_slice_in_dim(master_down, core * unit_block, unit_block, 0).astype(BF16)
    low_ups = [low_up[:, :, index].reshape(block, quarter) for index in range(2)]
    wave = Doubling(
        [low_ups[0][None], low_down[None, :block], low_ups[1][None], low_down[None, block:]],
        [orders["zyx"], orders["xzy"], orders["xzy"], orders["yzx"]],
    )

    held = first_wave.finish()
    wave.behind(*held)
    wave.start()
    for step in range(1, count - 1):
        first_wave.start()
        held = first_wave.finish()
    both_own = jnp.pad(after(both_moved, *held), ((0, 0), (0, padded - half_rows), (0, 0)))
    held = wave.finish(both_own)
    first_wave.behind(*held)
    first_wave.start()
    wave_a, wave_b = wave.pair(0), wave.pair(2)
    for step in range(1, count - 3):
        wave_a.start()
        wave_a.finish()
        wave_b.start()
        wave_b.finish()
    wave_a.start()
    w_qkv, w_out_own, small = place_first(first_wave.halves(), shards, block, half, cut, small_rows)
    both_other, w_out_other = (
        across_cores(after(both_own, *first_wave.got)),
        across_cores(after(w_out_own, *wave_a.got).reshape(width, half)),
    )
    w_qkv, w_out_own = w_qkv.reshape(width, 3 * half), w_out_own.reshape(width, half)
    small = small.reshape(shards, -1)[:, :small_size].reshape(-1).astype(F32)
    wave_b.behind(w_qkv)
    wave_b.start()
    held_a = wave_a.finish(w_qkv)
    wave_a.start()

    pieces = [small[index * width : (index + 1) * width] for index in range(8)]
    gain_one, shift_one, bias_query, bias_value, bias_out, gain_two, shift_two, bias_down = [
        piece[None] for piece in pieces
    ]
    bias_up = lax.dynamic_index_in_dim(
        small[8 * width :].reshape(shards, 2, 2, unit_block // 2), core, 1, keepdims=False
    )
    bias_query = lax.dynamic_slice_in_dim(bias_query, core * half, half, 1)
    bias_value = lax.dynamic_slice_in_dim(bias_value, core * half, half, 1)
    bias_qkv = jnp.concatenate([bias_query, jnp.zeros_like(bias_query), bias_value], 1)

    rep_of_clip = 2 * (rep // 2) + here % 2
    clip = (rep_of_clip * shards + here) // 2
    length = lax.dynamic_index_in_dim(lengths, clip, 0, keepdims=False)
    steps = jnp.arange(padded, dtype=jnp.int32)
    positions = jnp.concatenate([core * half_rows + steps, (1 - core) * half_rows + steps])
    real = jnp.concatenate([steps, steps]) < half_rows
    fill = jnp.where(real & (positions < length), 0.0, NEG_FILL).astype(BF16)
    first_row = jnp.arange(MASK_ROWS)[:, None] == 0
    masks = jnp.concatenate(
        [
            jnp.where(first_row, fill[None, :], 0.0),
            jnp.broadcast_to(jnp.where(first_row, 1.0, 0.0), (MASK_ROWS, rows)),
        ],
        0,
    ).astype(BF16)

    normed_one, qkv = project(
        after(both_own, *held_a, *wave_b.held, w_out_other),
        both_other,
        gain_one,
        shift_one,
        w_qkv,
        bias_qkv,
    )
    held = wave_a.finish(qkv) + wave_b.finish(qkv)
    wave_a.start()
    wave_b.start()
    qkv = qkv.reshape(3, heads, HEAD_DIM, rows)
    some = heads // 2
    context_a, lse_a = attend(after(qkv, *held), masks, 0, some)
    context_b, lse_b = attend(after(qkv, context_a), masks, some, heads - some)
    flat_a = context_a.reshape(half // 2, rows)
    flat_b = context_b.reshape(half // 2, rows)
    wave_a.finish(context_b)
    held = wave_b.finish(context_b)
    wave_b.start()
    got_a = across_cores(after(flat_a, *wave_a.got, *held))
    got_b = across_cores(after(flat_b, *wave_a.got, *held))
    middle, normed_own = attended(
        (flat_a, flat_b), (got_a, got_b), w_out_own, w_out_other, both_own, bias_out, gain_two, shift_two
    )
    normed_other = across_cores(normed_own)

    back = {name: order[::-1] for name, order in orders.items()}
    feed_names = (("zxy", "yxz"), ("zxy", "xyz"))
    groups = []

    def feed_half(index, weights, *behind):
        names = feed_names[index]
        sums, up_parts, down_parts = feed(
            after(normed_own, *behind),
            normed_other,
            both_own,
            both_other,
            weights,
            bias_up[:, index].reshape(1, quarter),
            [scatter_plan(back[name]) for name in names],
        )
        return sums, Halving([list(up_parts), list(down_parts)], [back[name] for name in names])

    (mixed_a, grad_a, send_a, sums_up_a), chunks_a = feed_half(0, wave_a.halves(), *held)
    sent = chunks_a.step()
    got_sums_a = across_cores(send_a)
    wave_b.finish(grad_a)
    (mixed_b, grad_b, send_b, sums_up_b), chunks_b = feed_half(1, wave_b.halves(), *sent, send_a)
    arrived = [after(got[0], grad_b) for got in chunks_a.got]
    chunks_a.got = [[got] for got in arrived]
    got_sums_a = after(got_sums_a, grad_b)
    got_sums_b = across_cores(after(send_b, got_sums_a, *arrived))
    grad_middle, grad_attended, sums_two = norm_back(
        (grad_a, grad_b, (got_sums_a, 0), (got_sums_b, 0)),
        middle,
        gain_two,
        (both_own, 1),
        True,
    )
    grad_attended_other = across_cores(grad_attended)
    sent = chunks_b.step(grad_attended_other)
    sent = sent + chunks_a.step(grad_attended_other)
    grad_context, out_parts = attended_back(
        after(grad_attended, *sent),
        grad_attended_other,
        w_out_own,
        w_out_other,
        (flat_a, flat_b),
        (got_a, got_b),
        scatter_plan(back["xyz"]),
        shards,
    )
    chunks_out = Halving([list(out_parts)], [back["xyz"]])
    grad_context = grad_context.reshape(heads, HEAD_DIM, rows)
    calls = 4
    each = heads // calls
    grads = []
    sent = []
    for index in range(calls):
        inside = index * each
        context, lse = (context_a, lse_a) if inside < some else (context_b, lse_b)
        grads.append(
            attend_back(
                after(qkv, *sent), masks, grad_context, context, lse, inside, inside % some, each
            )
        )
        done = grads[-1][0]
        if index == 0:
            mixed = after(mixed_a, done) + mixed_b + got_sums_a[1].astype(F32) + got_sums_b[1].astype(F32)
            mixed = (mixed + bias_down + middle)[:half_rows]
            sent = [mixed] + chunks_out.step(mixed)
        elif index == 1:
            for _ in range(count - 4):
                chunks_a.step(done)
            sent = chunks_a.step(done)
            sent = sent + chunks_b.step(done) + chunks_out.step(done)
        elif index == 2:
            sent = chunks_a.step(done)
            sent = sent + chunks_b.step(done) + chunks_out.step(done)
            for _ in range(count - 4):
                sent = chunks_b.step() + chunks_out.step()
            mixed = after(mixed, *sent)
            sent = sent + [mixed]
            swapped_mixed = swap_clips(mixed)
        else:
            own_a = chunks_a.result(done)
            sent = chunks_b.step(done) + own_a + chunks_out.step(done)
    flat = [[piece[which].reshape(each * HEAD_DIM, rows) for piece in grads] for which in range(3)]
    flat[0][0] = after(flat[0][0], *sent)
    partial_one, send_one = project_back([piece for group in flat for piece in group], w_qkv)
    mixed = after(swapped_mixed, partial_one)
    own_b = chunks_b.result(partial_one)
    (own_out,) = chunks_out.result(partial_one)
    got_one = across_cores(after(send_one, mixed, *own_b, own_out))
    early = [over_groups(value) for value in own_a + own_b + [own_out]]
    cut_rows = block // 2
    wide_out = jnp.concatenate([early[4][:, :cut_rows], early[4][:, cut_rows:]], 2)
    early_other = across_cores(jnp.concatenate(early[:4] + [wide_out], 1))
    grad_frames, sums_one = norm_back(
        (partial_one, got_one), (both_own, 0), gain_one, grad_middle, False
    )
    early_send = grad_frames[:half_rows]
    swapped = swap_clips(early_send)
    names = ("zxy", "xyz", "yzx")
    parts = project_grads(
        after(normed_one, early_send), flat, [scatter_plan(back[name]) for name in names]
    )
    early_other = after(early_other, parts[0][0])
    splits = [early_other[:, i * block : (i + 1) * block] for i in range(4)]
    wide_out = early_other[:, 4 * block :]
    early_other = splits + [jnp.concatenate([wide_out[:, :, :half], wide_out[:, :, half:]], 1)]
    chunks_late = Halving(parts, [back[name] for name in names])
    sent = chunks_late.step(early_other[0])

    def in_half(values):
        return lax.dynamic_update_slice_in_dim(jnp.zeros((width,), F32), values, core * half, 0)

    def head_sums(pieces_of):
        return in_half(jnp.concatenate([jnp.sum(piece.astype(F32), 1) for piece in pieces_of]))

    sums_up = jnp.stack([sums.reshape(shards, unit_block // 2) for sums in (sums_up_a, sums_up_b)], 1)
    sums_up_all = lax.dynamic_update_slice_in_dim(
        jnp.zeros((shards, 2, unit_block), F32), sums_up.reshape(shards, 1, unit_block), core, 1
    )
    grad_small = jnp.concatenate(
        [
            sums_one[0],
            sums_one[1],
            head_sums(flat[0]),
            head_sums(flat[2]),
            sums_two[2],
            sums_two[0],
            sums_two[1],
            sums_two[3],
            sums_up_all.reshape(-1),
        ]
    ).reshape(shards, small_size)
    new_up, new_down = adam_feed(
        [after(early[0], *sent)] + early[1:4],
        early_other[:4],
        (master_up, first_up, second_up),
        (master_down, first_down, second_down),
        shards,
    )
    grad_frames = after(swapped, new_up[0])
    sent = chunks_late.step(new_up[0], grad_frames)
    total_small = reduce_small(after(grad_small, *sent))
    total_out = by_core(core, early[4][0], after(early_other[4], *sent)[0], 1)
    while len(chunks_late.got[0]) < count:
        sent = chunks_late.step()
    late = over_groups(jnp.concatenate(chunks_late.result(), 0))
    late_other = across_cores(late)
    total_qkv = by_core(core, late, late_other, 2)

    new_qkv = adam_update(master_qkv, first_qkv, second_qkv, total_qkv, RATES[0], DECAYS[0])
    new_out = adam_update(master_out, first_out, second_out, total_out, RATES[1], DECAYS[1])
    new_small = adam_update(
        master_small, first_small, second_small, total_small, RATES[4], DECAYS[4]
    )
    return (mixed, grad_frames) + new_qkv + new_out + new_up + new_down + new_small


def solution(mesh):
    rows = P(("rep", "shard"), None)
    weights = (P(None, "shard", None), P("shard", None), P("shard", None), P("shard", None), P("shard"))
    outs = (rows, rows)
    for spec in weights:
        outs = outs + (spec,) * 4
    return jax.shard_map(
        local,
        mesh=mesh,
        in_specs=(rows, rows, P()) + weights * 3,
        out_specs=outs,
        check_vma=False,
    )
```

```python
import functools
import math

import jax
import jax.numpy as jnp
from jax import lax
from jax.experimental import pallas as pl
from jax.experimental.pallas import tpu as pltpu
from jax.sharding import PartitionSpec as P

HEAD_DIM = 80
STEP = 10

LN_EPS = 1e-05
NEG_FILL = -1e30
BETA_ONE = 0.5
BETA_TWO = 0.5
ADAM_EPS = 1e-08
RATES = (0.04, 0.5, 0.04, 0.02, 0.3)
DECAYS = (0.01, 0.01, 0.01, 0.01, 0.0)

F32 = jnp.float32
BF16 = jnp.bfloat16
MIB = 1024 * 1024
SCALING = HEAD_DIM**-0.5
SCORE_SCALE = SCALING * math.log2(math.e)
MASK_ROWS = 16
SMALL_COST = pl.CostEstimate(flops=0, bytes_accessed=MIB, transcendentals=0)
VMEM_SPEC = pl.BlockSpec(memory_space=pltpu.VMEM)
ANY_SPEC = pl.BlockSpec(memory_space=pl.ANY)
NN = (((1,), (0,)), ((), ()))
NT = (((1,), (1,)), ((), ()))


def product(left, right, dims=NN):
    return lax.dot_general(left, right, dims, preferred_element_type=F32)


def call(body, out_shape, limit=48, **options):
    return pl.pallas_call(
        body,
        out_shape=out_shape,
        compiler_params=pltpu.CompilerParams(vmem_limit_bytes=limit * MIB),
        cost_estimate=SMALL_COST,
        **options,
    )


def array(shape, dtype):
    return jax.ShapeDtypeStruct(tuple(shape), dtype)


def xor_pairs(count, mask):
    return [(source, source ^ mask) for source in range(count)]


def across_cores(value):
    return lax.ppermute(value, "rep", xor_pairs(lax.axis_size("rep"), 1))


def swap_pairs():
    reps, shards = lax.axis_size("rep"), lax.axis_size("shard")
    pairs = []
    for rep in range(reps):
        for shard in range(shards):
            if (rep % 2) != (shard % 2):
                pairs.append((rep * shards + shard, (rep ^ 1) * shards + (shard ^ 1)))
    return pairs


def swap_clips(own, sent):
    got = lax.ppermute(sent, ("rep", "shard"), swap_pairs())
    moved = (lax.axis_index("rep") % 2) != (lax.axis_index("shard") % 2)

    def finish(*behind):
        arrived = (after(got, *behind) if behind else got)[: own.shape[0]]
        return jnp.where(moved, arrived.astype(own.dtype), own)

    return finish, got


def after(value, *others):
    return lax.optimization_barrier((value,) + others)[0]


def flip(index, mask):
    out, bit = index, 1
    while bit <= mask:
        if mask & bit:
            out = out + bit * (1 - 2 * ((index // bit) % 2))
        bit *= 2
    return out


def gather_orders(shards):
    far = [1 << k for k in range(int(math.log2(shards)))][::-1]
    most = [b for b in far if b >= 8]
    axes = {"x": 1, "y": 2, "z": 4}
    names = ("xyz", "xzy", "yxz", "yzx", "zxy", "zyx")
    return {name: most + [axes[axis] for axis in name] for name in names}


def relative_places(order):
    places = [0]
    for mask in order:
        places = places + [mask ^ r for r in places]
    return places


class Doubling:
    def __init__(self, blocks, orders):
        self.held, self.orders, self.step, self.got = blocks, orders, 0, None

    def behind(self, *others):
        self.held = [after(held, *others) for held in self.held]

    def start(self):
        shards = lax.axis_size("shard")
        masks = [order[self.step] for order in self.orders]
        if self.step == 0:
            rows = [held.shape[1] for held in self.held]
            together = jnp.concatenate(self.held, 1)
            together = lax.ppermute(together, "shard", xor_pairs(shards, masks[0]))
            ends = [sum(rows[: i + 1]) for i in range(len(rows))]
            self.got = [together[:, end - row : end] for end, row in zip(ends, rows)]
        else:
            self.got = [
                lax.ppermute(held, "shard", xor_pairs(shards, mask))
                for held, mask in zip(self.held, masks)
            ]
        self.step += 1

    def finish(self, *behind):
        if behind:
            self.got = [after(got, *behind) for got in self.got]
        if self.step < len(self.orders[0]):
            self.held = [jnp.concatenate(pair, 0) for pair in zip(self.held, self.got)]
        return self.held

    def halves(self):
        return list(zip(self.held, self.got, self.orders))

    def pair(self, at):
        part = Doubling(self.held[at : at + 2], self.orders[at : at + 2])
        part.step = self.step
        return part


def scatter_plan(order):
    kept = [0]
    sent = []
    for mask in order[::-1]:
        sent.append([mask ^ r for r in kept])
        kept = kept + sent[-1]
    return sent[::-1] + [[0]]


class Halving:
    def __init__(self, chunks, orders):
        self.chunks, self.orders = chunks, orders
        self.got = [[] for _ in chunks]

    def step(self, *behind):
        index = len(self.got[0])
        shards = lax.axis_size("shard")
        sends = [chunk[index] for chunk in self.chunks]
        if behind:
            sends = [after(send, *behind) for send in sends]
        if index:
            sends = add_blocks(sends, self.got, 1, BF16)
        masks = [order[index] for order in self.orders]
        if index == len(self.orders[0]) - 1 and len(sends) > 1:
            rows = [send.shape[1] for send in sends]
            together = jnp.concatenate(sends, 1)
            together = lax.ppermute(together, "shard", xor_pairs(shards, masks[0]))
            ends = [sum(rows[: i + 1]) for i in range(len(rows))]
            arrived = [together[:, end - row : end] for end, row in zip(ends, rows)]
        else:
            arrived = [
                lax.ppermute(send, "shard", xor_pairs(shards, mask))
                for send, mask in zip(sends, masks)
            ]
        for got, new in zip(self.got, arrived):
            got.append(new)
        return sends

    def result(self, *behind):
        stays = [chunk[-1] for chunk in self.chunks]
        if behind:
            stays = [after(stay, *behind) for stay in stays]
        return add_blocks(stays, self.got, 0, F32)


def over_groups(value):
    reps = lax.axis_size("rep")
    mask = 2
    while mask < reps:
        value = value + lax.ppermute(value, "rep", xor_pairs(reps, mask))
        mask *= 2
    return value


class SmallSum:
    def __init__(self, vector):
        self.held, self.mask = vector, vector.shape[0] // 2
        self.kept = self.got = None

    def start(self):
        shards, here = lax.axis_size("shard"), lax.axis_index("shard")
        upper = (here // self.mask) % 2 == 1
        low, high = self.held[: self.mask], self.held[self.mask :]
        self.kept = jnp.where(upper, high, low)
        self.got = lax.ppermute(
            jnp.where(upper, low, high), "shard", xor_pairs(shards, self.mask)
        )
        self.mask //= 2

    def finish(self, *behind):
        self.held = self.kept + (after(self.got, *behind) if behind else self.got)
        return self.held

    def result(self):
        while self.mask >= 1:
            self.start()
            self.finish()
        reps = lax.axis_size("rep")
        held, mask = self.held[0], 1
        while mask < reps:
            held = held + lax.ppermute(held, "rep", xor_pairs(reps, mask))
            mask *= 2
        return held


def row_slice(start, size):
    return pl.ds(pl.multiple_of(start, 8), size)


def place_first(halves, shards, block, half, cut, small_rows):
    rest = block - 2 * cut

    def body(*refs):
        ins, (qkv, out, small) = refs[:6], refs[6:]
        here = lax.axis_index("shard")
        for index, (low, _, order) in enumerate(halves):
            for place, rel in enumerate(relative_places(order)):
                ref = ins[2 * index + place // low.shape[0]].at[place % low.shape[0]]
                at = flip(here, rel)
                qkv[at, :, index * half : (index + 1) * half] = ref[:block, :]
                if index < 2:
                    out[at, index * cut : (index + 1) * cut, :] = ref[block : block + cut, :]
                else:
                    out[at, 2 * cut :, :] = ref[block : block + rest, :]
                    small[at] = ref[block + rest :, :]

    shapes = (
        array((shards, block, 3 * half), BF16),
        array((shards, block, half), BF16),
        array((shards, small_rows, half), BF16),
    )
    return call(
        body, shapes, in_specs=[VMEM_SPEC] * 6, out_specs=[VMEM_SPEC] * 3, name="place_first"
    )(*[part for low, got, _ in halves for part in (low, got)])


def write_parts(outs, plan, source, here):
    for out, part in zip(outs, plan):
        for place, rel in enumerate(part):
            out[place] = source[flip(here, rel)]


def add_blocks(firsts, others, place, dtype):
    inputs, specs = [], []
    for first, rest in zip(firsts, others):
        inputs.append(first)
        specs.append(pl.BlockSpec(first.shape, lambda i: (0, 0, 0)))
        for other in rest:
            inputs.append(other)
            specs.append(pl.BlockSpec(first.shape, lambda i, at=place: (at, 0, 0)))

    def body(*refs):
        at = 0
        for index, rest in enumerate(others):
            total = refs[at][...].astype(F32)
            for ref in refs[at + 1 : at + 1 + len(rest)]:
                total = total + ref[...].astype(F32)
            refs[len(inputs) + index][...] = total.astype(dtype)
            at += 1 + len(rest)

    return list(call(
        body,
        [array(first.shape, dtype) for first in firsts],
        grid=(1,),
        in_specs=specs,
        out_specs=[pl.BlockSpec(first.shape, lambda i: (0, 0, 0)) for first in firsts],
        name="add_blocks",
    )(*inputs))


def part_shapes(plan, rows, width):
    return [array((len(part), rows, width), BF16) for part in plan]


def norm_rows(values):
    center = values - jnp.mean(values, -1, keepdims=True)
    spread = jnp.mean(center * center, -1, keepdims=True)
    inverse = lax.rsqrt(spread + LN_EPS)
    return center * inverse, inverse


def project(own, other, gain, shift, w_qkv, bias):
    padded, width = own.shape
    columns = w_qkv.shape[1]
    third = columns // 3
    step = padded // 2

    def body(own_ref, other_ref, gain_ref, shift_ref, w_ref, bias_ref, normed_ref, out_ref):
        index = pl.program_id(0)
        values = jnp.where(index < 2, own_ref[...], other_ref[...]).astype(F32)
        unit, _ = norm_rows(values)
        normed = (unit * gain_ref[...] + shift_ref[...]).astype(BF16)
        normed_ref[...] = normed
        for part in range(3):
            cols = slice(part * third, (part + 1) * third)
            result = product(normed, w_ref[:, cols]) + bias_ref[:, cols]
            out_ref[cols, :] = result.astype(BF16).T

    line = pl.BlockSpec((1, width), lambda i: (0, 0))
    return call(
        body,
        (array((2 * padded, width), BF16), array((columns, 2 * padded), BF16)),
        grid=(4,),
        in_specs=[
            pl.BlockSpec((step, width), lambda i: (jnp.minimum(i, 1), 0)),
            pl.BlockSpec((step, width), lambda i: (jnp.maximum(i - 2, 0), 0)),
            line,
            line,
            pl.BlockSpec((width, columns), lambda i: (0, 0)),
            pl.BlockSpec((1, columns), lambda i: (0, 0)),
        ],
        out_specs=(
            pl.BlockSpec((step, width), lambda i: (i, 0)),
            pl.BlockSpec((columns, step), lambda i: (0, i)),
        ),
        name="project",
    )(own, other, gain, shift, w_qkv, bias)


def attend_kernel(mask_ref, q_ref, k_ref, v_ref, out_ref, lse_ref, kt, qt, *, step):
    dim, keys = k_ref.shape
    kt[...] = jnp.zeros_like(kt)
    kt[:dim, :] = k_ref[...]
    kt[dim : dim + MASK_ROWS, :] = mask_ref[:MASK_ROWS, :]
    k_rows = kt[...].T
    qt[...] = jnp.zeros_like(qt)
    qt[:dim, :] = q_ref[...]
    qt[dim : dim + MASK_ROWS, :] = mask_ref[MASK_ROWS:, :]
    for start in range(0, keys, step):
        cols = slice(start, start + step)
        scores = jnp.dot(k_rows, qt[:, cols], preferred_element_type=F32)
        top = jnp.max(scores, 0, keepdims=True) * SCORE_SCALE
        powers = jnp.exp2(scores * SCORE_SCALE - top)
        total = jnp.sum(powers, 0, keepdims=True)
        context = jnp.dot(v_ref[...], powers.astype(BF16), preferred_element_type=F32)
        out_ref[:, cols] = (context / total).astype(BF16)
        lse_ref[:, cols] = top + jnp.log2(total)


def attend(qkv, masks, first, heads):
    _, _, dim, rows = qkv.shape
    step = 512

    def head_block(which):
        return pl.BlockSpec((None, None, dim, rows), lambda h: (which, first + h, 0, 0))

    return pl.pallas_call(
        functools.partial(attend_kernel, step=step),
        grid=(heads,),
        out_shape=(
            jax.ShapeDtypeStruct((heads, dim, rows), BF16),
            jax.ShapeDtypeStruct((heads, 1, rows), F32),
        ),
        in_specs=[
            pl.BlockSpec(masks.shape, lambda h: (0, 0)),
            head_block(0),
            head_block(1),
            head_block(2),
        ],
        out_specs=(
            pl.BlockSpec((None, dim, rows), lambda h: (h, 0, 0)),
            pl.BlockSpec((None, 1, rows), lambda h: (h, 0, 0)),
        ),
        scratch_shapes=[pltpu.VMEM((128, rows), BF16), pltpu.VMEM((128, rows), BF16)],
        compiler_params=pltpu.CompilerParams(vmem_limit_bytes=48 * MIB),
        cost_estimate=SMALL_COST,
        name="attend",
    )(masks, qkv, qkv, qkv)


def attend_back_kernel(
    mask_ref, q_ref, k_ref, v_ref, g_ref, ctx_ref, lse_ref, gq_ref, gk_ref, gv_ref, kt, qt, pad, acc_k, acc_v, *, step
):
    dim, keys = k_ref.shape
    kt[...] = jnp.zeros_like(kt)
    kt[:dim, :] = k_ref[...]
    kt[dim : dim + MASK_ROWS, :] = mask_ref[:MASK_ROWS, :]
    k_rows = kt[...].T
    pad[...] = jnp.zeros_like(pad)
    pad[:dim, :] = v_ref[...]
    v_rows = pad[...].T
    qt[...] = jnp.zeros_like(qt)
    qt[:dim, :] = q_ref[...]
    qt[dim : dim + MASK_ROWS, :] = mask_ref[MASK_ROWS:, :]
    q_rows = qt[...].T
    pad[:dim, :] = g_ref[...]
    g_rows = pad[...].T
    inner = jnp.sum(g_ref[...].astype(F32) * ctx_ref[...].astype(F32), 0, keepdims=True)
    for start in range(0, keys, step):
        cols = slice(start, start + step)
        scores = jnp.dot(k_rows, qt[:, cols], preferred_element_type=F32)
        probs = jnp.exp2(scores * SCORE_SCALE - lse_ref[:, cols])
        grad_probs = jnp.dot(v_rows, pad[:, cols], preferred_element_type=F32)
        grad_scores = (probs * (grad_probs - inner[:, cols])).astype(BF16)
        part_v = jnp.dot(probs.astype(BF16), g_rows[cols, :], preferred_element_type=F32)
        part_k = jnp.dot(grad_scores, q_rows[cols, :], preferred_element_type=F32)
        if start == 0:
            acc_v[...] = part_v
            acc_k[...] = part_k
        else:
            acc_v[...] += part_v
            acc_k[...] += part_k
        grad_query = jnp.dot(k_ref[...], grad_scores, preferred_element_type=F32)
        gq_ref[:, cols] = (grad_query * SCALING).astype(BF16)
    gv_ref[...] = acc_v[...].T[:dim, :].astype(BF16)
    gk_ref[...] = (acc_k[...].T[:dim, :] * SCALING).astype(BF16)


def attend_back(qkv, masks, grad_context, context, lse, first, inside, heads):
    _, dim, rows = context.shape
    step = 512

    def head_block(which):
        return pl.BlockSpec((None, None, dim, rows), lambda h: (which, first + h, 0, 0))

    plain = pl.BlockSpec((None, dim, rows), lambda h: (h, 0, 0))
    return pl.pallas_call(
        functools.partial(attend_back_kernel, step=step),
        grid=(heads,),
        out_shape=[jax.ShapeDtypeStruct((heads, dim, rows), BF16)] * 3,
        in_specs=[
            pl.BlockSpec(masks.shape, lambda h: (0, 0)),
            head_block(0),
            head_block(1),
            head_block(2),
            pl.BlockSpec((None, dim, rows), lambda h: (first + h, 0, 0)),
            pl.BlockSpec((None, dim, rows), lambda h: (inside + h, 0, 0)),
            pl.BlockSpec((None, 1, rows), lambda h: (inside + h, 0, 0)),
        ],
        out_specs=[plain] * 3,
        scratch_shapes=[pltpu.VMEM((128, rows), BF16)] * 3 + [pltpu.VMEM((rows, 128), F32)] * 2,
        compiler_params=pltpu.CompilerParams(vmem_limit_bytes=48 * MIB),
        cost_estimate=SMALL_COST,
        name="attend_back",
    )(masks, qkv, qkv, qkv, grad_context, context, lse)


def attended(contexts, gots, w_own, w_other, frames, bias, gain, shift):
    padded, width = frames.shape
    half = width // 2
    step = 256
    tiles = padded // step

    def body(ca, cb, ga, gb, wo_ref, wt_ref, frames_ref, bias_ref, gain_ref, shift_ref, middle_ref, normed_ref):
        first = lax.axis_index("rep") % 2 == 0
        own = jnp.concatenate([ca[...], cb[...]], 0)
        got = jnp.concatenate([ga[...], gb[...]], 0)
        low = jnp.where(first, own, got).T
        high = jnp.where(first, got, own).T
        by_own = product(low, wo_ref[:half, :]) + product(high, wo_ref[half:, :])
        by_other = product(low, wt_ref[:half, :]) + product(high, wt_ref[half:, :])
        result = jnp.concatenate(
            [jnp.where(first, by_own, by_other), jnp.where(first, by_other, by_own)], 1
        )
        middle = result + frames_ref[...].astype(F32) + bias_ref[...]
        middle_ref[...] = middle
        unit, _ = norm_rows(middle)
        normed_ref[...] = (unit * gain_ref[...] + shift_ref[...]).astype(BF16)

    part = half // 2
    line = pl.BlockSpec((1, width), lambda i: (0, 0))
    here = pl.BlockSpec((part, step), lambda i: (0, i))
    there = pl.BlockSpec((part, step), lambda i: (0, i + tiles))
    matrix = pl.BlockSpec((width, half), lambda i: (0, 0))
    rows = pl.BlockSpec((step, width), lambda i: (i, 0))
    return call(
        body,
        (array((padded, width), F32), array((padded, width), BF16)),
        grid=(tiles,),
        in_specs=[here, here, there, there, matrix, matrix, rows, line, line, line],
        out_specs=(rows, rows),
        name="attended",
    )(*contexts, *gots, w_own, w_other, frames, bias, gain, shift)


def feed(own, other, up_own, up_other, weights, bias, plans):
    padded, width = own.shape
    stacks_given = [part for halves in weights for part in halves[:2]] if isinstance(weights, list) else [weights]
    count_in = len(stacks_given)
    block, units = stacks_given[0].shape[-2:]
    shards = width // block
    tile = 256
    tiles = units // tile
    up_plan, down_plan = plans

    def body(*refs):
        x_refs, u_refs = refs[0:2], refs[2:4]
        stacks, refs = refs[4 : 4 + count_in], refs[4 + count_in :]
        bias_ref, mixed_own, grad_own, send, sums_ref = refs[:5]
        up_outs = refs[5 : 5 + len(up_plan)]
        down_outs = refs[5 + len(up_plan) : 5 + len(up_plan) + len(down_plan)]
        w_up, w_down, hidden_t, x_t, grad_pre, hidden, blocks, sems = refs[5 + len(up_plan) + len(down_plan) :]
        index = pl.program_id(0)
        here = lax.axis_index("shard")

        def rows_step(which):
            x_ref, u_ref = x_refs[which], u_refs[which]
            cols = slice(which * padded, (which + 1) * padded)
            wu, wd = w_up[...].reshape(width, units), w_down[...].reshape(units, width)

            def products(t):
                part = slice(t * tile, (t + 1) * tile)
                return product(x_ref[...], wu[:, part]), product(u_ref[...], wd[part, :], NT)

            ahead = products(0)
            for t in range(tiles):
                part = slice(t * tile, (t + 1) * tile)
                pre, grad_hidden = ahead
                if t + 1 < tiles:
                    ahead = products(t + 1)
                pre = pre + bias_ref[:, part]
                phi = 0.5 + 0.5 * lax.erf(pre * (0.5**0.5))
                hid = (pre * phi).astype(BF16)
                hidden[:, part] = hid
                hidden_t[part, cols] = hid.T
                density = jnp.exp(pre * pre * -0.5) * (1.0 / math.sqrt(2.0 * math.pi))
                grad = (grad_hidden * (phi + pre * density)).astype(BF16)
                grad_pre[cols, part] = grad
                total = jnp.sum(grad.astype(F32), 0, keepdims=True)
                if which == 1:
                    sums_ref[:, part] = total
                else:
                    sums_ref[:, part] += total
            mixed_ref, grad_ref = ((mixed_own, grad_own), (send.at[1], send.at[0]))[which]
            for t in range(width // tile):
                part = slice(t * tile, (t + 1) * tile)
                mixed_ref[:, part] = product(hidden[...], wd[:, part]).astype(mixed_ref.dtype)
                grad_ref[:, part] = product(grad_pre[cols, :], wu[part, :], NT).astype(grad_ref.dtype)

        @pl.when(index == 0)
        def _():
            copies = []

            def copy_in(source, matrix, at):
                copies.append(pltpu.make_async_copy(source, matrix.at[at], sems.at[len(copies)]))
                copies[-1].start()

            for which, matrix in enumerate((w_up, w_down)):
                if count_in == 1:
                    for at in range(shards):
                        copy_in(stacks[0].at[at, which], matrix, at)
                else:
                    for place, rel in enumerate(relative_places(weights[which][2])):
                        stack = stacks[2 * which + place // (shards // 2)]
                        copy_in(stack.at[place % (shards // 2)], matrix, flip(here, rel))
            for which in range(2):
                x_t[:, which * padded : (which + 1) * padded] = x_refs[which][...].T
            for copy in copies:
                copy.wait()
            rows_step(1)

        @pl.when(index == 1)
        def _():
            rows_step(0)

        @pl.when(index >= 2)
        def _():
            part = pl.ds(pl.multiple_of((index - 2) * tile, tile), tile)
            down = product(hidden_t[:, :padded], u_refs[0][:, part]) + product(
                hidden_t[:, padded:], u_refs[1][:, part]
            )
            blocks[...] = down.astype(BF16).reshape(shards, block, tile)
            write_parts(down_outs, down_plan, blocks, here)
            up = product(x_t[...], grad_pre[:, part])
            blocks[...] = up.astype(BF16).reshape(shards, block, tile)
            write_parts(up_outs, up_plan, blocks, here)

    once = pl.Buffered(1)
    whole = pl.BlockSpec((padded, width), lambda i: (0, 0), pipeline_mode=once)
    line = pl.BlockSpec((1, units), lambda i: (0, 0))
    shapes = [
        array((padded, width), F32),
        array((padded, width), F32),
        array((2, padded, width), BF16),
        array((1, units), F32),
    ]
    specs = [
        whole,
        whole,
        pl.BlockSpec((2, padded, width), lambda i: (0, 0, 0), pipeline_mode=once),
        line,
    ]
    for plan, size in ((up_plan, units), (down_plan, width)):
        shapes += part_shapes(plan, block, size)
        specs += [
            pl.BlockSpec((len(part), block, tile), lambda i: (0, 0, jnp.maximum(i - 2, 0)))
            for part in plan
        ]
    results = call(
        body,
        shapes,
        limit=60,
        grid=(2 + tiles,),
        in_specs=[whole] * 4 + [ANY_SPEC] * count_in + [line],
        out_specs=specs,
        scratch_shapes=[
            pltpu.VMEM((shards, block, units), BF16),
            pltpu.VMEM((shards, block, width), BF16),
            pltpu.VMEM((units, 2 * padded), BF16),
            pltpu.VMEM((width, 2 * padded), BF16),
            pltpu.VMEM((2 * padded, units), BF16),
            pltpu.VMEM((padded, units), BF16),
            pltpu.VMEM((shards, block, tile), BF16),
            pltpu.SemaphoreType.DMA((2 * shards,)),
        ],
        name="feed",
    )(own, other, up_own, up_other, *stacks_given, bias)
    count = 4 + len(up_plan)
    return results[:4], results[4:count], results[count:]


def norm_back(sums, values, gain, base, more_sums):
    given = [item if isinstance(item, tuple) else (item, None) for item in (*sums, values, base)]
    padded, width = given[0][0].shape[-2:]
    step = 256

    def body(*refs):
        parts = refs[: len(sums)]
        values_ref, base_ref, gain_ref = refs[len(parts) : len(parts) + 3]
        outs = refs[len(parts) + 3 :]
        sums_ref = outs[-1]
        grads = parts[0][...].astype(F32)
        for ref in parts[1:]:
            grads = grads + ref[...].astype(F32)
        unit, inverse = norm_rows(values_ref[...].astype(F32))
        scaled = grads * gain_ref[...]
        inner = (
            scaled
            - jnp.mean(scaled, -1, keepdims=True)
            - unit * jnp.mean(scaled * unit, -1, keepdims=True)
        )
        result = base_ref[...].astype(F32) + inverse * inner
        outs[0][...] = result
        low = result.astype(BF16)
        outs[1][...] = low
        lines = [jnp.sum(grads * unit, 0, keepdims=True), jnp.sum(grads, 0, keepdims=True)]
        if more_sums:
            lines.append(jnp.sum(low.astype(F32), 0, keepdims=True))
            lines.append(jnp.sum(base_ref[...].astype(F32), 0, keepdims=True))

        @pl.when(pl.program_id(0) == 0)
        def _():
            sums_ref[...] = jnp.zeros_like(sums_ref)

        for place, line in enumerate(lines):
            sums_ref[place : place + 1, :] += line

    rows = pl.BlockSpec((step, width), lambda i: (i, 0))
    shapes = [array((padded, width), F32), array((padded, width), BF16), array((8, width), F32)]
    return call(
        body,
        shapes,
        grid=(padded // step,),
        in_specs=[
            rows
            if place is None
            else pl.BlockSpec((None, step, width), lambda i, place=place: (place, i, 0))
            for _, place in given
        ]
        + [pl.BlockSpec((1, width), lambda i: (0, 0))],
        out_specs=[rows] * (len(shapes) - 1) + [pl.BlockSpec((8, width), lambda i: (0, 0))],
        name="norm_back",
    )(*[item for item, _ in given], gain)


def mix(own_a, own_b, got_a, got_b, middle, bias):
    padded, width = middle.shape
    step = 256

    def body(a_ref, b_ref, ga_ref, gb_ref, middle_ref, bias_ref, out_ref, low_ref):
        total = a_ref[...] + b_ref[...] + ga_ref[...].astype(F32) + gb_ref[...].astype(F32)
        total = total + bias_ref[...] + middle_ref[...]
        out_ref[...] = total
        low_ref[...] = total.astype(BF16)

    rows = pl.BlockSpec((step, width), lambda i: (i, 0))
    plane = pl.BlockSpec((None, step, width), lambda i: (1, i, 0))
    return call(
        body,
        (array((padded, width), F32), array((padded, width), BF16)),
        grid=(padded // step,),
        in_specs=[rows, rows, plane, plane, rows, pl.BlockSpec((1, width), lambda i: (0, 0))],
        out_specs=(rows, rows),
        name="mix",
    )(own_a, own_b, got_a, got_b, middle, bias)


def attended_back(own, other, w_own, w_other, contexts, gots, plan, shards):
    padded, width = own.shape
    half = width // 2
    block = width // shards

    def body(*refs):
        own_ref, other_ref, wo_ref, wt_ref, ca, cb, ga, gb = refs[:8]
        context_ref, outs, blocks = refs[8], refs[9:-1], refs[-1]
        core = lax.axis_index("rep") % 2
        here = lax.axis_index("shard")
        mine = pl.ds(pl.multiple_of(core * half, half), half)
        theirs = pl.ds(pl.multiple_of((1 - core) * half, half), half)
        for place, ref in enumerate((own_ref, other_ref)):
            cols = slice(place * padded, (place + 1) * padded)
            result = product(wo_ref[mine, :], ref[:, mine], NT)
            result = result + product(wt_ref[mine, :], ref[:, theirs], NT)
            context_ref[:, cols] = result.astype(BF16)
        for heads, (pair, near, far) in enumerate(
            (
                ((ca, cb), slice(0, padded), slice(padded, 2 * padded)),
                ((ga, gb), slice(padded, 2 * padded), slice(0, padded)),
            )
        ):
            for place, ref in enumerate(pair):
                result = product(ref[:, near], own_ref[:, mine])
                result = result + product(ref[:, far], other_ref[:, mine])
                count = shards // 4
                at = (core if heads == 0 else 1 - core) * (shards // 2) + place * count
                blocks[pl.ds(at, count)] = result.astype(BF16).reshape(count, block, half)
        write_parts(outs, plan, blocks, here)

    shapes = [array((half, 2 * padded), BF16)] + part_shapes(plan, block, half)
    results = call(
        body,
        shapes,
        in_specs=[VMEM_SPEC] * 8,
        out_specs=[VMEM_SPEC] * len(shapes),
        scratch_shapes=[pltpu.VMEM((shards, block, half), BF16)],
        name="attended_back",
    )(own, other, w_own, w_other, *contexts, *gots)
    return results[0], results[1:]


def project_back(grads, w_qkv):
    part, rows = grads[0].shape
    count = len(grads)
    padded = rows // 2
    width, columns = w_qkv.shape

    def body(*refs):
        w_ref, own_ref, other_ref = refs[count:]

        def run(out_ref):
            stacked = jnp.concatenate([ref[...] for ref in refs[:count]], 0).T
            out_ref[...] = product(stacked, w_ref[...], NT).astype(out_ref.dtype)

        @pl.when(pl.program_id(0) == 0)
        def _():
            run(other_ref)

        @pl.when(pl.program_id(0) == 1)
        def _():
            run(own_ref)

    whole = pl.BlockSpec((padded, width), lambda i: (0, 0))
    return call(
        body,
        (array((padded, width), F32), array((padded, width), BF16)),
        grid=(2,),
        in_specs=[pl.BlockSpec((part, padded), lambda i: (0, 1 - i))] * count
        + [pl.BlockSpec((width, columns), lambda i: (0, 0))],
        out_specs=(whole, whole),
        name="project_back",
    )(*grads, w_qkv)


def project_grads(normed, groups, plans):
    rows, width = normed.shape
    half = sum(piece.shape[0] for piece in groups[0])
    shards = sum(len(p) for p in plans[0])
    block = width // shards
    given = [normed] + [piece for group in groups for piece in group]

    def body(*refs):
        normed_ref, outs, (turned, blocks) = refs[0], refs[len(given) : -2], refs[-2:]
        here = lax.axis_index("shard")
        turned[...] = normed_ref[...].T
        at, place_in = 0, 1
        for group, plan in zip(groups, plans):
            stacked = jnp.concatenate([ref[...] for ref in refs[place_in : place_in + len(group)]], 0)
            place_in += len(group)
            result = product(turned[...], stacked, NT)
            blocks[...] = result.astype(BF16).reshape(shards, block, half)
            write_parts(outs[at : at + len(plan)], plan, blocks, here)
            at += len(plan)

    shapes = []
    for plan in plans:
        shapes += part_shapes(plan, block, half)
    flat = call(
        body,
        shapes,
        in_specs=[VMEM_SPEC] * len(given),
        out_specs=[VMEM_SPEC] * len(shapes),
        scratch_shapes=[pltpu.VMEM((width, rows), BF16), pltpu.VMEM((shards, block, half), BF16)],
        name="project_grads",
    )(*given)
    parts, at = [], 0
    for plan in plans:
        parts.append(list(flat[at : at + len(plan)]))
        at += len(plan)
    return parts


def adam_values(master, moment_one, second, gradient, step_rate, decay_rate):
    momentum = BETA_ONE * moment_one.astype(F32) + (1.0 - BETA_ONE) * gradient
    variance = BETA_TWO * second + (1.0 - BETA_TWO) * gradient * gradient
    momentum_hat = momentum / (1.0 - BETA_ONE**STEP)
    variance_hat = variance / (1.0 - BETA_TWO**STEP)
    updated = master - step_rate * (
        momentum_hat / (jnp.sqrt(variance_hat) + ADAM_EPS) + decay_rate * master
    )
    return updated, updated.astype(BF16), momentum, variance


def adam_feed(own, other, up_state, down_state, shards):
    block, columns = up_state[0].shape
    down_rows, width = down_state[0].shape
    piece = columns // (4 * shards)
    step = 8
    tiles = block // step

    def gradients(refs, core):
        own_refs, other_refs = refs[:4], refs[4:8]
        first = core == 0
        lows = [jnp.where(first, a[0], b[0]) for a, b in zip(own_refs, other_refs)]
        highs = [jnp.where(first, b[0], a[0]) for a, b in zip(own_refs, other_refs)]
        return lows, highs

    def body(*refs):
        core = lax.axis_index("rep") % 2
        lows, highs = gradients(refs, core)
        ups = refs[8:11]
        downs = refs[11:14]
        up_outs, down_outs = refs[14:18], refs[18:22]
        sources = (lows[0], lows[2], highs[0], highs[2])
        gradient = jnp.concatenate(
            [
                source[:, at * piece : (at + 1) * piece]
                for at in range(shards)
                for source in sources
            ],
            1,
        )
        values = adam_values(*[ref[...] for ref in ups], gradient, RATES[2], DECAYS[2])
        for out, value in zip(up_outs, values):
            out[...] = value
        for place, gradient in enumerate((lows[1], lows[3], highs[1], highs[3])):
            values = adam_values(*[ref[place] for ref in downs], gradient, RATES[3], DECAYS[3])
            for out, value in zip(down_outs, values):
                out[place] = value

    grads = [pl.BlockSpec((1, step * 2, g.shape[2]), lambda i: (0, i, 0)) for g in own]
    up_spec = pl.BlockSpec((step * 2, columns), lambda i: (i, 0))
    down_spec = pl.BlockSpec((4, step * 2, width), lambda i: (0, i, 0))
    kinds = (F32, BF16, F32, F32)
    downs = [value.reshape(4, block, width) for value in down_state]
    results = call(
        body,
        [array((block, columns), kind) for kind in kinds]
        + [array((4, block, width), kind) for kind in kinds],
        grid=(-(-block // (step * 2)),),
        in_specs=grads * 2 + [up_spec] * 3 + [down_spec] * 3,
        out_specs=[up_spec] * 4 + [down_spec] * 4,
        name="adam_feed",
    )(*own, *other, *up_state, *downs)
    return tuple(results[:4]), tuple(value.reshape(down_rows, width) for value in results[4:])


def adam_update(master, moment_one, second, gradient, step_rate, decay_rate):
    momentum = BETA_ONE * moment_one.astype(F32) + (1.0 - BETA_ONE) * gradient
    variance = BETA_TWO * second + (1.0 - BETA_TWO) * gradient * gradient
    momentum_hat = momentum / (1.0 - BETA_ONE**STEP)
    variance_hat = variance / (1.0 - BETA_TWO**STEP)
    updated = master - step_rate * (
        momentum_hat / (jnp.sqrt(variance_hat) + ADAM_EPS) + decay_rate * master
    )
    return (updated, updated.astype(BF16), momentum, variance)


def by_core(core, own, other, axis):
    return jnp.where(
        core == 0, jnp.concatenate([own, other], axis), jnp.concatenate([other, own], axis)
    )


def local(
    frames,
    upstream,
    lengths,
    master_qkv,
    master_out,
    master_up,
    master_down,
    master_small,
    first_qkv,
    first_out,
    first_up,
    first_down,
    first_small,
    second_qkv,
    second_out,
    second_up,
    second_down,
    second_small,
):
    half_rows, width = frames.shape
    shards, here = lax.axis_size("shard"), lax.axis_index("shard")
    rep = lax.axis_index("rep")
    core = rep % 2
    padded = -(-half_rows // 256) * 256
    rows = 2 * padded
    half = width // 2
    heads = half // HEAD_DIM
    units = master_up.shape[1] // 2
    unit_block = units // shards
    block = width // shards
    quarter = units // 2
    orders = gather_orders(shards)
    count = len(orders["xyz"])
    cut = 2 * block // 5
    small_rows = 16 * block // 80
    small_size = master_small.shape[0]

    frames_moved, _ = swap_clips(frames, frames)
    low_qkv = lax.dynamic_slice_in_dim(master_qkv, core * half, half, 2).astype(BF16)
    low_out = lax.dynamic_slice_in_dim(master_out, core * half, half, 1).astype(BF16)
    low_small = jnp.pad(master_small.astype(BF16), (0, small_rows * half - small_size))
    first_wave = Doubling(
        [
            jnp.concatenate([low_qkv[0], low_out[:cut]], 0)[None],
            jnp.concatenate([low_qkv[1], low_out[cut : 2 * cut]], 0)[None],
            jnp.concatenate(
                [low_qkv[2], low_out[2 * cut :], low_small.reshape(small_rows, half)], 0
            )[None],
        ],
        [orders["xzy"], orders["yxz"], orders["zyx"]],
    )
    first_wave.start()

    low_up = lax.dynamic_index_in_dim(
        master_up.reshape(block, shards, 2, 2, unit_block // 2), core, 2, keepdims=False
    ).astype(BF16)
    low_down = lax.dynamic_slice_in_dim(master_down, core * unit_block, unit_block, 0).astype(BF16)
    low_ups = [low_up[:, :, index].reshape(block, quarter) for index in range(2)]
    wave = Doubling(
        [low_ups[0][None], low_down[None, :block], low_ups[1][None], low_down[None, block:]],
        [orders["zyx"], orders["xzy"], orders["xzy"], orders["yzx"]],
    )

    def own_half(values):
        return jnp.pad(values, ((0, padded - half_rows), (0, 0)))

    held = first_wave.finish()
    for step in range(1, count - 1):
        first_wave.start()
        if step == count - 2:
            wave.behind(*held)
            wave.start()
        held = first_wave.finish()
    frames_own = own_half(frames_moved(*held))
    first_wave.behind(frames_own)
    first_wave.start()
    upstream_moved, upstream_got = swap_clips(upstream, after(upstream, frames_own))
    wave.finish(*first_wave.got)
    wave_a, wave_b = wave.pair(0), wave.pair(2)
    for step in range(1, count - 3):
        wave_a.start()
        wave_a.finish()
        wave_b.start()
        wave_b.finish()
    wave_a.start()
    frames_other = across_cores(after(frames_own, *first_wave.got))
    w_qkv, w_out_own, small = place_first(first_wave.halves(), shards, block, half, cut, small_rows)
    w_out_own = w_out_own.reshape(width, half)
    held_a = wave_a.finish(w_qkv)
    wave_b.behind(*held_a)
    wave_a.start()
    wave_b.start()
    w_qkv = w_qkv.reshape(width, 3 * half)
    small = small.reshape(shards, -1)[:, :small_size].reshape(-1).astype(F32)

    pieces = [small[index * width : (index + 1) * width] for index in range(8)]
    gain_one, shift_one, bias_query, bias_value, bias_out, gain_two, shift_two, bias_down = [
        piece[None] for piece in pieces
    ]
    bias_up = lax.dynamic_index_in_dim(
        small[8 * width :].reshape(shards, 2, 2, unit_block // 2), core, 1, keepdims=False
    )
    bias_query = lax.dynamic_slice_in_dim(bias_query, core * half, half, 1)
    bias_value = lax.dynamic_slice_in_dim(bias_value, core * half, half, 1)
    bias_qkv = jnp.concatenate([bias_query, jnp.zeros_like(bias_query), bias_value], 1)

    rep_of_clip = 2 * (rep // 2) + here % 2
    clip = (rep_of_clip * shards + here) // 2
    length = lax.dynamic_index_in_dim(lengths, clip, 0, keepdims=False)
    steps = jnp.arange(padded, dtype=jnp.int32)
    positions = jnp.concatenate([core * half_rows + steps, (1 - core) * half_rows + steps])
    real = jnp.concatenate([steps, steps]) < half_rows
    fill = jnp.where(real & (positions < length), 0.0, NEG_FILL).astype(BF16)
    first_row = jnp.arange(MASK_ROWS)[:, None] == 0
    masks = jnp.concatenate(
        [
            jnp.where(first_row, fill[None, :], 0.0),
            jnp.broadcast_to(jnp.where(first_row, 1.0, 0.0), (MASK_ROWS, rows)),
        ],
        0,
    ).astype(BF16)

    normed_one, qkv = project(
        after(frames_own, *wave_a.held, *wave_b.held), frames_other, gain_one, shift_one, w_qkv, bias_qkv
    )
    held = wave_a.finish(qkv) + wave_b.finish(qkv)
    w_out_other = across_cores(after(w_out_own, *held))
    upstream_own = own_half(upstream_moved(qkv, *held))
    wave_a.behind(w_out_other, upstream_own)
    wave_b.behind(w_out_other, upstream_own)
    wave_a.start()
    wave_b.start()
    upstream_other = across_cores(upstream_own)
    qkv = qkv.reshape(3, heads, HEAD_DIM, rows)
    some = heads // 2
    context_a, lse_a = attend(after(qkv, *wave_a.held, *wave_b.held), masks, 0, some)
    context_b, lse_b = attend(after(qkv, context_a), masks, some, heads - some)
    flat_a = context_a.reshape(half // 2, rows)
    flat_b = context_b.reshape(half // 2, rows)
    wave_a.finish(context_b)
    upstream_other = after(upstream_other, context_b)
    held = wave_b.finish(context_b, upstream_other)
    wave_b.start()
    got_a = across_cores(after(flat_a, *wave_a.got, *held))
    got_b = across_cores(after(flat_b, *wave_a.got, *held))
    middle, normed_own = attended(
        (flat_a, flat_b), (got_a, got_b), w_out_own, w_out_other, frames_own, bias_out, gain_two, shift_two
    )
    normed_other = across_cores(normed_own)

    back = {name: order[::-1] for name, order in orders.items()}
    feed_names = (("zxy", "yxz"), ("zxy", "xyz"))
    groups = []

    def feed_half(index, weights, *behind):
        names = feed_names[index]
        sums, up_parts, down_parts = feed(
            after(normed_own, *behind),
            normed_other,
            upstream_own,
            upstream_other,
            weights,
            bias_up[:, index].reshape(1, quarter),
            [scatter_plan(back[name]) for name in names],
        )
        return sums, Halving([list(up_parts), list(down_parts)], [back[name] for name in names])

    (mixed_a, grad_a, send_a, sums_up_a), chunks_a = feed_half(0, wave_a.halves(), *held)
    wave_b.finish(grad_a)
    sent = chunks_a.step(*wave_b.got)
    send_a = after(send_a, *wave_b.got)
    got_sums_a = across_cores(send_a)
    (mixed_b, grad_b, send_b, sums_up_b), chunks_b = feed_half(1, wave_b.halves(), *sent, send_a)
    arrived = [after(got[0], grad_b) for got in chunks_a.got]
    chunks_a.got = [[got] for got in arrived]
    got_sums_a = after(got_sums_a, grad_b)
    got_sums_b = across_cores(after(send_b, got_sums_a, *arrived))
    grad_middle, grad_attended, sums_two = norm_back(
        (grad_a, grad_b, (got_sums_a, 0), (got_sums_b, 0)),
        middle,
        gain_two,
        upstream_own,
        True,
    )
    grad_attended_other = across_cores(grad_attended)
    sent = chunks_b.step(grad_attended_other)
    sent = sent + chunks_a.step(grad_attended_other)
    grad_context, out_parts = attended_back(
        after(grad_attended, *sent),
        grad_attended_other,
        w_out_own,
        w_out_other,
        (flat_a, flat_b),
        (got_a, got_b),
        scatter_plan(back["xyz"]),
        shards,
    )
    chunks_out = Halving([list(out_parts)], [back["xyz"]])
    grad_context = grad_context.reshape(heads, HEAD_DIM, rows)
    calls = 4
    each = heads // calls
    grads = []
    sent = []
    for index in range(calls):
        inside = index * each
        context, lse = (context_a, lse_a) if inside < some else (context_b, lse_b)
        grads.append(
            attend_back(
                after(qkv, *sent), masks, grad_context, context, lse, inside, inside % some, each
            )
        )
        done = grads[-1][0]
        if index == 0:
            mixed, mixed_low = mix(
                after(mixed_a, done), mixed_b, got_sums_a, got_sums_b, middle, bias_down
            )
            sent = [mixed_low] + chunks_out.step(mixed_low)
        elif index == 1:
            for _ in range(count - 4):
                chunks_a.step(done)
            sent = chunks_a.step(done)
            sent = sent + chunks_b.step(done) + chunks_out.step(done)
        elif index == 2:
            sent = chunks_a.step(done)
            sent = sent + chunks_b.step(done) + chunks_out.step(done)
            for _ in range(count - 4):
                sent = chunks_b.step() + chunks_out.step()
            mixed_low = after(mixed_low, *sent)
            sent = sent + [mixed_low]
            swapped_mixed, _ = swap_clips(mixed[:half_rows], mixed_low)
        else:
            own_a = chunks_a.result(done)
            sent = chunks_b.step(done) + own_a + chunks_out.step(done)
    flat = [[piece[which].reshape(each * HEAD_DIM, rows) for piece in grads] for which in range(3)]
    flat[0][0] = after(flat[0][0], *sent)
    partial_one, send_one = project_back([piece for group in flat for piece in group], w_qkv)
    mixed = swapped_mixed(partial_one)
    own_b = chunks_b.result(partial_one)
    (own_out,) = chunks_out.result(partial_one)
    got_one = across_cores(after(send_one, *own_b, own_out))
    early = [over_groups(value) for value in own_a + own_b + [own_out]]
    cut_rows = block // 2
    wide_out = jnp.concatenate([early[4][:, :cut_rows], early[4][:, cut_rows:]], 2)
    early_other = across_cores(jnp.concatenate(early[:4] + [wide_out], 1))
    grad_frames, early_send, sums_one = norm_back(
        (partial_one, got_one), frames_own, gain_one, grad_middle, False
    )
    swapped, swapped_got = swap_clips(grad_frames[:half_rows], early_send)
    def in_half(values):
        return lax.dynamic_update_slice_in_dim(jnp.zeros((width,), F32), values, core * half, 0)

    def head_sums(pieces_of):
        return in_half(jnp.concatenate([jnp.sum(piece.astype(F32), 1) for piece in pieces_of]))

    sums_up = jnp.stack([sums.reshape(shards, unit_block // 2) for sums in (sums_up_a, sums_up_b)], 1)
    sums_up_all = lax.dynamic_update_slice_in_dim(
        jnp.zeros((shards, 2, unit_block), F32), sums_up.reshape(shards, 1, unit_block), core, 1
    )
    grad_small = jnp.concatenate(
        [
            sums_one[0],
            sums_one[1],
            head_sums(flat[0]),
            head_sums(flat[2]),
            sums_two[2],
            sums_two[0],
            sums_two[1],
            sums_two[3],
            sums_up_all.reshape(-1),
        ]
    ).reshape(shards, small_size)
    small_sum = SmallSum(grad_small)
    small_sum.start()
    names = ("zxy", "xyz", "yzx")
    parts = project_grads(
        after(normed_one, early_send, small_sum.kept), flat, [scatter_plan(back[name]) for name in names]
    )
    early_other = after(early_other, parts[0][0])
    small_sum.finish(parts[0][0])
    splits = [early_other[:, i * block : (i + 1) * block] for i in range(4)]
    wide_out = early_other[:, 4 * block :]
    early_other = splits + [jnp.concatenate([wide_out[:, :, :half], wide_out[:, :, half:]], 1)]
    chunks_late = Halving(parts, [back[name] for name in names])
    sent = chunks_late.step(early_other[0], small_sum.held)
    small_sum.start()

    new_up, new_down = adam_feed(
        [after(early[0], *sent)] + early[1:4],
        early_other[:4],
        (master_up, first_up, second_up),
        (master_down, first_down, second_down),
        shards,
    )
    small_sum.finish(new_up[0])
    sent = chunks_late.step(new_up[0], small_sum.held, after(swapped_got, new_up[0]))
    small_sum.start()
    grad_frames = swapped(*sent)
    total_out = by_core(core, early[4][0], after(early_other[4], *sent)[0], 1)
    while len(chunks_late.got[0]) < count:
        sent = chunks_late.step(*([small_sum.finish()] if small_sum.mask >= 1 else []))
        if small_sum.mask >= 1:
            small_sum.start()
    if small_sum.held.shape[0] > 1:
        small_sum.finish()
    total_small = small_sum.result()
    late = over_groups(jnp.concatenate(chunks_late.result(), 0))
    late_other = across_cores(late)
    total_qkv = by_core(core, late, late_other, 2)

    new_qkv = adam_update(master_qkv, first_qkv, second_qkv, total_qkv, RATES[0], DECAYS[0])
    new_out = adam_update(master_out, first_out, second_out, total_out, RATES[1], DECAYS[1])
    new_small = adam_update(
        master_small, first_small, second_small, total_small, RATES[4], DECAYS[4]
    )
    return (mixed, grad_frames) + new_qkv + new_out + new_up + new_down + new_small


def solution(mesh):
    rows = P(("rep", "shard"), None)
    weights = (P(None, "shard", None), P("shard", None), P("shard", None), P("shard", None), P("shard"))
    outs = (rows, rows)
    for spec in weights:
        outs = outs + (spec,) * 4
    return jax.shard_map(
        local,
        mesh=mesh,
        in_specs=(rows, rows, P()) + weights * 3,
        out_specs=outs,
        check_vma=False,
    )
```

```python
import functools
import math

import jax
import jax.numpy as jnp
from jax import lax
from jax.experimental import pallas as pl
from jax.experimental.pallas import tpu as pltpu
from jax.sharding import PartitionSpec as P

HEAD_DIM = 80
STEP = 10

LN_EPS = 1e-05
NEG_FILL = -1e30
BETA_ONE = 0.5
BETA_TWO = 0.5
ADAM_EPS = 1e-08
RATES = (0.04, 0.5, 0.04, 0.02, 0.3)
DECAYS = (0.01, 0.01, 0.01, 0.01, 0.0)

F32 = jnp.float32
BF16 = jnp.bfloat16
MIB = 1024 * 1024
SCALING = HEAD_DIM**-0.5
SCORE_SCALE = SCALING * math.log2(math.e)
MASK_ROWS = 16
SMALL_COST = pl.CostEstimate(flops=0, bytes_accessed=MIB, transcendentals=0)
VMEM_SPEC = pl.BlockSpec(memory_space=pltpu.VMEM)
ANY_SPEC = pl.BlockSpec(memory_space=pl.ANY)
NN = (((1,), (0,)), ((), ()))
NT = (((1,), (1,)), ((), ()))


def product(left, right, dims=NN):
    return lax.dot_general(left, right, dims, preferred_element_type=F32)


def call(body, out_shape, limit=48, **options):
    return pl.pallas_call(
        body,
        out_shape=out_shape,
        compiler_params=pltpu.CompilerParams(vmem_limit_bytes=limit * MIB),
        cost_estimate=SMALL_COST,
        **options,
    )


def array(shape, dtype):
    return jax.ShapeDtypeStruct(tuple(shape), dtype)


def xor_pairs(count, mask):
    return [(source, source ^ mask) for source in range(count)]


def across_cores(value):
    return lax.ppermute(value, "rep", xor_pairs(lax.axis_size("rep"), 1))


def swap_pairs():
    reps, shards = lax.axis_size("rep"), lax.axis_size("shard")
    pairs = []
    for rep in range(reps):
        for shard in range(shards):
            if (rep % 2) != (shard % 2):
                pairs.append((rep * shards + shard, (rep ^ 1) * shards + (shard ^ 1)))
    return pairs


def swap_clips(own, sent):
    got = lax.ppermute(sent, ("rep", "shard"), swap_pairs())
    moved = (lax.axis_index("rep") % 2) != (lax.axis_index("shard") % 2)

    def finish(*behind):
        arrived = (after(got, *behind) if behind else got)[: own.shape[0]]
        return jnp.where(moved, arrived.astype(own.dtype), own)

    return finish, got


def after(value, *others):
    return lax.optimization_barrier((value,) + others)[0]


def flip(index, mask):
    out, bit = index, 1
    while bit <= mask:
        if mask & bit:
            out = out + bit * (1 - 2 * ((index // bit) % 2))
        bit *= 2
    return out


def gather_orders(shards):
    far = [1 << k for k in range(int(math.log2(shards)))][::-1]
    most = [b for b in far if b >= 8]
    axes = {"x": 1, "y": 2, "z": 4}
    names = ("xyz", "xzy", "yxz", "yzx", "zxy", "zyx")
    return {name: most + [axes[axis] for axis in name] for name in names}


def relative_places(order):
    places = [0]
    for mask in order:
        places = places + [mask ^ r for r in places]
    return places


class Doubling:
    def __init__(self, blocks, orders):
        self.held, self.orders, self.step, self.got = blocks, orders, 0, None

    def behind(self, *others):
        self.held = [after(held, *others) for held in self.held]

    def start(self):
        shards = lax.axis_size("shard")
        masks = [order[self.step] for order in self.orders]
        if self.step == 0:
            rows = [held.shape[1] for held in self.held]
            together = jnp.concatenate(self.held, 1)
            together = lax.ppermute(together, "shard", xor_pairs(shards, masks[0]))
            ends = [sum(rows[: i + 1]) for i in range(len(rows))]
            self.got = [together[:, end - row : end] for end, row in zip(ends, rows)]
        else:
            self.got = [
                lax.ppermute(held, "shard", xor_pairs(shards, mask))
                for held, mask in zip(self.held, masks)
            ]
        self.step += 1

    def finish(self, *behind):
        if behind:
            self.got = [after(got, *behind) for got in self.got]
        if self.step < len(self.orders[0]):
            self.held = [jnp.concatenate(pair, 0) for pair in zip(self.held, self.got)]
        return self.held

    def halves(self):
        return list(zip(self.held, self.got, self.orders))

    def pair(self, at):
        part = Doubling(self.held[at : at + 2], self.orders[at : at + 2])
        part.step = self.step
        return part


def scatter_plan(order):
    kept = [0]
    sent = []
    for mask in order[::-1]:
        sent.append([mask ^ r for r in kept])
        kept = kept + sent[-1]
    return sent[::-1] + [[0]]


class Halving:
    def __init__(self, chunks, orders):
        self.chunks, self.orders = chunks, orders
        self.got = [[] for _ in chunks]

    def step(self, *behind):
        index = len(self.got[0])
        shards = lax.axis_size("shard")
        sends = [chunk[index] for chunk in self.chunks]
        if behind:
            sends = [after(send, *behind) for send in sends]
        if index:
            sends = add_blocks(sends, self.got, 1, BF16)
        masks = [order[index] for order in self.orders]
        if index == len(self.orders[0]) - 1 and len(sends) > 1:
            rows = [send.shape[1] for send in sends]
            together = jnp.concatenate(sends, 1)
            together = lax.ppermute(together, "shard", xor_pairs(shards, masks[0]))
            ends = [sum(rows[: i + 1]) for i in range(len(rows))]
            arrived = [together[:, end - row : end] for end, row in zip(ends, rows)]
        else:
            arrived = [
                lax.ppermute(send, "shard", xor_pairs(shards, mask))
                for send, mask in zip(sends, masks)
            ]
        for got, new in zip(self.got, arrived):
            got.append(new)
        return sends

    def result(self, *behind):
        stays = [chunk[-1] for chunk in self.chunks]
        if behind:
            stays = [after(stay, *behind) for stay in stays]
        return add_blocks(stays, self.got, 0, F32)


def over_groups(value):
    reps = lax.axis_size("rep")
    mask = 2
    while mask < reps:
        value = value + lax.ppermute(value, "rep", xor_pairs(reps, mask))
        mask *= 2
    return value


class SmallSum:
    def __init__(self, vector):
        self.held, self.mask = vector, vector.shape[0] // 2
        self.kept = self.got = None

    def start(self):
        shards, here = lax.axis_size("shard"), lax.axis_index("shard")
        upper = (here // self.mask) % 2 == 1
        low, high = self.held[: self.mask], self.held[self.mask :]
        self.kept = jnp.where(upper, high, low)
        self.got = lax.ppermute(
            jnp.where(upper, low, high), "shard", xor_pairs(shards, self.mask)
        )
        self.mask //= 2

    def finish(self, *behind):
        self.held = self.kept + (after(self.got, *behind) if behind else self.got)
        return self.held

    def result(self):
        while self.mask >= 1:
            self.start()
            self.finish()
        reps = lax.axis_size("rep")
        held, mask = self.held[0], 1
        while mask < reps:
            held = held + lax.ppermute(held, "rep", xor_pairs(reps, mask))
            mask *= 2
        return held


def row_slice(start, size):
    return pl.ds(pl.multiple_of(start, 8), size)


def place_first(halves, shards, block, half, cut, small_rows):
    rest = block - 2 * cut

    def body(*refs):
        ins, (qkv, out, small) = refs[:6], refs[6:]
        here = lax.axis_index("shard")
        for index, (low, _, order) in enumerate(halves):
            for place, rel in enumerate(relative_places(order)):
                ref = ins[2 * index + place // low.shape[0]].at[place % low.shape[0]]
                at = flip(here, rel)
                qkv[at, :, index * half : (index + 1) * half] = ref[:block, :]
                if index < 2:
                    out[at, index * cut : (index + 1) * cut, :] = ref[block : block + cut, :]
                else:
                    out[at, 2 * cut :, :] = ref[block : block + rest, :]
                    small[at] = ref[block + rest :, :]

    shapes = (
        array((shards, block, 3 * half), BF16),
        array((shards, block, half), BF16),
        array((shards, small_rows, half), BF16),
    )
    return call(
        body, shapes, in_specs=[VMEM_SPEC] * 6, out_specs=[VMEM_SPEC] * 3, name="place_first"
    )(*[part for low, got, _ in halves for part in (low, got)])


def write_parts(outs, plan, source, here):
    for out, part in zip(outs, plan):
        for place, rel in enumerate(part):
            out[place] = source[flip(here, rel)]


def add_blocks(firsts, others, place, dtype):
    inputs, specs = [], []
    for first, rest in zip(firsts, others):
        inputs.append(first)
        specs.append(pl.BlockSpec(first.shape, lambda i: (0, 0, 0)))
        for other in rest:
            inputs.append(other)
            specs.append(pl.BlockSpec(first.shape, lambda i, at=place: (at, 0, 0)))

    def body(*refs):
        at = 0
        for index, rest in enumerate(others):
            total = refs[at][...].astype(F32)
            for ref in refs[at + 1 : at + 1 + len(rest)]:
                total = total + ref[...].astype(F32)
            refs[len(inputs) + index][...] = total.astype(dtype)
            at += 1 + len(rest)

    return list(call(
        body,
        [array(first.shape, dtype) for first in firsts],
        grid=(1,),
        in_specs=specs,
        out_specs=[pl.BlockSpec(first.shape, lambda i: (0, 0, 0)) for first in firsts],
        name="add_blocks",
    )(*inputs))


def part_shapes(plan, rows, width):
    return [array((len(part), rows, width), BF16) for part in plan]


def norm_rows(values):
    center = values - jnp.mean(values, -1, keepdims=True)
    spread = jnp.mean(center * center, -1, keepdims=True)
    inverse = lax.rsqrt(spread + LN_EPS)
    return center * inverse, inverse


def project(own, other, gain, shift, w_qkv, bias):
    padded, width = own.shape
    columns = w_qkv.shape[1]
    third = columns // 3
    step = padded // 2

    def body(own_ref, other_ref, gain_ref, shift_ref, w_ref, bias_ref, normed_ref, out_ref):
        index = pl.program_id(0)
        values = jnp.where(index < 2, own_ref[...], other_ref[...]).astype(F32)
        unit, _ = norm_rows(values)
        normed = (unit * gain_ref[...] + shift_ref[...]).astype(BF16)
        normed_ref[...] = normed
        for part in range(3):
            cols = slice(part * third, (part + 1) * third)
            result = product(normed, w_ref[:, cols]) + bias_ref[:, cols]
            out_ref[cols, :] = result.astype(BF16).T

    line = pl.BlockSpec((1, width), lambda i: (0, 0))
    return call(
        body,
        (array((2 * padded, width), BF16), array((columns, 2 * padded), BF16)),
        grid=(4,),
        in_specs=[
            pl.BlockSpec((step, width), lambda i: (jnp.minimum(i, 1), 0)),
            pl.BlockSpec((step, width), lambda i: (jnp.maximum(i - 2, 0), 0)),
            line,
            line,
            pl.BlockSpec((width, columns), lambda i: (0, 0)),
            pl.BlockSpec((1, columns), lambda i: (0, 0)),
        ],
        out_specs=(
            pl.BlockSpec((step, width), lambda i: (i, 0)),
            pl.BlockSpec((columns, step), lambda i: (0, i)),
        ),
        name="project",
    )(own, other, gain, shift, w_qkv, bias)


def attend_kernel(mask_ref, q_ref, k_ref, v_ref, out_ref, lse_ref, kt, qt, *, step):
    dim, keys = k_ref.shape
    kt[...] = jnp.zeros_like(kt)
    kt[:dim, :] = k_ref[...]
    kt[dim : dim + MASK_ROWS, :] = mask_ref[:MASK_ROWS, :]
    k_rows = kt[...].T
    qt[...] = jnp.zeros_like(qt)
    qt[:dim, :] = q_ref[...]
    qt[dim : dim + MASK_ROWS, :] = mask_ref[MASK_ROWS:, :]
    for start in range(0, keys, step):
        cols = slice(start, start + step)
        scores = jnp.dot(k_rows, qt[:, cols], preferred_element_type=F32)
        top = jnp.max(scores, 0, keepdims=True) * SCORE_SCALE
        powers = jnp.exp2(scores * SCORE_SCALE - top)
        total = jnp.sum(powers, 0, keepdims=True)
        context = jnp.dot(v_ref[...], powers.astype(BF16), preferred_element_type=F32)
        out_ref[:, cols] = (context / total).astype(BF16)
        lse_ref[:, cols] = top + jnp.log2(total)


def attend(qkv, masks, first, heads):
    _, _, dim, rows = qkv.shape
    step = 512

    def head_block(which):
        return pl.BlockSpec((None, None, dim, rows), lambda h: (which, first + h, 0, 0))

    return pl.pallas_call(
        functools.partial(attend_kernel, step=step),
        grid=(heads,),
        out_shape=(
            jax.ShapeDtypeStruct((heads, dim, rows), BF16),
            jax.ShapeDtypeStruct((heads, 1, rows), F32),
        ),
        in_specs=[
            pl.BlockSpec(masks.shape, lambda h: (0, 0)),
            head_block(0),
            head_block(1),
            head_block(2),
        ],
        out_specs=(
            pl.BlockSpec((None, dim, rows), lambda h: (h, 0, 0)),
            pl.BlockSpec((None, 1, rows), lambda h: (h, 0, 0)),
        ),
        scratch_shapes=[pltpu.VMEM((128, rows), BF16), pltpu.VMEM((128, rows), BF16)],
        compiler_params=pltpu.CompilerParams(vmem_limit_bytes=48 * MIB),
        cost_estimate=SMALL_COST,
        name="attend",
    )(masks, qkv, qkv, qkv)


def attend_back_kernel(
    mask_ref, q_ref, k_ref, v_ref, g_ref, ctx_ref, lse_ref, gq_ref, gk_ref, gv_ref, kt, qt, pad, acc_k, acc_v, *, step
):
    dim, keys = k_ref.shape
    kt[...] = jnp.zeros_like(kt)
    kt[:dim, :] = k_ref[...]
    kt[dim : dim + MASK_ROWS, :] = mask_ref[:MASK_ROWS, :]
    k_rows = kt[...].T
    pad[...] = jnp.zeros_like(pad)
    pad[:dim, :] = v_ref[...]
    v_rows = pad[...].T
    qt[...] = jnp.zeros_like(qt)
    qt[:dim, :] = q_ref[...]
    qt[dim : dim + MASK_ROWS, :] = mask_ref[MASK_ROWS:, :]
    q_rows = qt[...].T
    pad[:dim, :] = g_ref[...]
    g_rows = pad[...].T
    inner = jnp.sum(g_ref[...].astype(F32) * ctx_ref[...].astype(F32), 0, keepdims=True)
    for start in range(0, keys, step):
        cols = slice(start, start + step)
        scores = jnp.dot(k_rows, qt[:, cols], preferred_element_type=F32)
        probs = jnp.exp2(scores * SCORE_SCALE - lse_ref[:, cols])
        grad_probs = jnp.dot(v_rows, pad[:, cols], preferred_element_type=F32)
        grad_scores = (probs * (grad_probs - inner[:, cols])).astype(BF16)
        part_v = jnp.dot(probs.astype(BF16), g_rows[cols, :], preferred_element_type=F32)
        part_k = jnp.dot(grad_scores, q_rows[cols, :], preferred_element_type=F32)
        if start == 0:
            acc_v[...] = part_v
            acc_k[...] = part_k
        else:
            acc_v[...] += part_v
            acc_k[...] += part_k
        grad_query = jnp.dot(k_ref[...], grad_scores, preferred_element_type=F32)
        gq_ref[:, cols] = (grad_query * SCALING).astype(BF16)
    gv_ref[...] = acc_v[...].T[:dim, :].astype(BF16)
    gk_ref[...] = (acc_k[...].T[:dim, :] * SCALING).astype(BF16)


def attend_back(qkv, masks, grad_context, context, lse, first, inside, heads):
    _, dim, rows = context.shape
    step = 512

    def head_block(which):
        return pl.BlockSpec((None, None, dim, rows), lambda h: (which, first + h, 0, 0))

    plain = pl.BlockSpec((None, dim, rows), lambda h: (h, 0, 0))
    return pl.pallas_call(
        functools.partial(attend_back_kernel, step=step),
        grid=(heads,),
        out_shape=[jax.ShapeDtypeStruct((heads, dim, rows), BF16)] * 3,
        in_specs=[
            pl.BlockSpec(masks.shape, lambda h: (0, 0)),
            head_block(0),
            head_block(1),
            head_block(2),
            pl.BlockSpec((None, dim, rows), lambda h: (first + h, 0, 0)),
            pl.BlockSpec((None, dim, rows), lambda h: (inside + h, 0, 0)),
            pl.BlockSpec((None, 1, rows), lambda h: (inside + h, 0, 0)),
        ],
        out_specs=[plain] * 3,
        scratch_shapes=[pltpu.VMEM((128, rows), BF16)] * 3 + [pltpu.VMEM((rows, 128), F32)] * 2,
        compiler_params=pltpu.CompilerParams(vmem_limit_bytes=48 * MIB),
        cost_estimate=SMALL_COST,
        name="attend_back",
    )(masks, qkv, qkv, qkv, grad_context, context, lse)


def attended(contexts, gots, w_own, w_other, frames, bias, gain, shift):
    padded, width = frames.shape
    half = width // 2
    step = 256
    tiles = padded // step

    def body(ca, cb, ga, gb, wo_ref, wt_ref, frames_ref, bias_ref, gain_ref, shift_ref, middle_ref, normed_ref):
        first = lax.axis_index("rep") % 2 == 0
        own = jnp.concatenate([ca[...], cb[...]], 0)
        got = jnp.concatenate([ga[...], gb[...]], 0)
        low = jnp.where(first, own, got).T
        high = jnp.where(first, got, own).T
        by_own = product(low, wo_ref[:half, :]) + product(high, wo_ref[half:, :])
        by_other = product(low, wt_ref[:half, :]) + product(high, wt_ref[half:, :])
        result = jnp.concatenate(
            [jnp.where(first, by_own, by_other), jnp.where(first, by_other, by_own)], 1
        )
        middle = result + frames_ref[...].astype(F32) + bias_ref[...]
        middle_ref[...] = middle
        unit, _ = norm_rows(middle)
        normed_ref[...] = (unit * gain_ref[...] + shift_ref[...]).astype(BF16)

    part = half // 2
    line = pl.BlockSpec((1, width), lambda i: (0, 0))
    here = pl.BlockSpec((part, step), lambda i: (0, i))
    there = pl.BlockSpec((part, step), lambda i: (0, i + tiles))
    matrix = pl.BlockSpec((width, half), lambda i: (0, 0))
    rows = pl.BlockSpec((step, width), lambda i: (i, 0))
    return call(
        body,
        (array((padded, width), F32), array((padded, width), BF16)),
        grid=(tiles,),
        in_specs=[here, here, there, there, matrix, matrix, rows, line, line, line],
        out_specs=(rows, rows),
        name="attended",
    )(*contexts, *gots, w_own, w_other, frames, bias, gain, shift)


def feed(own, other, up_own, up_other, weights, bias, plans):
    padded, width = own.shape
    stacks_given = [part for halves in weights for part in halves[:2]] if isinstance(weights, list) else [weights]
    count_in = len(stacks_given)
    block, units = stacks_given[0].shape[-2:]
    shards = width // block
    tile = 256
    tiles = units // tile
    up_plan, down_plan = plans

    def body(*refs):
        x_refs, u_refs = refs[0:2], refs[2:4]
        stacks, refs = refs[4 : 4 + count_in], refs[4 + count_in :]
        bias_ref, mixed_own, grad_own, send, sums_ref = refs[:5]
        up_outs = refs[5 : 5 + len(up_plan)]
        down_outs = refs[5 + len(up_plan) : 5 + len(up_plan) + len(down_plan)]
        w_up, w_down, hidden_t, x_t, grad_pre, hidden, blocks, sems = refs[5 + len(up_plan) + len(down_plan) :]
        index = pl.program_id(0)
        here = lax.axis_index("shard")

        def rows_step(which):
            x_ref, u_ref = x_refs[which], u_refs[which]
            cols = slice(which * padded, (which + 1) * padded)
            wu, wd = w_up[...].reshape(width, units), w_down[...].reshape(units, width)

            def products(t):
                part = slice(t * tile, (t + 1) * tile)
                return product(x_ref[...], wu[:, part]), product(u_ref[...], wd[part, :], NT)

            ahead = products(0)
            for t in range(tiles):
                part = slice(t * tile, (t + 1) * tile)
                pre, grad_hidden = ahead
                if t + 1 < tiles:
                    ahead = products(t + 1)
                pre = pre + bias_ref[:, part]
                phi = 0.5 + 0.5 * lax.erf(pre * (0.5**0.5))
                hid = (pre * phi).astype(BF16)
                hidden[:, part] = hid
                hidden_t[part, cols] = hid.T
                density = jnp.exp(pre * pre * -0.5) * (1.0 / math.sqrt(2.0 * math.pi))
                grad = (grad_hidden * (phi + pre * density)).astype(BF16)
                grad_pre[cols, part] = grad
                total = jnp.sum(grad.astype(F32), 0, keepdims=True)
                if which == 1:
                    sums_ref[:, part] = total
                else:
                    sums_ref[:, part] += total
            mixed_ref, grad_ref = ((mixed_own, grad_own), (send.at[1], send.at[0]))[which]
            for t in range(width // tile):
                part = slice(t * tile, (t + 1) * tile)
                mixed_ref[:, part] = product(hidden[...], wd[:, part]).astype(mixed_ref.dtype)
                grad_ref[:, part] = product(grad_pre[cols, :], wu[part, :], NT).astype(grad_ref.dtype)

        @pl.when(index == 0)
        def _():
            copies = []

            def copy_in(source, matrix, at):
                copies.append(pltpu.make_async_copy(source, matrix.at[at], sems.at[len(copies)]))
                copies[-1].start()

            for which, matrix in enumerate((w_up, w_down)):
                if count_in == 1:
                    for at in range(shards):
                        copy_in(stacks[0].at[at, which], matrix, at)
                else:
                    for place, rel in enumerate(relative_places(weights[which][2])):
                        stack = stacks[2 * which + place // (shards // 2)]
                        copy_in(stack.at[place % (shards // 2)], matrix, flip(here, rel))
            for which in range(2):
                x_t[:, which * padded : (which + 1) * padded] = x_refs[which][...].T
            for copy in copies:
                copy.wait()
            rows_step(1)

        @pl.when(index == 1)
        def _():
            rows_step(0)

        @pl.when(index >= 2)
        def _():
            part = pl.ds(pl.multiple_of((index - 2) * tile, tile), tile)
            down = product(hidden_t[:, :padded], u_refs[0][:, part]) + product(
                hidden_t[:, padded:], u_refs[1][:, part]
            )
            blocks[...] = down.astype(BF16).reshape(shards, block, tile)
            write_parts(down_outs, down_plan, blocks, here)
            up = product(x_t[...], grad_pre[:, part])
            blocks[...] = up.astype(BF16).reshape(shards, block, tile)
            write_parts(up_outs, up_plan, blocks, here)

    once = pl.Buffered(1)
    whole = pl.BlockSpec((padded, width), lambda i: (0, 0), pipeline_mode=once)
    line = pl.BlockSpec((1, units), lambda i: (0, 0))
    shapes = [
        array((padded, width), F32),
        array((padded, width), F32),
        array((2, padded, width), BF16),
        array((1, units), F32),
    ]
    specs = [
        whole,
        whole,
        pl.BlockSpec((2, padded, width), lambda i: (0, 0, 0), pipeline_mode=once),
        line,
    ]
    for plan, size in ((up_plan, units), (down_plan, width)):
        shapes += part_shapes(plan, block, size)
        specs += [
            pl.BlockSpec((len(part), block, tile), lambda i: (0, 0, jnp.maximum(i - 2, 0)))
            for part in plan
        ]
    results = call(
        body,
        shapes,
        limit=60,
        grid=(2 + tiles,),
        in_specs=[whole] * 4 + [ANY_SPEC] * count_in + [line],
        out_specs=specs,
        scratch_shapes=[
            pltpu.VMEM((shards, block, units), BF16),
            pltpu.VMEM((shards, block, width), BF16),
            pltpu.VMEM((units, 2 * padded), BF16),
            pltpu.VMEM((width, 2 * padded), BF16),
            pltpu.VMEM((2 * padded, units), BF16),
            pltpu.VMEM((padded, units), BF16),
            pltpu.VMEM((shards, block, tile), BF16),
            pltpu.SemaphoreType.DMA((2 * shards,)),
        ],
        name="feed",
    )(own, other, up_own, up_other, *stacks_given, bias)
    count = 4 + len(up_plan)
    return results[:4], results[4:count], results[count:]


def norm_back(sums, values, gain, base, more_sums):
    given = [item if isinstance(item, tuple) else (item, None) for item in (*sums, values, base)]
    padded, width = given[0][0].shape[-2:]
    step = 256

    def body(*refs):
        parts = refs[: len(sums)]
        values_ref, base_ref, gain_ref = refs[len(parts) : len(parts) + 3]
        outs = refs[len(parts) + 3 :]
        sums_ref = outs[-1]
        grads = parts[0][...].astype(F32)
        for ref in parts[1:]:
            grads = grads + ref[...].astype(F32)
        unit, inverse = norm_rows(values_ref[...].astype(F32))
        scaled = grads * gain_ref[...]
        inner = (
            scaled
            - jnp.mean(scaled, -1, keepdims=True)
            - unit * jnp.mean(scaled * unit, -1, keepdims=True)
        )
        result = base_ref[...].astype(F32) + inverse * inner
        outs[0][...] = result
        low = result.astype(BF16)
        outs[1][...] = low
        lines = [jnp.sum(grads * unit, 0, keepdims=True), jnp.sum(grads, 0, keepdims=True)]
        if more_sums:
            lines.append(jnp.sum(low.astype(F32), 0, keepdims=True))
            lines.append(jnp.sum(base_ref[...].astype(F32), 0, keepdims=True))

        @pl.when(pl.program_id(0) == 0)
        def _():
            sums_ref[...] = jnp.zeros_like(sums_ref)

        for place, line in enumerate(lines):
            sums_ref[place : place + 1, :] += line

    rows = pl.BlockSpec((step, width), lambda i: (i, 0))
    shapes = [array((padded, width), F32), array((padded, width), BF16), array((8, width), F32)]
    return call(
        body,
        shapes,
        grid=(padded // step,),
        in_specs=[
            rows
            if place is None
            else pl.BlockSpec((None, step, width), lambda i, place=place: (place, i, 0))
            for _, place in given
        ]
        + [pl.BlockSpec((1, width), lambda i: (0, 0))],
        out_specs=[rows] * (len(shapes) - 1) + [pl.BlockSpec((8, width), lambda i: (0, 0))],
        name="norm_back",
    )(*[item for item, _ in given], gain)


def mix(own_a, own_b, got_a, got_b, middle, bias):
    padded, width = middle.shape
    step = 256

    def body(a_ref, b_ref, ga_ref, gb_ref, middle_ref, bias_ref, out_ref, low_ref):
        total = a_ref[...] + b_ref[...] + ga_ref[...].astype(F32) + gb_ref[...].astype(F32)
        total = total + bias_ref[...] + middle_ref[...]
        out_ref[...] = total
        low_ref[...] = total.astype(BF16)

    rows = pl.BlockSpec((step, width), lambda i: (i, 0))
    plane = pl.BlockSpec((None, step, width), lambda i: (1, i, 0))
    return call(
        body,
        (array((padded, width), F32), array((padded, width), BF16)),
        grid=(padded // step,),
        in_specs=[rows, rows, plane, plane, rows, pl.BlockSpec((1, width), lambda i: (0, 0))],
        out_specs=(rows, rows),
        name="mix",
    )(own_a, own_b, got_a, got_b, middle, bias)


def attended_back(own, other, w_own, w_other, contexts, gots, plan, shards):
    padded, width = own.shape
    half = width // 2
    block = width // shards

    def body(*refs):
        own_ref, other_ref, wo_ref, wt_ref, ca, cb, ga, gb = refs[:8]
        context_ref, outs, blocks = refs[8], refs[9:-1], refs[-1]
        core = lax.axis_index("rep") % 2
        here = lax.axis_index("shard")
        mine = pl.ds(pl.multiple_of(core * half, half), half)
        theirs = pl.ds(pl.multiple_of((1 - core) * half, half), half)
        for place, ref in enumerate((own_ref, other_ref)):
            cols = slice(place * padded, (place + 1) * padded)
            result = product(wo_ref[mine, :], ref[:, mine], NT)
            result = result + product(wt_ref[mine, :], ref[:, theirs], NT)
            context_ref[:, cols] = result.astype(BF16)
        for heads, (pair, near, far) in enumerate(
            (
                ((ca, cb), slice(0, padded), slice(padded, 2 * padded)),
                ((ga, gb), slice(padded, 2 * padded), slice(0, padded)),
            )
        ):
            for place, ref in enumerate(pair):
                result = product(ref[:, near], own_ref[:, mine])
                result = result + product(ref[:, far], other_ref[:, mine])
                count = shards // 4
                at = (core if heads == 0 else 1 - core) * (shards // 2) + place * count
                blocks[pl.ds(at, count)] = result.astype(BF16).reshape(count, block, half)
        write_parts(outs, plan, blocks, here)

    shapes = [array((half, 2 * padded), BF16)] + part_shapes(plan, block, half)
    results = call(
        body,
        shapes,
        in_specs=[VMEM_SPEC] * 8,
        out_specs=[VMEM_SPEC] * len(shapes),
        scratch_shapes=[pltpu.VMEM((shards, block, half), BF16)],
        name="attended_back",
    )(own, other, w_own, w_other, *contexts, *gots)
    return results[0], results[1:]


def project_back(grads, w_qkv):
    part, rows = grads[0].shape
    count = len(grads)
    padded = rows // 2
    width, columns = w_qkv.shape

    def body(*refs):
        w_ref, own_ref, other_ref = refs[count:]

        def run(out_ref):
            stacked = jnp.concatenate([ref[...] for ref in refs[:count]], 0).T
            out_ref[...] = product(stacked, w_ref[...], NT).astype(out_ref.dtype)

        @pl.when(pl.program_id(0) == 0)
        def _():
            run(other_ref)

        @pl.when(pl.program_id(0) == 1)
        def _():
            run(own_ref)

    whole = pl.BlockSpec((padded, width), lambda i: (0, 0))
    return call(
        body,
        (array((padded, width), F32), array((padded, width), BF16)),
        grid=(2,),
        in_specs=[pl.BlockSpec((part, padded), lambda i: (0, 1 - i))] * count
        + [pl.BlockSpec((width, columns), lambda i: (0, 0))],
        out_specs=(whole, whole),
        name="project_back",
    )(*grads, w_qkv)


def project_grads(normed, groups, plans):
    rows, width = normed.shape
    half = sum(piece.shape[0] for piece in groups[0])
    shards = sum(len(p) for p in plans[0])
    block = width // shards
    given = [normed] + [piece for group in groups for piece in group]

    def body(*refs):
        normed_ref, outs, (turned, blocks) = refs[0], refs[len(given) : -2], refs[-2:]
        here = lax.axis_index("shard")
        turned[...] = normed_ref[...].T
        at, place_in = 0, 1
        for group, plan in zip(groups, plans):
            stacked = jnp.concatenate([ref[...] for ref in refs[place_in : place_in + len(group)]], 0)
            place_in += len(group)
            result = product(turned[...], stacked, NT)
            blocks[...] = result.astype(BF16).reshape(shards, block, half)
            write_parts(outs[at : at + len(plan)], plan, blocks, here)
            at += len(plan)

    shapes = []
    for plan in plans:
        shapes += part_shapes(plan, block, half)
    flat = call(
        body,
        shapes,
        in_specs=[VMEM_SPEC] * len(given),
        out_specs=[VMEM_SPEC] * len(shapes),
        scratch_shapes=[pltpu.VMEM((width, rows), BF16), pltpu.VMEM((shards, block, half), BF16)],
        name="project_grads",
    )(*given)
    parts, at = [], 0
    for plan in plans:
        parts.append(list(flat[at : at + len(plan)]))
        at += len(plan)
    return parts


def adam_values(master, moment_one, second, gradient, step_rate, decay_rate):
    momentum = BETA_ONE * moment_one.astype(F32) + (1.0 - BETA_ONE) * gradient
    variance = BETA_TWO * second + (1.0 - BETA_TWO) * gradient * gradient
    momentum_hat = momentum / (1.0 - BETA_ONE**STEP)
    variance_hat = variance / (1.0 - BETA_TWO**STEP)
    updated = master - step_rate * (
        momentum_hat / (jnp.sqrt(variance_hat) + ADAM_EPS) + decay_rate * master
    )
    return updated, updated.astype(BF16), momentum, variance


def adam_feed(own, other, up_state, down_state, shards):
    block, columns = up_state[0].shape
    down_rows, width = down_state[0].shape
    piece = columns // (4 * shards)
    step = 8
    tiles = block // step

    def gradients(refs, core):
        own_refs, other_refs = refs[:4], refs[4:8]
        first = core == 0
        lows = [jnp.where(first, a[0], b[0]) for a, b in zip(own_refs, other_refs)]
        highs = [jnp.where(first, b[0], a[0]) for a, b in zip(own_refs, other_refs)]
        return lows, highs

    def body(*refs):
        core = lax.axis_index("rep") % 2
        lows, highs = gradients(refs, core)
        ups = refs[8:11]
        downs = refs[11:14]
        up_outs, down_outs = refs[14:18], refs[18:22]
        sources = (lows[0], lows[2], highs[0], highs[2])
        gradient = jnp.concatenate(
            [
                source[:, at * piece : (at + 1) * piece]
                for at in range(shards)
                for source in sources
            ],
            1,
        )
        values = adam_values(*[ref[...] for ref in ups], gradient, RATES[2], DECAYS[2])
        for out, value in zip(up_outs, values):
            out[...] = value
        for place, gradient in enumerate((lows[1], lows[3], highs[1], highs[3])):
            values = adam_values(*[ref[place] for ref in downs], gradient, RATES[3], DECAYS[3])
            for out, value in zip(down_outs, values):
                out[place] = value

    grads = [pl.BlockSpec((1, step * 2, g.shape[2]), lambda i: (0, i, 0)) for g in own]
    up_spec = pl.BlockSpec((step * 2, columns), lambda i: (i, 0))
    down_spec = pl.BlockSpec((4, step * 2, width), lambda i: (0, i, 0))
    kinds = (F32, BF16, F32, F32)
    downs = [value.reshape(4, block, width) for value in down_state]
    results = call(
        body,
        [array((block, columns), kind) for kind in kinds]
        + [array((4, block, width), kind) for kind in kinds],
        grid=(-(-block // (step * 2)),),
        in_specs=grads * 2 + [up_spec] * 3 + [down_spec] * 3,
        out_specs=[up_spec] * 4 + [down_spec] * 4,
        name="adam_feed",
    )(*own, *other, *up_state, *downs)
    return tuple(results[:4]), tuple(value.reshape(down_rows, width) for value in results[4:])


def adam_update(master, moment_one, second, gradient, step_rate, decay_rate):
    momentum = BETA_ONE * moment_one.astype(F32) + (1.0 - BETA_ONE) * gradient
    variance = BETA_TWO * second + (1.0 - BETA_TWO) * gradient * gradient
    momentum_hat = momentum / (1.0 - BETA_ONE**STEP)
    variance_hat = variance / (1.0 - BETA_TWO**STEP)
    updated = master - step_rate * (
        momentum_hat / (jnp.sqrt(variance_hat) + ADAM_EPS) + decay_rate * master
    )
    return (updated, updated.astype(BF16), momentum, variance)


def by_core(core, own, other, axis):
    return jnp.where(
        core == 0, jnp.concatenate([own, other], axis), jnp.concatenate([other, own], axis)
    )


def local(
    frames,
    upstream,
    lengths,
    master_qkv,
    master_out,
    master_up,
    master_down,
    master_small,
    first_qkv,
    first_out,
    first_up,
    first_down,
    first_small,
    second_qkv,
    second_out,
    second_up,
    second_down,
    second_small,
):
    half_rows, width = frames.shape
    shards, here = lax.axis_size("shard"), lax.axis_index("shard")
    rep = lax.axis_index("rep")
    core = rep % 2
    padded = -(-half_rows // 256) * 256
    rows = 2 * padded
    half = width // 2
    heads = half // HEAD_DIM
    units = master_up.shape[1] // 2
    unit_block = units // shards
    block = width // shards
    quarter = units // 2
    orders = gather_orders(shards)
    count = len(orders["xyz"])
    cut = 2 * block // 5
    small_rows = 16 * block // 80
    small_size = master_small.shape[0]

    frames_moved, _ = swap_clips(frames, frames)
    low_qkv = lax.dynamic_slice_in_dim(master_qkv, core * half, half, 2).astype(BF16)
    low_out = lax.dynamic_slice_in_dim(master_out, core * half, half, 1).astype(BF16)
    low_small = jnp.pad(master_small.astype(BF16), (0, small_rows * half - small_size))
    first_wave = Doubling(
        [
            jnp.concatenate([low_qkv[0], low_out[:cut]], 0)[None],
            jnp.concatenate([low_qkv[1], low_out[cut : 2 * cut]], 0)[None],
            jnp.concatenate(
                [low_qkv[2], low_out[2 * cut :], low_small.reshape(small_rows, half)], 0
            )[None],
        ],
        [orders["xzy"], orders["yxz"], orders["zyx"]],
    )
    first_wave.start()

    low_up = lax.dynamic_index_in_dim(
        master_up.reshape(block, shards, 2, 2, unit_block // 2), core, 2, keepdims=False
    ).astype(BF16)
    low_down = lax.dynamic_slice_in_dim(master_down, core * unit_block, unit_block, 0).astype(BF16)
    low_ups = [low_up[:, :, index].reshape(block, quarter) for index in range(2)]
    wave = Doubling(
        [low_ups[0][None], low_down[None, :block], low_ups[1][None], low_down[None, block:]],
        [orders["zyx"], orders["xzy"], orders["xzy"], orders["yzx"]],
    )

    def own_half(values):
        return jnp.pad(values, ((0, padded - half_rows), (0, 0)))

    held = first_wave.finish()
    for step in range(1, count - 1):
        first_wave.start()
        if step == count - 2:
            wave.behind(*held)
            wave.start()
        held = first_wave.finish()
    frames_own = own_half(frames_moved(*held))
    first_wave.behind(frames_own)
    first_wave.start()
    upstream_moved, upstream_got = swap_clips(upstream, after(upstream, frames_own))
    wave.finish(*first_wave.got)
    wave_a, wave_b = wave.pair(0), wave.pair(2)
    for step in range(1, count - 3):
        wave_a.start()
        wave_a.finish()
        wave_b.start()
        wave_b.finish()
    wave_a.start()
    frames_other = across_cores(after(frames_own, *first_wave.got))
    w_qkv, w_out_own, small = place_first(first_wave.halves(), shards, block, half, cut, small_rows)
    w_out_own = w_out_own.reshape(width, half)
    held_a = wave_a.finish(w_qkv)
    wave_b.behind(*held_a)
    wave_a.start()
    wave_b.start()
    w_qkv = w_qkv.reshape(width, 3 * half)
    small = small.reshape(shards, -1)[:, :small_size].reshape(-1).astype(F32)

    pieces = [small[index * width : (index + 1) * width] for index in range(8)]
    gain_one, shift_one, bias_query, bias_value, bias_out, gain_two, shift_two, bias_down = [
        piece[None] for piece in pieces
    ]
    bias_up = lax.dynamic_index_in_dim(
        small[8 * width :].reshape(shards, 2, 2, unit_block // 2), core, 1, keepdims=False
    )
    bias_query = lax.dynamic_slice_in_dim(bias_query, core * half, half, 1)
    bias_value = lax.dynamic_slice_in_dim(bias_value, core * half, half, 1)
    bias_qkv = jnp.concatenate([bias_query, jnp.zeros_like(bias_query), bias_value], 1)

    rep_of_clip = 2 * (rep // 2) + here % 2
    clip = (rep_of_clip * shards + here) // 2
    length = lax.dynamic_index_in_dim(lengths, clip, 0, keepdims=False)
    steps = jnp.arange(padded, dtype=jnp.int32)
    positions = jnp.concatenate([core * half_rows + steps, (1 - core) * half_rows + steps])
    real = jnp.concatenate([steps, steps]) < half_rows
    fill = jnp.where(real & (positions < length), 0.0, NEG_FILL).astype(BF16)
    first_row = jnp.arange(MASK_ROWS)[:, None] == 0
    masks = jnp.concatenate(
        [
            jnp.where(first_row, fill[None, :], 0.0),
            jnp.broadcast_to(jnp.where(first_row, 1.0, 0.0), (MASK_ROWS, rows)),
        ],
        0,
    ).astype(BF16)

    normed_one, qkv = project(
        after(frames_own, *wave_a.held, *wave_b.held), frames_other, gain_one, shift_one, w_qkv, bias_qkv
    )
    held = wave_a.finish(qkv) + wave_b.finish(qkv)
    w_out_other = across_cores(after(w_out_own, *held))
    upstream_own = own_half(upstream_moved(qkv, *held))
    wave_a.behind(w_out_other, upstream_own)
    wave_b.behind(w_out_other, upstream_own)
    wave_a.start()
    wave_b.start()
    upstream_other = across_cores(upstream_own)
    qkv = qkv.reshape(3, heads, HEAD_DIM, rows)
    some = heads // 2
    context_a, lse_a = attend(after(qkv, *wave_a.held, *wave_b.held), masks, 0, some)
    context_b, lse_b = attend(after(qkv, context_a), masks, some, heads - some)
    flat_a = context_a.reshape(half // 2, rows)
    flat_b = context_b.reshape(half // 2, rows)
    wave_a.finish(context_b)
    upstream_other = after(upstream_other, context_b)
    held = wave_b.finish(context_b, upstream_other)
    wave_b.start()
    got_a = across_cores(after(flat_a, *wave_a.got, *held))
    got_b = across_cores(after(flat_b, *wave_a.got, *held))
    middle, normed_own = attended(
        (flat_a, flat_b), (got_a, got_b), w_out_own, w_out_other, frames_own, bias_out, gain_two, shift_two
    )
    normed_other = across_cores(normed_own)

    back = {name: order[::-1] for name, order in orders.items()}
    feed_names = (("zxy", "yxz"), ("zxy", "xyz"))
    groups = []

    def feed_half(index, weights, *behind):
        names = feed_names[index]
        sums, up_parts, down_parts = feed(
            after(normed_own, *behind),
            normed_other,
            upstream_own,
            upstream_other,
            weights,
            bias_up[:, index].reshape(1, quarter),
            [scatter_plan(back[name]) for name in names],
        )
        return sums, Halving([list(up_parts), list(down_parts)], [back[name] for name in names])

    (mixed_a, grad_a, send_a, sums_up_a), chunks_a = feed_half(0, wave_a.halves(), *held)
    wave_b.finish(grad_a)
    sent = chunks_a.step(*wave_b.got)
    send_a = after(send_a, *wave_b.got)
    got_sums_a = across_cores(send_a)
    (mixed_b, grad_b, send_b, sums_up_b), chunks_b = feed_half(1, wave_b.halves(), *sent, send_a)
    arrived = [after(got[0], grad_b) for got in chunks_a.got]
    chunks_a.got = [[got] for got in arrived]
    got_sums_a = after(got_sums_a, grad_b)
    got_sums_b = across_cores(after(send_b, got_sums_a, *arrived))
    grad_middle, grad_attended, sums_two = norm_back(
        (grad_a, grad_b, (got_sums_a, 0), (got_sums_b, 0)),
        middle,
        gain_two,
        upstream_own,
        True,
    )
    grad_attended_other = across_cores(grad_attended)
    sent = chunks_b.step(grad_attended_other)
    sent = sent + chunks_a.step(grad_attended_other)
    grad_context, out_parts = attended_back(
        after(grad_attended, *sent),
        grad_attended_other,
        w_out_own,
        w_out_other,
        (flat_a, flat_b),
        (got_a, got_b),
        scatter_plan(back["xyz"]),
        shards,
    )
    chunks_out = Halving([list(out_parts)], [back["xyz"]])
    grad_context = grad_context.reshape(heads, HEAD_DIM, rows)
    calls = 4
    each = heads // calls
    grads = []
    sent = []
    for index in range(calls):
        inside = index * each
        context, lse = (context_a, lse_a) if inside < some else (context_b, lse_b)
        grads.append(
            attend_back(
                after(qkv, *sent), masks, grad_context, context, lse, inside, inside % some, each
            )
        )
        done = grads[-1][0]
        if index == 0:
            mixed, mixed_low = mix(
                after(mixed_a, done), mixed_b, got_sums_a, got_sums_b, middle, bias_down
            )
            sent = [mixed_low] + chunks_out.step(mixed_low)
        elif index == 1:
            for _ in range(count - 4):
                chunks_a.step(done)
            sent = chunks_a.step(done)
            sent = sent + chunks_b.step(done) + chunks_out.step(done)
        elif index == 2:
            sent = chunks_a.step(done)
            sent = sent + chunks_b.step(done) + chunks_out.step(done)
            for _ in range(count - 4):
                sent = chunks_b.step() + chunks_out.step()
            mixed_low = after(mixed_low, *sent)
            sent = sent + [mixed_low]
            swapped_mixed, mixed_got = swap_clips(mixed[:half_rows], mixed_low)
        else:
            own_a = chunks_a.result(done)
            sent = chunks_b.step(done) + own_a + chunks_out.step(done)
    flat = [[piece[which].reshape(each * HEAD_DIM, rows) for piece in grads] for which in range(3)]
    flat[0][0] = after(flat[0][0], *sent)
    names = ("zxy", "xyz", "yzx")
    parts = project_grads(normed_one, flat, [scatter_plan(back[name]) for name in names])
    own_b = chunks_b.result(parts[0][0])
    (own_out,) = chunks_out.result(parts[0][0])
    early = [over_groups(value) for value in own_a + own_b + [own_out]]
    cut_rows = block // 2
    wide_out = jnp.concatenate([early[4][:, :cut_rows], early[4][:, cut_rows:]], 2)
    early_other = across_cores(jnp.concatenate(early[:4] + [wide_out], 1))
    chunks_late = Halving(parts, [back[name] for name in names])
    sent = chunks_late.step(*own_b, own_out, after(mixed_got, parts[0][0]))
    flat[0][0] = after(flat[0][0], *sent)
    partial_one, send_one = project_back([piece for group in flat for piece in group], w_qkv)
    early_other = after(early_other, partial_one)
    splits = [early_other[:, i * block : (i + 1) * block] for i in range(4)]
    wide_out = early_other[:, 4 * block :]
    early_other = splits + [jnp.concatenate([wide_out[:, :, :half], wide_out[:, :, half:]], 1)]
    sent = chunks_late.step(partial_one)
    got_one = across_cores(after(send_one, *sent))
    grad_frames, early_send, sums_one = norm_back(
        (after(partial_one, *sent), got_one), frames_own, gain_one, grad_middle, False
    )
    sent = chunks_late.step(early_send)
    for _ in range(count - 4):
        sent = chunks_late.step()
    swapped, swapped_got = swap_clips(grad_frames[:half_rows], after(early_send, *sent))

    def in_half(values):
        return lax.dynamic_update_slice_in_dim(jnp.zeros((width,), F32), values, core * half, 0)

    def head_sums(pieces_of):
        return in_half(jnp.concatenate([jnp.sum(piece.astype(F32), 1) for piece in pieces_of]))

    sums_up = jnp.stack([sums.reshape(shards, unit_block // 2) for sums in (sums_up_a, sums_up_b)], 1)
    sums_up_all = lax.dynamic_update_slice_in_dim(
        jnp.zeros((shards, 2, unit_block), F32), sums_up.reshape(shards, 1, unit_block), core, 1
    )
    grad_small = jnp.concatenate(
        [
            sums_one[0],
            sums_one[1],
            head_sums(flat[0]),
            head_sums(flat[2]),
            sums_two[2],
            sums_two[0],
            sums_two[1],
            sums_two[3],
            sums_up_all.reshape(-1),
        ]
    ).reshape(shards, small_size)
    small_sum = SmallSum(grad_small)
    small_sum.start()
    mixed = swapped_mixed(*sent, small_sum.kept)
    small_sum.finish(mixed)
    sent = chunks_late.step(small_sum.held)
    small_sum.start()
    new_up, new_down = adam_feed(
        [after(early[0], *sent, small_sum.kept)] + early[1:4],
        early_other[:4],
        (master_up, first_up, second_up),
        (master_down, first_down, second_down),
        shards,
    )
    late = chunks_late.result(new_up[0])
    small_sum.finish(*late)
    small_sum.start()
    grad_frames = swapped(*late)
    total_out = by_core(core, early[4][0], after(early_other[4], *late)[0], 1)
    late = over_groups(jnp.concatenate(late, 0))
    late_other = across_cores(late)
    small_sum.finish(grad_frames)
    total_small = small_sum.result()
    total_qkv = by_core(core, late, late_other, 2)

    new_qkv = adam_update(master_qkv, first_qkv, second_qkv, total_qkv, RATES[0], DECAYS[0])
    new_out = adam_update(master_out, first_out, second_out, total_out, RATES[1], DECAYS[1])
    new_small = adam_update(
        master_small, first_small, second_small, total_small, RATES[4], DECAYS[4]
    )
    return (mixed, grad_frames) + new_qkv + new_out + new_up + new_down + new_small


def solution(mesh):
    rows = P(("rep", "shard"), None)
    weights = (P(None, "shard", None), P("shard", None), P("shard", None), P("shard", None), P("shard"))
    outs = (rows, rows)
    for spec in weights:
        outs = outs + (spec,) * 4
    return jax.shard_map(
        local,
        mesh=mesh,
        in_specs=(rows, rows, P()) + weights * 3,
        out_specs=outs,
        check_vma=False,
    )
```

```python
import functools
import math

import jax
import jax.numpy as jnp
from jax import lax
from jax.experimental import pallas as pl
from jax.experimental.pallas import tpu as pltpu
from jax.sharding import PartitionSpec as P

HEAD_DIM = 80
STEP = 10

LN_EPS = 1e-05
NEG_FILL = -1e30
BETA_ONE = 0.5
BETA_TWO = 0.5
ADAM_EPS = 1e-08
RATES = (0.04, 0.5, 0.04, 0.02, 0.3)
DECAYS = (0.01, 0.01, 0.01, 0.01, 0.0)

F32 = jnp.float32
BF16 = jnp.bfloat16
MIB = 1024 * 1024
SCALING = HEAD_DIM**-0.5
SCORE_SCALE = SCALING * math.log2(math.e)
MASK_ROWS = 16
SMALL_COST = pl.CostEstimate(flops=0, bytes_accessed=MIB, transcendentals=0)
VMEM_SPEC = pl.BlockSpec(memory_space=pltpu.VMEM)
ANY_SPEC = pl.BlockSpec(memory_space=pl.ANY)
NN = (((1,), (0,)), ((), ()))
NT = (((1,), (1,)), ((), ()))


def product(left, right, dims=NN):
    return lax.dot_general(left, right, dims, preferred_element_type=F32)


def call(body, out_shape, limit=48, **options):
    return pl.pallas_call(
        body,
        out_shape=out_shape,
        compiler_params=pltpu.CompilerParams(vmem_limit_bytes=limit * MIB),
        cost_estimate=SMALL_COST,
        **options,
    )


def array(shape, dtype):
    return jax.ShapeDtypeStruct(tuple(shape), dtype)


def xor_pairs(count, mask):
    return [(source, source ^ mask) for source in range(count)]


def across_cores(value):
    return lax.ppermute(value, "rep", xor_pairs(lax.axis_size("rep"), 1))


def swap_pairs():
    reps, shards = lax.axis_size("rep"), lax.axis_size("shard")
    pairs = []
    for rep in range(reps):
        for shard in range(shards):
            if (rep % 2) != (shard % 2):
                pairs.append((rep * shards + shard, (rep ^ 1) * shards + (shard ^ 1)))
    return pairs


def swap_clips(own, sent):
    got = lax.ppermute(sent, ("rep", "shard"), swap_pairs())
    moved = (lax.axis_index("rep") % 2) != (lax.axis_index("shard") % 2)

    def finish(*behind):
        arrived = (after(got, *behind) if behind else got)[: own.shape[0]]
        return jnp.where(moved, arrived.astype(own.dtype), own)

    return finish, got


def after(value, *others):
    return lax.optimization_barrier((value,) + others)[0]


def flip(index, mask):
    out, bit = index, 1
    while bit <= mask:
        if mask & bit:
            out = out + bit * (1 - 2 * ((index // bit) % 2))
        bit *= 2
    return out


def gather_orders(shards):
    far = [1 << k for k in range(int(math.log2(shards)))][::-1]
    most = [b for b in far if b >= 8]
    axes = {"x": 1, "y": 2, "z": 4}
    names = ("xyz", "xzy", "yxz", "yzx", "zxy", "zyx")
    return {name: most + [axes[axis] for axis in name] for name in names}


def relative_places(order):
    places = [0]
    for mask in order:
        places = places + [mask ^ r for r in places]
    return places


class Doubling:
    def __init__(self, blocks, orders):
        self.held, self.orders, self.step, self.got = blocks, orders, 0, None

    def behind(self, *others):
        self.held = [after(held, *others) for held in self.held]

    def start(self):
        shards = lax.axis_size("shard")
        masks = [order[self.step] for order in self.orders]
        if self.step == 0:
            rows = [held.shape[1] for held in self.held]
            together = jnp.concatenate(self.held, 1)
            together = lax.ppermute(together, "shard", xor_pairs(shards, masks[0]))
            ends = [sum(rows[: i + 1]) for i in range(len(rows))]
            self.got = [together[:, end - row : end] for end, row in zip(ends, rows)]
        else:
            self.got = [
                lax.ppermute(held, "shard", xor_pairs(shards, mask))
                for held, mask in zip(self.held, masks)
            ]
        self.step += 1

    def finish(self, *behind):
        if behind:
            self.got = [after(got, *behind) for got in self.got]
        if self.step < len(self.orders[0]):
            self.held = [jnp.concatenate(pair, 0) for pair in zip(self.held, self.got)]
        return self.held

    def halves(self):
        return list(zip(self.held, self.got, self.orders))

    def pair(self, at):
        part = Doubling(self.held[at : at + 2], self.orders[at : at + 2])
        part.step = self.step
        return part


def scatter_plan(order):
    kept = [0]
    sent = []
    for mask in order[::-1]:
        sent.append([mask ^ r for r in kept])
        kept = kept + sent[-1]
    return sent[::-1] + [[0]]


class Halving:
    def __init__(self, chunks, orders):
        self.chunks, self.orders = chunks, orders
        self.got = [[] for _ in chunks]

    def step(self, *behind):
        index = len(self.got[0])
        shards = lax.axis_size("shard")
        sends = [chunk[index] for chunk in self.chunks]
        if behind:
            sends = [after(send, *behind) for send in sends]
        if index:
            sends = add_blocks(sends, self.got, 1, BF16)
        masks = [order[index] for order in self.orders]
        if index == len(self.orders[0]) - 1 and len(sends) > 1:
            rows = [send.shape[1] for send in sends]
            together = jnp.concatenate(sends, 1)
            together = lax.ppermute(together, "shard", xor_pairs(shards, masks[0]))
            ends = [sum(rows[: i + 1]) for i in range(len(rows))]
            arrived = [together[:, end - row : end] for end, row in zip(ends, rows)]
        else:
            arrived = [
                lax.ppermute(send, "shard", xor_pairs(shards, mask))
                for send, mask in zip(sends, masks)
            ]
        for got, new in zip(self.got, arrived):
            got.append(new)
        return sends

    def result(self, *behind):
        stays = [chunk[-1] for chunk in self.chunks]
        if behind:
            stays = [after(stay, *behind) for stay in stays]
        return add_blocks(stays, self.got, 0, F32)


def over_groups(value):
    reps = lax.axis_size("rep")
    mask = 2
    while mask < reps:
        value = value + lax.ppermute(value, "rep", xor_pairs(reps, mask))
        mask *= 2
    return value


class SmallSum:
    def __init__(self, vector):
        self.held, self.mask = vector, vector.shape[0] // 2
        self.kept = self.got = None

    def start(self):
        shards, here = lax.axis_size("shard"), lax.axis_index("shard")
        upper = (here // self.mask) % 2 == 1
        low, high = self.held[: self.mask], self.held[self.mask :]
        self.kept = jnp.where(upper, high, low)
        self.got = lax.ppermute(
            jnp.where(upper, low, high), "shard", xor_pairs(shards, self.mask)
        )
        self.mask //= 2

    def finish(self, *behind):
        self.held = self.kept + (after(self.got, *behind) if behind else self.got)
        return self.held

    def result(self):
        while self.mask >= 1:
            self.start()
            self.finish()
        reps = lax.axis_size("rep")
        held, mask = self.held[0], 1
        while mask < reps:
            held = held + lax.ppermute(held, "rep", xor_pairs(reps, mask))
            mask *= 2
        return held


def row_slice(start, size):
    return pl.ds(pl.multiple_of(start, 8), size)


def place_first(halves, shards, block, half, cut, small_rows):
    rest = block - 2 * cut

    def body(*refs):
        ins, (qkv, out, small) = refs[:6], refs[6:]
        here = lax.axis_index("shard")
        for index, (low, _, order) in enumerate(halves):
            for place, rel in enumerate(relative_places(order)):
                ref = ins[2 * index + place // low.shape[0]].at[place % low.shape[0]]
                at = flip(here, rel)
                qkv[at, :, index * half : (index + 1) * half] = ref[:block, :]
                if index < 2:
                    out[at, index * cut : (index + 1) * cut, :] = ref[block : block + cut, :]
                else:
                    out[at, 2 * cut :, :] = ref[block : block + rest, :]
                    small[at] = ref[block + rest :, :]

    shapes = (
        array((shards, block, 3 * half), BF16),
        array((shards, block, half), BF16),
        array((shards, small_rows, half), BF16),
    )
    return call(
        body, shapes, in_specs=[VMEM_SPEC] * 6, out_specs=[VMEM_SPEC] * 3, name="place_first"
    )(*[part for low, got, _ in halves for part in (low, got)])


def write_parts(outs, plan, source, here):
    for out, part in zip(outs, plan):
        for place, rel in enumerate(part):
            out[place] = source[flip(here, rel)]


def add_blocks(firsts, others, place, dtype):
    inputs, specs = [], []
    for first, rest in zip(firsts, others):
        inputs.append(first)
        specs.append(pl.BlockSpec(first.shape, lambda i: (0, 0, 0)))
        for other in rest:
            inputs.append(other)
            specs.append(pl.BlockSpec(first.shape, lambda i, at=place: (at, 0, 0)))

    def body(*refs):
        at = 0
        for index, rest in enumerate(others):
            total = refs[at][...].astype(F32)
            for ref in refs[at + 1 : at + 1 + len(rest)]:
                total = total + ref[...].astype(F32)
            refs[len(inputs) + index][...] = total.astype(dtype)
            at += 1 + len(rest)

    return list(call(
        body,
        [array(first.shape, dtype) for first in firsts],
        grid=(1,),
        in_specs=specs,
        out_specs=[pl.BlockSpec(first.shape, lambda i: (0, 0, 0)) for first in firsts],
        name="add_blocks",
    )(*inputs))


def part_shapes(plan, rows, width):
    return [array((len(part), rows, width), BF16) for part in plan]


def norm_rows(values):
    center = values - jnp.mean(values, -1, keepdims=True)
    spread = jnp.mean(center * center, -1, keepdims=True)
    inverse = lax.rsqrt(spread + LN_EPS)
    return center * inverse, inverse


def project(own, other, gain, shift, w_qkv, bias):
    padded, width = own.shape
    columns = w_qkv.shape[1]
    third = columns // 3
    step = padded // 2

    def body(own_ref, other_ref, gain_ref, shift_ref, w_ref, bias_ref, normed_ref, out_ref):
        index = pl.program_id(0)
        values = jnp.where(index < 2, own_ref[...], other_ref[...]).astype(F32)
        unit, _ = norm_rows(values)
        normed = (unit * gain_ref[...] + shift_ref[...]).astype(BF16)
        normed_ref[...] = normed
        for part in range(3):
            cols = slice(part * third, (part + 1) * third)
            result = product(normed, w_ref[:, cols]) + bias_ref[:, cols]
            out_ref[cols, :] = result.astype(BF16).T

    line = pl.BlockSpec((1, width), lambda i: (0, 0))
    return call(
        body,
        (array((2 * padded, width), BF16), array((columns, 2 * padded), BF16)),
        grid=(4,),
        in_specs=[
            pl.BlockSpec((step, width), lambda i: (jnp.minimum(i, 1), 0)),
            pl.BlockSpec((step, width), lambda i: (jnp.maximum(i - 2, 0), 0)),
            line,
            line,
            pl.BlockSpec((width, columns), lambda i: (0, 0)),
            pl.BlockSpec((1, columns), lambda i: (0, 0)),
        ],
        out_specs=(
            pl.BlockSpec((step, width), lambda i: (i, 0)),
            pl.BlockSpec((columns, step), lambda i: (0, i)),
        ),
        name="project",
    )(own, other, gain, shift, w_qkv, bias)


def attend_kernel(mask_ref, q_ref, k_ref, v_ref, out_ref, lse_ref, kt, qt, *, step):
    dim, keys = k_ref.shape
    kt[...] = jnp.zeros_like(kt)
    kt[:dim, :] = k_ref[...]
    kt[dim : dim + MASK_ROWS, :] = mask_ref[:MASK_ROWS, :]
    k_rows = kt[...].T
    qt[...] = jnp.zeros_like(qt)
    qt[:dim, :] = q_ref[...]
    qt[dim : dim + MASK_ROWS, :] = mask_ref[MASK_ROWS:, :]
    for start in range(0, keys, step):
        cols = slice(start, start + step)
        scores = jnp.dot(k_rows, qt[:, cols], preferred_element_type=F32)
        top = jnp.max(scores, 0, keepdims=True) * SCORE_SCALE
        powers = jnp.exp2(scores * SCORE_SCALE - top)
        total = jnp.sum(powers, 0, keepdims=True)
        context = jnp.dot(v_ref[...], powers.astype(BF16), preferred_element_type=F32)
        out_ref[:, cols] = (context / total).astype(BF16)
        lse_ref[:, cols] = top + jnp.log2(total)


def attend(qkv, masks, first, heads):
    _, _, dim, rows = qkv.shape
    step = 512

    def head_block(which):
        return pl.BlockSpec((None, None, dim, rows), lambda h: (which, first + h, 0, 0))

    return pl.pallas_call(
        functools.partial(attend_kernel, step=step),
        grid=(heads,),
        out_shape=(
            jax.ShapeDtypeStruct((heads, dim, rows), BF16),
            jax.ShapeDtypeStruct((heads, 1, rows), F32),
        ),
        in_specs=[
            pl.BlockSpec(masks.shape, lambda h: (0, 0)),
            head_block(0),
            head_block(1),
            head_block(2),
        ],
        out_specs=(
            pl.BlockSpec((None, dim, rows), lambda h: (h, 0, 0)),
            pl.BlockSpec((None, 1, rows), lambda h: (h, 0, 0)),
        ),
        scratch_shapes=[pltpu.VMEM((128, rows), BF16), pltpu.VMEM((128, rows), BF16)],
        compiler_params=pltpu.CompilerParams(vmem_limit_bytes=48 * MIB),
        cost_estimate=SMALL_COST,
        name="attend",
    )(masks, qkv, qkv, qkv)


def attend_back_kernel(
    mask_ref, q_ref, k_ref, v_ref, g_ref, ctx_ref, lse_ref, gq_ref, gk_ref, gv_ref, kt, qt, pad, acc_k, acc_v, *, step
):
    dim, keys = k_ref.shape
    kt[...] = jnp.zeros_like(kt)
    kt[:dim, :] = k_ref[...]
    kt[dim : dim + MASK_ROWS, :] = mask_ref[:MASK_ROWS, :]
    k_rows = kt[...].T
    pad[...] = jnp.zeros_like(pad)
    pad[:dim, :] = v_ref[...]
    v_rows = pad[...].T
    qt[...] = jnp.zeros_like(qt)
    qt[:dim, :] = q_ref[...]
    qt[dim : dim + MASK_ROWS, :] = mask_ref[MASK_ROWS:, :]
    q_rows = qt[...].T
    pad[:dim, :] = g_ref[...]
    g_rows = pad[...].T
    inner = jnp.sum(g_ref[...].astype(F32) * ctx_ref[...].astype(F32), 0, keepdims=True)
    for start in range(0, keys, step):
        cols = slice(start, start + step)
        scores = jnp.dot(k_rows, qt[:, cols], preferred_element_type=F32)
        probs = jnp.exp2(scores * SCORE_SCALE - lse_ref[:, cols])
        grad_probs = jnp.dot(v_rows, pad[:, cols], preferred_element_type=F32)
        grad_scores = (probs * (grad_probs - inner[:, cols])).astype(BF16)
        part_v = jnp.dot(probs.astype(BF16), g_rows[cols, :], preferred_element_type=F32)
        part_k = jnp.dot(grad_scores, q_rows[cols, :], preferred_element_type=F32)
        if start == 0:
            acc_v[...] = part_v
            acc_k[...] = part_k
        else:
            acc_v[...] += part_v
            acc_k[...] += part_k
        grad_query = jnp.dot(k_ref[...], grad_scores, preferred_element_type=F32)
        gq_ref[:, cols] = (grad_query * SCALING).astype(BF16)
    gv_ref[...] = acc_v[...].T[:dim, :].astype(BF16)
    gk_ref[...] = (acc_k[...].T[:dim, :] * SCALING).astype(BF16)


def attend_back(qkv, masks, grad_context, context, lse, first, inside, heads):
    _, dim, rows = context.shape
    step = 512

    def head_block(which):
        return pl.BlockSpec((None, None, dim, rows), lambda h: (which, first + h, 0, 0))

    plain = pl.BlockSpec((None, dim, rows), lambda h: (h, 0, 0))
    return pl.pallas_call(
        functools.partial(attend_back_kernel, step=step),
        grid=(heads,),
        out_shape=[jax.ShapeDtypeStruct((heads, dim, rows), BF16)] * 3,
        in_specs=[
            pl.BlockSpec(masks.shape, lambda h: (0, 0)),
            head_block(0),
            head_block(1),
            head_block(2),
            pl.BlockSpec((None, dim, rows), lambda h: (first + h, 0, 0)),
            pl.BlockSpec((None, dim, rows), lambda h: (inside + h, 0, 0)),
            pl.BlockSpec((None, 1, rows), lambda h: (inside + h, 0, 0)),
        ],
        out_specs=[plain] * 3,
        scratch_shapes=[pltpu.VMEM((128, rows), BF16)] * 3 + [pltpu.VMEM((rows, 128), F32)] * 2,
        compiler_params=pltpu.CompilerParams(vmem_limit_bytes=48 * MIB),
        cost_estimate=SMALL_COST,
        name="attend_back",
    )(masks, qkv, qkv, qkv, grad_context, context, lse)


def attended(contexts, gots, w_own, w_other, frames, bias, gain, shift):
    padded, width = frames.shape
    half = width // 2
    step = 256
    tiles = padded // step

    def body(ca, cb, ga, gb, wo_ref, wt_ref, frames_ref, bias_ref, gain_ref, shift_ref, middle_ref, normed_ref):
        first = lax.axis_index("rep") % 2 == 0
        own = jnp.concatenate([ca[...], cb[...]], 0)
        got = jnp.concatenate([ga[...], gb[...]], 0)
        low = jnp.where(first, own, got).T
        high = jnp.where(first, got, own).T
        by_own = product(low, wo_ref[:half, :]) + product(high, wo_ref[half:, :])
        by_other = product(low, wt_ref[:half, :]) + product(high, wt_ref[half:, :])
        result = jnp.concatenate(
            [jnp.where(first, by_own, by_other), jnp.where(first, by_other, by_own)], 1
        )
        middle = result + frames_ref[...].astype(F32) + bias_ref[...]
        middle_ref[...] = middle
        unit, _ = norm_rows(middle)
        normed_ref[...] = (unit * gain_ref[...] + shift_ref[...]).astype(BF16)

    part = half // 2
    line = pl.BlockSpec((1, width), lambda i: (0, 0))
    here = pl.BlockSpec((part, step), lambda i: (0, i))
    there = pl.BlockSpec((part, step), lambda i: (0, i + tiles))
    matrix = pl.BlockSpec((width, half), lambda i: (0, 0))
    rows = pl.BlockSpec((step, width), lambda i: (i, 0))
    return call(
        body,
        (array((padded, width), F32), array((padded, width), BF16)),
        grid=(tiles,),
        in_specs=[here, here, there, there, matrix, matrix, rows, line, line, line],
        out_specs=(rows, rows),
        name="attended",
    )(*contexts, *gots, w_own, w_other, frames, bias, gain, shift)


def feed(own, other, up_own, up_other, weights, bias, plans):
    padded, width = own.shape
    stacks_given = [part for halves in weights for part in halves[:2]] if isinstance(weights, list) else [weights]
    count_in = len(stacks_given)
    block, units = stacks_given[0].shape[-2:]
    shards = width // block
    tile = 256
    tiles = units // tile
    up_plan, down_plan = plans

    def body(*refs):
        x_refs, u_refs = refs[0:2], refs[2:4]
        stacks, refs = refs[4 : 4 + count_in], refs[4 + count_in :]
        bias_ref, mixed_own, grad_own, send, sums_ref = refs[:5]
        up_outs = refs[5 : 5 + len(up_plan)]
        down_outs = refs[5 + len(up_plan) : 5 + len(up_plan) + len(down_plan)]
        w_up, w_down, hidden_t, x_t, grad_pre, hidden, blocks, sems = refs[5 + len(up_plan) + len(down_plan) :]
        index = pl.program_id(0)
        here = lax.axis_index("shard")

        def rows_step(which):
            x_ref, u_ref = x_refs[which], u_refs[which]
            cols = slice(which * padded, (which + 1) * padded)
            wu, wd = w_up[...].reshape(width, units), w_down[...].reshape(units, width)

            def products(t):
                part = slice(t * tile, (t + 1) * tile)
                return product(x_ref[...], wu[:, part]), product(u_ref[...], wd[part, :], NT)

            ahead = products(0)
            for t in range(tiles):
                part = slice(t * tile, (t + 1) * tile)
                pre, grad_hidden = ahead
                if t + 1 < tiles:
                    ahead = products(t + 1)
                pre = pre + bias_ref[:, part]
                phi = 0.5 + 0.5 * lax.erf(pre * (0.5**0.5))
                hid = (pre * phi).astype(BF16)
                hidden[:, part] = hid
                hidden_t[part, cols] = hid.T
                density = jnp.exp(pre * pre * -0.5) * (1.0 / math.sqrt(2.0 * math.pi))
                grad = (grad_hidden * (phi + pre * density)).astype(BF16)
                grad_pre[cols, part] = grad
                total = jnp.sum(grad.astype(F32), 0, keepdims=True)
                if which == 1:
                    sums_ref[:, part] = total
                else:
                    sums_ref[:, part] += total
            mixed_ref, grad_ref = ((mixed_own, grad_own), (send.at[1], send.at[0]))[which]
            for t in range(width // tile):
                part = slice(t * tile, (t + 1) * tile)
                mixed_ref[:, part] = product(hidden[...], wd[:, part]).astype(mixed_ref.dtype)
                grad_ref[:, part] = product(grad_pre[cols, :], wu[part, :], NT).astype(grad_ref.dtype)

        @pl.when(index == 0)
        def _():
            copies = []

            def copy_in(source, matrix, at):
                copies.append(pltpu.make_async_copy(source, matrix.at[at], sems.at[len(copies)]))
                copies[-1].start()

            for which, matrix in enumerate((w_up, w_down)):
                if count_in == 1:
                    for at in range(shards):
                        copy_in(stacks[0].at[at, which], matrix, at)
                else:
                    for place, rel in enumerate(relative_places(weights[which][2])):
                        stack = stacks[2 * which + place // (shards // 2)]
                        copy_in(stack.at[place % (shards // 2)], matrix, flip(here, rel))
            for which in range(2):
                x_t[:, which * padded : (which + 1) * padded] = x_refs[which][...].T
            for copy in copies:
                copy.wait()
            rows_step(1)

        @pl.when(index == 1)
        def _():
            rows_step(0)

        @pl.when(index >= 2)
        def _():
            part = pl.ds(pl.multiple_of((index - 2) * tile, tile), tile)
            down = product(hidden_t[:, :padded], u_refs[0][:, part]) + product(
                hidden_t[:, padded:], u_refs[1][:, part]
            )
            blocks[...] = down.astype(BF16).reshape(shards, block, tile)
            write_parts(down_outs, down_plan, blocks, here)
            up = product(x_t[...], grad_pre[:, part])
            blocks[...] = up.astype(BF16).reshape(shards, block, tile)
            write_parts(up_outs, up_plan, blocks, here)

    once = pl.Buffered(1)
    whole = pl.BlockSpec((padded, width), lambda i: (0, 0), pipeline_mode=once)
    line = pl.BlockSpec((1, units), lambda i: (0, 0))
    shapes = [
        array((padded, width), F32),
        array((padded, width), F32),
        array((2, padded, width), BF16),
        array((1, units), F32),
    ]
    specs = [
        whole,
        whole,
        pl.BlockSpec((2, padded, width), lambda i: (0, 0, 0), pipeline_mode=once),
        line,
    ]
    for plan, size in ((up_plan, units), (down_plan, width)):
        shapes += part_shapes(plan, block, size)
        specs += [
            pl.BlockSpec((len(part), block, tile), lambda i: (0, 0, jnp.maximum(i - 2, 0)))
            for part in plan
        ]
    results = call(
        body,
        shapes,
        limit=60,
        grid=(2 + tiles,),
        in_specs=[whole] * 4 + [ANY_SPEC] * count_in + [line],
        out_specs=specs,
        scratch_shapes=[
            pltpu.VMEM((shards, block, units), BF16),
            pltpu.VMEM((shards, block, width), BF16),
            pltpu.VMEM((units, 2 * padded), BF16),
            pltpu.VMEM((width, 2 * padded), BF16),
            pltpu.VMEM((2 * padded, units), BF16),
            pltpu.VMEM((padded, units), BF16),
            pltpu.VMEM((shards, block, tile), BF16),
            pltpu.SemaphoreType.DMA((2 * shards,)),
        ],
        name="feed",
    )(own, other, up_own, up_other, *stacks_given, bias)
    count = 4 + len(up_plan)
    return results[:4], results[4:count], results[count:]


def norm_back(sums, values, gain, base, more_sums):
    given = [item if isinstance(item, tuple) else (item, None) for item in (*sums, values, base)]
    padded, width = given[0][0].shape[-2:]
    step = 256

    def body(*refs):
        parts = refs[: len(sums)]
        values_ref, base_ref, gain_ref = refs[len(parts) : len(parts) + 3]
        outs = refs[len(parts) + 3 :]
        sums_ref = outs[-1]
        grads = parts[0][...].astype(F32)
        for ref in parts[1:]:
            grads = grads + ref[...].astype(F32)
        unit, inverse = norm_rows(values_ref[...].astype(F32))
        scaled = grads * gain_ref[...]
        inner = (
            scaled
            - jnp.mean(scaled, -1, keepdims=True)
            - unit * jnp.mean(scaled * unit, -1, keepdims=True)
        )
        result = base_ref[...].astype(F32) + inverse * inner
        outs[0][...] = result
        low = result.astype(BF16)
        outs[1][...] = low
        lines = [jnp.sum(grads * unit, 0, keepdims=True), jnp.sum(grads, 0, keepdims=True)]
        if more_sums:
            lines.append(jnp.sum(low.astype(F32), 0, keepdims=True))
            lines.append(jnp.sum(base_ref[...].astype(F32), 0, keepdims=True))

        @pl.when(pl.program_id(0) == 0)
        def _():
            sums_ref[...] = jnp.zeros_like(sums_ref)

        for place, line in enumerate(lines):
            sums_ref[place : place + 1, :] += line

    rows = pl.BlockSpec((step, width), lambda i: (i, 0))
    shapes = [array((padded, width), F32), array((padded, width), BF16), array((8, width), F32)]
    return call(
        body,
        shapes,
        grid=(padded // step,),
        in_specs=[
            rows
            if place is None
            else pl.BlockSpec((None, step, width), lambda i, place=place: (place, i, 0))
            for _, place in given
        ]
        + [pl.BlockSpec((1, width), lambda i: (0, 0))],
        out_specs=[rows] * (len(shapes) - 1) + [pl.BlockSpec((8, width), lambda i: (0, 0))],
        name="norm_back",
    )(*[item for item, _ in given], gain)


def mix(own_a, own_b, got_a, got_b, middle, bias):
    padded, width = middle.shape
    step = 256

    def body(a_ref, b_ref, ga_ref, gb_ref, middle_ref, bias_ref, out_ref, low_ref):
        total = a_ref[...] + b_ref[...] + ga_ref[...].astype(F32) + gb_ref[...].astype(F32)
        total = total + bias_ref[...] + middle_ref[...]
        out_ref[...] = total
        low_ref[...] = total.astype(BF16)

    rows = pl.BlockSpec((step, width), lambda i: (i, 0))
    plane = pl.BlockSpec((None, step, width), lambda i: (1, i, 0))
    return call(
        body,
        (array((padded, width), F32), array((padded, width), BF16)),
        grid=(padded // step,),
        in_specs=[rows, rows, plane, plane, rows, pl.BlockSpec((1, width), lambda i: (0, 0))],
        out_specs=(rows, rows),
        name="mix",
    )(own_a, own_b, got_a, got_b, middle, bias)


def attended_back(own, other, w_own, w_other, contexts, gots, plan, shards):
    padded, width = own.shape
    half = width // 2
    block = width // shards

    def body(*refs):
        own_ref, other_ref, wo_ref, wt_ref, ca, cb, ga, gb = refs[:8]
        context_ref, outs, blocks = refs[8], refs[9:-1], refs[-1]
        core = lax.axis_index("rep") % 2
        here = lax.axis_index("shard")
        mine = pl.ds(pl.multiple_of(core * half, half), half)
        theirs = pl.ds(pl.multiple_of((1 - core) * half, half), half)
        for place, ref in enumerate((own_ref, other_ref)):
            cols = slice(place * padded, (place + 1) * padded)
            result = product(wo_ref[mine, :], ref[:, mine], NT)
            result = result + product(wt_ref[mine, :], ref[:, theirs], NT)
            context_ref[:, cols] = result.astype(BF16)
        for heads, (pair, near, far) in enumerate(
            (
                ((ca, cb), slice(0, padded), slice(padded, 2 * padded)),
                ((ga, gb), slice(padded, 2 * padded), slice(0, padded)),
            )
        ):
            for place, ref in enumerate(pair):
                result = product(ref[:, near], own_ref[:, mine])
                result = result + product(ref[:, far], other_ref[:, mine])
                count = shards // 4
                at = (core if heads == 0 else 1 - core) * (shards // 2) + place * count
                blocks[pl.ds(at, count)] = result.astype(BF16).reshape(count, block, half)
        write_parts(outs, plan, blocks, here)

    shapes = [array((half, 2 * padded), BF16)] + part_shapes(plan, block, half)
    results = call(
        body,
        shapes,
        in_specs=[VMEM_SPEC] * 8,
        out_specs=[VMEM_SPEC] * len(shapes),
        scratch_shapes=[pltpu.VMEM((shards, block, half), BF16)],
        name="attended_back",
    )(own, other, w_own, w_other, *contexts, *gots)
    return results[0], results[1:]


def project_back(grads, w_qkv):
    part, rows = grads[0].shape
    count = len(grads)
    padded = rows // 2
    width, columns = w_qkv.shape

    def body(*refs):
        w_ref, own_ref, other_ref = refs[count:]

        def run(out_ref):
            stacked = jnp.concatenate([ref[...] for ref in refs[:count]], 0).T
            out_ref[...] = product(stacked, w_ref[...], NT).astype(out_ref.dtype)

        @pl.when(pl.program_id(0) == 0)
        def _():
            run(other_ref)

        @pl.when(pl.program_id(0) == 1)
        def _():
            run(own_ref)

    whole = pl.BlockSpec((padded, width), lambda i: (0, 0))
    return call(
        body,
        (array((padded, width), F32), array((padded, width), BF16)),
        grid=(2,),
        in_specs=[pl.BlockSpec((part, padded), lambda i: (0, 1 - i))] * count
        + [pl.BlockSpec((width, columns), lambda i: (0, 0))],
        out_specs=(whole, whole),
        name="project_back",
    )(*grads, w_qkv)


def project_grads(normed, groups, plans):
    rows, width = normed.shape
    half = sum(piece.shape[0] for piece in groups[0])
    shards = sum(len(p) for p in plans[0])
    block = width // shards
    given = [normed] + [piece for group in groups for piece in group]

    def body(*refs):
        normed_ref, outs, (turned, blocks) = refs[0], refs[len(given) : -2], refs[-2:]
        here = lax.axis_index("shard")
        turned[...] = normed_ref[...].T
        at, place_in = 0, 1
        for group, plan in zip(groups, plans):
            stacked = jnp.concatenate([ref[...] for ref in refs[place_in : place_in + len(group)]], 0)
            place_in += len(group)
            result = product(turned[...], stacked, NT)
            blocks[...] = result.astype(BF16).reshape(shards, block, half)
            write_parts(outs[at : at + len(plan)], plan, blocks, here)
            at += len(plan)

    shapes = []
    for plan in plans:
        shapes += part_shapes(plan, block, half)
    flat = call(
        body,
        shapes,
        in_specs=[VMEM_SPEC] * len(given),
        out_specs=[VMEM_SPEC] * len(shapes),
        scratch_shapes=[pltpu.VMEM((width, rows), BF16), pltpu.VMEM((shards, block, half), BF16)],
        name="project_grads",
    )(*given)
    parts, at = [], 0
    for plan in plans:
        parts.append(list(flat[at : at + len(plan)]))
        at += len(plan)
    return parts


def adam_values(master, moment_one, second, gradient, step_rate, decay_rate):
    momentum = BETA_ONE * moment_one.astype(F32) + (1.0 - BETA_ONE) * gradient
    variance = BETA_TWO * second + (1.0 - BETA_TWO) * gradient * gradient
    momentum_hat = momentum / (1.0 - BETA_ONE**STEP)
    variance_hat = variance / (1.0 - BETA_TWO**STEP)
    updated = master - step_rate * (
        momentum_hat / (jnp.sqrt(variance_hat) + ADAM_EPS) + decay_rate * master
    )
    return updated, updated.astype(BF16), momentum, variance


def adam_feed(own, other, up_state, down_state, shards):
    block, columns = up_state[0].shape
    down_rows, width = down_state[0].shape
    piece = columns // (4 * shards)
    step = 8
    tiles = block // step

    def gradients(refs, core):
        own_refs, other_refs = refs[:4], refs[4:8]
        first = core == 0
        lows = [jnp.where(first, a[0], b[0]) for a, b in zip(own_refs, other_refs)]
        highs = [jnp.where(first, b[0], a[0]) for a, b in zip(own_refs, other_refs)]
        return lows, highs

    def body(*refs):
        core = lax.axis_index("rep") % 2
        lows, highs = gradients(refs, core)
        ups = refs[8:11]
        downs = refs[11:14]
        up_outs, down_outs = refs[14:18], refs[18:22]
        sources = (lows[0], lows[2], highs[0], highs[2])
        gradient = jnp.concatenate(
            [
                source[:, at * piece : (at + 1) * piece]
                for at in range(shards)
                for source in sources
            ],
            1,
        )
        values = adam_values(*[ref[...] for ref in ups], gradient, RATES[2], DECAYS[2])
        for out, value in zip(up_outs, values):
            out[...] = value
        for place, gradient in enumerate((lows[1], lows[3], highs[1], highs[3])):
            values = adam_values(*[ref[place] for ref in downs], gradient, RATES[3], DECAYS[3])
            for out, value in zip(down_outs, values):
                out[place] = value

    grads = [pl.BlockSpec((1, step * 2, g.shape[2]), lambda i: (0, i, 0)) for g in own]
    up_spec = pl.BlockSpec((step * 2, columns), lambda i: (i, 0))
    down_spec = pl.BlockSpec((4, step * 2, width), lambda i: (0, i, 0))
    kinds = (F32, BF16, F32, F32)
    downs = [value.reshape(4, block, width) for value in down_state]
    results = call(
        body,
        [array((block, columns), kind) for kind in kinds]
        + [array((4, block, width), kind) for kind in kinds],
        grid=(-(-block // (step * 2)),),
        in_specs=grads * 2 + [up_spec] * 3 + [down_spec] * 3,
        out_specs=[up_spec] * 4 + [down_spec] * 4,
        name="adam_feed",
    )(*own, *other, *up_state, *downs)
    return tuple(results[:4]), tuple(value.reshape(down_rows, width) for value in results[4:])


def adam_update(master, moment_one, second, gradient, step_rate, decay_rate):
    momentum = BETA_ONE * moment_one.astype(F32) + (1.0 - BETA_ONE) * gradient
    variance = BETA_TWO * second + (1.0 - BETA_TWO) * gradient * gradient
    momentum_hat = momentum / (1.0 - BETA_ONE**STEP)
    variance_hat = variance / (1.0 - BETA_TWO**STEP)
    updated = master - step_rate * (
        momentum_hat / (jnp.sqrt(variance_hat) + ADAM_EPS) + decay_rate * master
    )
    return (updated, updated.astype(BF16), momentum, variance)


def by_core(core, own, other, axis):
    return jnp.where(
        core == 0, jnp.concatenate([own, other], axis), jnp.concatenate([other, own], axis)
    )


def local(
    frames,
    upstream,
    lengths,
    master_qkv,
    master_out,
    master_up,
    master_down,
    master_small,
    first_qkv,
    first_out,
    first_up,
    first_down,
    first_small,
    second_qkv,
    second_out,
    second_up,
    second_down,
    second_small,
):
    half_rows, width = frames.shape
    shards, here = lax.axis_size("shard"), lax.axis_index("shard")
    rep = lax.axis_index("rep")
    core = rep % 2
    padded = -(-half_rows // 256) * 256
    rows = 2 * padded
    half = width // 2
    heads = half // HEAD_DIM
    units = master_up.shape[1] // 2
    unit_block = units // shards
    block = width // shards
    quarter = units // 2
    orders = gather_orders(shards)
    count = len(orders["xyz"])
    cut = 2 * block // 5
    small_rows = 16 * block // 80
    small_size = master_small.shape[0]

    frames_moved, _ = swap_clips(frames, frames)
    low_qkv = lax.dynamic_slice_in_dim(master_qkv, core * half, half, 2).astype(BF16)
    low_out = lax.dynamic_slice_in_dim(master_out, core * half, half, 1).astype(BF16)
    low_small = jnp.pad(master_small.astype(BF16), (0, small_rows * half - small_size))
    first_wave = Doubling(
        [
            jnp.concatenate([low_qkv[0], low_out[:cut]], 0)[None],
            jnp.concatenate([low_qkv[1], low_out[cut : 2 * cut]], 0)[None],
            jnp.concatenate(
                [low_qkv[2], low_out[2 * cut :], low_small.reshape(small_rows, half)], 0
            )[None],
        ],
        [orders["xzy"], orders["yxz"], orders["zyx"]],
    )
    first_wave.start()

    low_up = lax.dynamic_index_in_dim(
        master_up.reshape(block, shards, 2, 2, unit_block // 2), core, 2, keepdims=False
    ).astype(BF16)
    low_down = lax.dynamic_slice_in_dim(master_down, core * unit_block, unit_block, 0).astype(BF16)
    low_ups = [low_up[:, :, index].reshape(block, quarter) for index in range(2)]
    wave = Doubling(
        [low_ups[0][None], low_down[None, :block], low_ups[1][None], low_down[None, block:]],
        [orders["zyx"], orders["xzy"], orders["xzy"], orders["yzx"]],
    )

    def own_half(values):
        return jnp.pad(values, ((0, padded - half_rows), (0, 0)))

    held = first_wave.finish()
    for step in range(1, count - 1):
        first_wave.start()
        if step == count - 2:
            wave.behind(*held)
            wave.start()
        held = first_wave.finish()
    frames_own = own_half(frames_moved(*held))
    first_wave.behind(frames_own)
    first_wave.start()
    upstream_moved, upstream_got = swap_clips(upstream, after(upstream, frames_own))
    wave.finish(*first_wave.got)
    wave_a, wave_b = wave.pair(0), wave.pair(2)
    for step in range(1, count - 3):
        wave_a.start()
        wave_a.finish()
        wave_b.start()
        wave_b.finish()
    wave_a.start()
    frames_other = across_cores(after(frames_own, *first_wave.got))
    w_qkv, w_out_own, small = place_first(first_wave.halves(), shards, block, half, cut, small_rows)
    w_out_own = w_out_own.reshape(width, half)
    held_a = wave_a.finish(w_qkv)
    wave_b.behind(*held_a)
    wave_a.start()
    wave_b.start()
    w_qkv = w_qkv.reshape(width, 3 * half)
    small = small.reshape(shards, -1)[:, :small_size].reshape(-1).astype(F32)

    pieces = [small[index * width : (index + 1) * width] for index in range(8)]
    gain_one, shift_one, bias_query, bias_value, bias_out, gain_two, shift_two, bias_down = [
        piece[None] for piece in pieces
    ]
    bias_up = lax.dynamic_index_in_dim(
        small[8 * width :].reshape(shards, 2, 2, unit_block // 2), core, 1, keepdims=False
    )
    bias_query = lax.dynamic_slice_in_dim(bias_query, core * half, half, 1)
    bias_value = lax.dynamic_slice_in_dim(bias_value, core * half, half, 1)
    bias_qkv = jnp.concatenate([bias_query, jnp.zeros_like(bias_query), bias_value], 1)

    rep_of_clip = 2 * (rep // 2) + here % 2
    clip = (rep_of_clip * shards + here) // 2
    length = lax.dynamic_index_in_dim(lengths, clip, 0, keepdims=False)
    steps = jnp.arange(padded, dtype=jnp.int32)
    positions = jnp.concatenate([core * half_rows + steps, (1 - core) * half_rows + steps])
    real = jnp.concatenate([steps, steps]) < half_rows
    fill = jnp.where(real & (positions < length), 0.0, NEG_FILL).astype(BF16)
    first_row = jnp.arange(MASK_ROWS)[:, None] == 0
    masks = jnp.concatenate(
        [
            jnp.where(first_row, fill[None, :], 0.0),
            jnp.broadcast_to(jnp.where(first_row, 1.0, 0.0), (MASK_ROWS, rows)),
        ],
        0,
    ).astype(BF16)

    normed_one, qkv = project(
        after(frames_own, *wave_a.held, *wave_b.held), frames_other, gain_one, shift_one, w_qkv, bias_qkv
    )
    held = wave_a.finish(qkv) + wave_b.finish(qkv)
    w_out_other = across_cores(after(w_out_own, *held))
    upstream_own = own_half(upstream_moved(qkv, *held))
    wave_a.behind(w_out_other, upstream_own)
    wave_b.behind(w_out_other, upstream_own)
    wave_a.start()
    wave_b.start()
    upstream_other = across_cores(upstream_own)
    qkv = qkv.reshape(3, heads, HEAD_DIM, rows)
    some = heads // 2
    context_a, lse_a = attend(after(qkv, *wave_a.held, *wave_b.held), masks, 0, some)
    context_b, lse_b = attend(after(qkv, context_a), masks, some, heads - some)
    flat_a = context_a.reshape(half // 2, rows)
    flat_b = context_b.reshape(half // 2, rows)
    wave_a.finish(context_b)
    upstream_other = after(upstream_other, context_b)
    held = wave_b.finish(context_b, upstream_other)
    wave_b.start()
    got_a = across_cores(after(flat_a, *wave_a.got, *held))
    got_b = across_cores(after(flat_b, *wave_a.got, *held))
    middle, normed_own = attended(
        (flat_a, flat_b), (got_a, got_b), w_out_own, w_out_other, frames_own, bias_out, gain_two, shift_two
    )
    normed_other = across_cores(normed_own)

    back = {name: order[::-1] for name, order in orders.items()}
    feed_names = (("zxy", "yxz"), ("zxy", "xyz"))
    groups = []

    def feed_half(index, weights, *behind):
        names = feed_names[index]
        sums, up_parts, down_parts = feed(
            after(normed_own, *behind),
            normed_other,
            upstream_own,
            upstream_other,
            weights,
            bias_up[:, index].reshape(1, quarter),
            [scatter_plan(back[name]) for name in names],
        )
        return sums, Halving([list(up_parts), list(down_parts)], [back[name] for name in names])

    (mixed_a, grad_a, send_a, sums_up_a), chunks_a = feed_half(0, wave_a.halves(), *held)
    wave_b.finish(grad_a)
    sent = chunks_a.step(*wave_b.got)
    send_a = after(send_a, *wave_b.got)
    got_sums_a = across_cores(send_a)
    (mixed_b, grad_b, send_b, sums_up_b), chunks_b = feed_half(1, wave_b.halves(), *sent, send_a)
    arrived = [after(got[0], grad_b) for got in chunks_a.got]
    chunks_a.got = [[got] for got in arrived]
    got_sums_a = after(got_sums_a, grad_b)
    got_sums_b = across_cores(after(send_b, got_sums_a, *arrived))
    grad_middle, grad_attended, sums_two = norm_back(
        (grad_a, grad_b, (got_sums_a, 0), (got_sums_b, 0)),
        middle,
        gain_two,
        upstream_own,
        True,
    )
    grad_attended_other = across_cores(grad_attended)
    sent = chunks_b.step(grad_attended_other)
    sent = sent + chunks_a.step(grad_attended_other)
    grad_context, out_parts = attended_back(
        after(grad_attended, *sent),
        grad_attended_other,
        w_out_own,
        w_out_other,
        (flat_a, flat_b),
        (got_a, got_b),
        scatter_plan(back["xzy"]),
        shards,
    )
    chunks_out = Halving([list(out_parts)], [back["xzy"]])
    grad_context = grad_context.reshape(heads, HEAD_DIM, rows)
    calls = 4
    each = heads // calls
    grads = []
    sent = []
    for index in range(calls):
        inside = index * each
        context, lse = (context_a, lse_a) if inside < some else (context_b, lse_b)
        grads.append(
            attend_back(
                after(qkv, *sent), masks, grad_context, context, lse, inside, inside % some, each
            )
        )
        done = grads[-1][0]
        if index == 0:
            mixed, mixed_low = mix(
                after(mixed_a, done), mixed_b, got_sums_a, got_sums_b, middle, bias_down
            )
            sent = [mixed_low] + chunks_out.step(mixed_low)
        elif index == 1:
            for _ in range(count - 4):
                chunks_a.step(done)
            sent = chunks_a.step(done)
            sent = sent + chunks_b.step(done) + chunks_out.step(done)
        elif index == 2:
            sent = chunks_a.step(done)
            sent = sent + chunks_b.step(done) + chunks_out.step(done)
            for _ in range(count - 4):
                sent = chunks_b.step() + chunks_out.step()
            mixed_low = after(mixed_low, *sent)
            sent = sent + [mixed_low]
            swapped_mixed, mixed_got = swap_clips(mixed[:half_rows], mixed_low)
        else:
            own_a = chunks_a.result(done)
            sent = chunks_b.step(done) + own_a + chunks_out.step(done)
    flat = [[piece[which].reshape(each * HEAD_DIM, rows) for piece in grads] for which in range(3)]
    flat[0][0] = after(flat[0][0], *sent)
    names = ("zxy", "xyz", "yzx")
    parts = project_grads(normed_one, flat, [scatter_plan(back[name]) for name in names])
    own_b = chunks_b.result(parts[0][0])
    (own_out,) = chunks_out.result(parts[0][0])
    early = [over_groups(value) for value in own_a + own_b + [own_out]]
    cut_rows = block // 2
    wide_out = jnp.concatenate([early[4][:, :cut_rows], early[4][:, cut_rows:]], 2)
    early_other = across_cores(jnp.concatenate(early[:4] + [wide_out], 1))
    chunks_late = Halving(parts, [back[name] for name in names])
    sent = chunks_late.step(*own_b, own_out, after(mixed_got, parts[0][0]))
    flat[0][0] = after(flat[0][0], *sent)
    partial_one, send_one = project_back([piece for group in flat for piece in group], w_qkv)
    early_other = after(early_other, partial_one)
    splits = [early_other[:, i * block : (i + 1) * block] for i in range(4)]
    wide_out = early_other[:, 4 * block :]
    early_other = splits + [jnp.concatenate([wide_out[:, :, :half], wide_out[:, :, half:]], 1)]
    sent = chunks_late.step(partial_one)
    got_one = across_cores(after(send_one, *sent))
    grad_frames, early_send, sums_one = norm_back(
        (after(partial_one, *sent), got_one), frames_own, gain_one, grad_middle, False
    )
    sent = chunks_late.step(early_send)
    for _ in range(count - 4):
        sent = chunks_late.step()
    swapped, swapped_got = swap_clips(grad_frames[:half_rows], after(early_send, *sent))

    def in_half(values):
        return lax.dynamic_update_slice_in_dim(jnp.zeros((width,), F32), values, core * half, 0)

    def head_sums(pieces_of):
        return in_half(jnp.concatenate([jnp.sum(piece.astype(F32), 1) for piece in pieces_of]))

    sums_up = jnp.stack([sums.reshape(shards, unit_block // 2) for sums in (sums_up_a, sums_up_b)], 1)
    sums_up_all = lax.dynamic_update_slice_in_dim(
        jnp.zeros((shards, 2, unit_block), F32), sums_up.reshape(shards, 1, unit_block), core, 1
    )
    grad_small = jnp.concatenate(
        [
            sums_one[0],
            sums_one[1],
            head_sums(flat[0]),
            head_sums(flat[2]),
            sums_two[2],
            sums_two[0],
            sums_two[1],
            sums_two[3],
            sums_up_all.reshape(-1),
        ]
    ).reshape(shards, small_size)
    small_sum = SmallSum(grad_small)
    small_sum.start()
    mixed = swapped_mixed(*sent, small_sum.kept)
    small_sum.finish(mixed)
    sent = chunks_late.step(small_sum.held)
    small_sum.start()
    new_up, new_down = adam_feed(
        [after(early[0], *sent, small_sum.kept)] + early[1:4],
        early_other[:4],
        (master_up, first_up, second_up),
        (master_down, first_down, second_down),
        shards,
    )
    late = chunks_late.result(new_up[0])
    small_sum.finish(*late)
    small_sum.start()
    grad_frames = swapped(*late)
    total_out = by_core(core, early[4][0], after(early_other[4], *late)[0], 1)
    late = over_groups(jnp.concatenate(late, 0))
    late_other = across_cores(late)
    small_sum.finish(grad_frames)
    total_small = small_sum.result()
    total_qkv = by_core(core, late, late_other, 2)

    new_qkv = adam_update(master_qkv, first_qkv, second_qkv, total_qkv, RATES[0], DECAYS[0])
    new_out = adam_update(master_out, first_out, second_out, total_out, RATES[1], DECAYS[1])
    new_small = adam_update(
        master_small, first_small, second_small, total_small, RATES[4], DECAYS[4]
    )
    return (mixed, grad_frames) + new_qkv + new_out + new_up + new_down + new_small


def solution(mesh):
    rows = P(("rep", "shard"), None)
    weights = (P(None, "shard", None), P("shard", None), P("shard", None), P("shard", None), P("shard"))
    outs = (rows, rows)
    for spec in weights:
        outs = outs + (spec,) * 4
    return jax.shard_map(
        local,
        mesh=mesh,
        in_specs=(rows, rows, P()) + weights * 3,
        out_specs=outs,
        check_vma=False,
    )
```
